32 devices in a mesh: seq: 8 (over z, x), tp: 4 (over y, core).
Axes of the slice: x: 2, y: 2, z: 4, core: 2. Of those that a mesh axis runs over, the one named last changes fastest.
Arguments:
- tokens: bfloat16 [1024, 2048], P('seq'), may hold values from -6 to 6
- input_heads: bfloat16 [1024, 4096], P('seq', 'tp'), may hold values from -6 to 6
- z_gate: bfloat16 [1024, 4096], P('seq', 'tp'), may hold values from -6 to 6
- b_proj: bfloat16 [1024, 128], P('seq'), may hold values from -0.5 to 0.5
- c_proj: bfloat16 [1024, 128], P('seq'), may hold values from -0.5 to 0.5
- step_size: float32 [1024, 64], P('seq', 'tp'), may hold values from 0.5 to 2
- decay_log: float32 [1024, 64], P('seq', 'tp'), as said below
- skip_gain: float32 [64], P('tp'), may hold values from 0.5 to 2
- init_state: float32 [64, 64, 128], P('tp'), may hold values from -48 to 48
- norm_gain: float32 [4096], P('tp'), may hold values from 0.1 to 1.9
- out_weight: bfloat16 [4096, 2048], P('tp'), may hold values from -0.09375 to 0.09375
- moe_gain: float32 [2048], replicated, may hold values from 0.1 to 1.9
- routes: int32 [1024, 2], P('seq'), may hold values from 0 to 7, all different within a row; in each aligned block of 128 rows (0 to 127, 128 to 255, ...) at most 64 rows name the same one
- route_weights: float32 [1024, 2], P('seq'), may hold values from 0.2 to 1
- w_gate: bfloat16 [8, 2048, 2048], P('seq', None, 'tp'), may hold values from -0.125 to 0.125
- w_up: bfloat16 [8, 2048, 2048], P('seq', None, 'tp'), may hold values from -0.125 to 0.125
- w_down: bfloat16 [8, 2048, 2048], P('seq', 'tp'), may hold values from -0.125 to 0.125
Outputs:
- mixed_out: bfloat16 [1024, 2048], P('seq', 'tp')
The draws below stay inside these ranges and needn't reach their ends.
Inputs may be any that keep to these rules, and one draw needn't show every extreme that they name: `decay_log`: every entry is negative. `routes`: the two experts of a row differ. In each aligned block of 128 rows (the rows of one device) no expert is named by more than 64 rows, a bound that some block reaches.
All inputs are finite; a program needn't handle non-finite values.
Results may differ from the reference program's by a relative error of at most 0.02.
Values may be sent and summed in bfloat16 or wider, within the bound.
No kernel may reach another device: no remote copies, remote signals or barrier semaphores. Data moves between devices by JAX's collectives and lax.ppermute only.
A program may use at most 128 MiB of HBM per device.

```python
import math
import jax
import jax.numpy as jnp
import numpy as np
from jax import lax

D = 2048
SSM_CHANNEL_COUNT = 64
HDIM = 64
STATE = 128
FF = 2048
TOP = 2
TOK_DEV = 128
TOKENS = 1024
INNER = 4096
EXPERTS = 8
CAP = 512
SLOTS = 64
N_TP = 4


def draw_decay_log(key, part):
    derived_prng_keys = jax.random.split(jax.random.fold_in(key, 11), 10)
    blocks = TOKENS // TOK_DEV
    forget_count = SSM_CHANNEL_COUNT // 2
    forget_heads = jax.random.permutation(derived_prng_keys[0], SSM_CHANNEL_COUNT) < forget_count
    slow_rate = 0.2 / TOKENS * jax.random.uniform(derived_prng_keys[1], (SSM_CHANNEL_COUNT,), minval=0.1, maxval=1.0)
    block_factor = jnp.exp(jax.random.uniform(derived_prng_keys[2], (blocks, SSM_CHANNEL_COUNT), minval=math.log(0.5), maxval=math.log(2.0)))
    jitter = jax.random.uniform(derived_prng_keys[3], (TOKENS, SSM_CHANNEL_COUNT), minval=0.7, maxval=1.4)
    slow_vals = -slow_rate[None, :] * jnp.repeat(block_factor, TOK_DEV, axis=0) * jitter
    block_phase = jax.random.randint(derived_prng_keys[4], (SSM_CHANNEL_COUNT,), 0, 9)
    block_ids = jnp.arange(blocks, dtype=jnp.int32)
    fast_block = jnp.logical_and((block_ids[:, None] + block_phase[None, :]) % 9 == 0, forget_heads[None, :])
    late_kind = jax.random.randint(derived_prng_keys[5], (blocks, SSM_CHANNEL_COUNT), 0, 2) == 1
    fast_rate = jnp.exp(jax.random.uniform(derived_prng_keys[6], (blocks, SSM_CHANNEL_COUNT), minval=math.log(1.0 / 50.0), maxval=math.log(1.0 / 30.0)))
    late_total = jax.random.uniform(derived_prng_keys[7], (blocks, SSM_CHANNEL_COUNT), minval=2.0, maxval=6.0)
    late_length = max(1, TOK_DEV // 16)
    row_place = jnp.arange(TOKENS, dtype=jnp.int32) % TOK_DEV
    late_rows = (row_place >= TOK_DEV - late_length)[:, None]
    uniform_fast = -jnp.repeat(fast_rate, TOK_DEV, axis=0) * jitter
    late_fast = jnp.where(late_rows, -jnp.repeat(late_total, TOK_DEV, axis=0) / late_length * jitter, slow_vals)
    fast_vals = jnp.where(jnp.repeat(late_kind, TOK_DEV, axis=0), late_fast, uniform_fast)
    fading_rates = jnp.where(jnp.repeat(fast_block, TOK_DEV, axis=0), fast_vals, slow_vals)
    spots = jax.random.randint(derived_prng_keys[8], (2,), 0, TOKENS)
    surge_amplitude_grid = jnp.log(jax.random.uniform(derived_prng_keys[9], (2, SSM_CHANNEL_COUNT), minval=0.5, maxval=0.8))
    locus_flags = (jnp.arange(TOKENS)[:, None] == spots[None, :]).astype(jnp.float32)
    surge_amounts = jnp.sum(locus_flags[:, :, None] * surge_amplitude_grid[None, :, :], axis=1)
    return (fading_rates + surge_amounts).astype(jnp.float32)


def level_of(stream_key, shape, shards, low, top_value):
    level, own = 1.0, jax.random.fold_in(stream_key, 6)
    for dim, parts in shards:
        steps = jnp.exp(jax.random.uniform(jax.random.fold_in(own, dim), (parts,), jnp.float32, low / len(shards), top_value / len(shards)))
        level = level * jnp.repeat(steps, shape[dim] // parts).reshape([-1 if axis == dim else 1 for axis in range(len(shape))])
    return level


def deal_out(stream_key, own, number, rows, count, top, reach, skew):
    order = jax.random.permutation(stream_key, count)
    crowded, ordinary = shares(count, rows * top, reach, skew, True), shares(count, rows * top, reach, skew, False)
    places = jnp.arange(count)

    def named(tallies, rotation):
        used = int((tallies > 0).sum())
        fixed = max(1, used // 4)
        shifted = fixed + (places - fixed + rotation * (used - fixed)) % max(1, count - fixed)
        return jnp.zeros((count,), jnp.int32).at[order[jnp.where(places < fixed, places, shifted)]].set(jnp.asarray(tallies, jnp.int32))

    tallies = jnp.where(number % 4 == 0, named(crowded, number // 4), named(ordinary, number - number // 4 - 1))
    mixed = jax.random.permutation(jax.random.fold_in(own, 3), count)
    source_of, receiver = mixed[0:count // 2 * 2:2], mixed[1:count // 2 * 2:2]
    margin = jnp.minimum(tallies[source_of] - 1, reach - tallies[receiver]) // 2
    margin = jnp.where((source_of == order[0]) | (receiver == order[0]) | (tallies[receiver] == 0), 0, jnp.maximum(margin, 0))
    shifted = jax.random.randint(jax.random.fold_in(own, 4), (count // 2,), 0, 1 << 20) % (margin + 1)
    tallies = tallies.at[source_of].add(-shifted).at[receiver].add(shifted)
    items = jnp.searchsorted(jnp.cumsum(tallies), jnp.arange(rows * top), side="right").astype(jnp.int32)
    grid = items.reshape(top, rows).T
    grid = grid[jax.random.permutation(jax.random.fold_in(own, 1), rows)]
    rotation = jax.random.randint(jax.random.fold_in(own, 2), (rows, 1), 0, top)
    return jnp.take_along_axis(grid, (jnp.arange(top)[None, :] + rotation) % top, axis=1)


def shares(amount, total, reach, lean, full):
    loads = [(1 << 20) // math.isqrt(standing ** lean) + 1 for standing in range(1, amount + 1)]
    largest = reach if full else min(reach, max(-(-total // amount), total * loads[0] // sum(loads)))
    least = 1 if total - largest >= amount - 1 else 0
    counts, spare = [largest] + [least] * (amount - 1), total - largest - least * (amount - 1)
    while spare > 0:
        candidates = [i for i in range(1, amount) if counts[i] < largest] or [i for i in range(1, amount) if counts[i] < reach]
        mass, left = sum([loads[i] for i in candidates]), spare
        for i in candidates:
            more = min(reach - counts[i], max(1, left * loads[i] // mass), spare)
            counts[i] = counts[i] + more
            spare = spare - more
    return np.array(counts)


def scatter_about(key, dims, spread, most, cuts=(), held_as=jnp.bfloat16):
    result = jax.random.normal(key, dims, jnp.float32) * spread
    if len(cuts) > 0:
        result = level_of(key, dims, cuts, -0.22, 0.18) * result
    return jnp.clip(result, min=-most, max=most).astype(held_as)


def setup_inputs(seed: int = 0) -> dict:
    key_of = jax.random.split(jax.random.key(seed), 18)
    tokens = scatter_about(key_of[0], (TOKENS, D), 1.0, 6.0, ((0, 8),))
    input_heads = scatter_about(key_of[1], (TOKENS, INNER), 1.0, 6.0, ((0, 8), (1, 4)))
    z_gate = scatter_about(key_of[2], (TOKENS, INNER), 1.0, 6.0, ((0, 8), (1, 4)))
    b_proj = scatter_about(key_of[3], (TOKENS, STATE), STATE ** -0.5, 0.5, ((0, 8),))
    c_proj = scatter_about(key_of[4], (TOKENS, STATE), STATE ** -0.5, 0.5, ((0, 8),))
    step_size = jnp.clip(jnp.exp(math.log(2.0) - 1.3862944 * jax.random.uniform(key_of[5], (TOKENS, SSM_CHANNEL_COUNT), jnp.float32) ** level_of(key_of[5], (TOKENS, SSM_CHANNEL_COUNT), ((0, 8), (1, 4)), -0.2, 0.2)), 0.5, 2.0)
    decay_log = draw_decay_log(jax.random.fold_in(key_of[17], 71), 0)
    skip_gain = jnp.clip(0.5 + 1.5 * jax.random.uniform(key_of[7], (SSM_CHANNEL_COUNT,), jnp.float32) ** level_of(key_of[7], (SSM_CHANNEL_COUNT,), ((0, 4),), -0.2, 0.2), 0.5, 2.0)
    init_state = scatter_about(key_of[8], (SSM_CHANNEL_COUNT, HDIM, STATE), 8.0, 48.0, ((0, 4),), jnp.float32)
    norm_gain = jnp.clip(1.0 + 0.18 * jax.random.normal(key_of[9], (INNER,), jnp.float32), 0.1, 1.9)
    out_weight = scatter_about(key_of[10], (INNER, D), INNER ** -0.5, 0.09375, ((0, 4),))
    moe_gain = jnp.clip(1.0 + 0.18 * jax.random.normal(key_of[11], (D,), jnp.float32), 0.1, 1.9)
    routes_keys = jax.random.split(jax.random.fold_in(key_of[12], 1), TOKENS // TOK_DEV)
    routes_turns = jax.random.permutation(jax.random.fold_in(key_of[12], 3), TOKENS // TOK_DEV)
    routes = jax.vmap(lambda own, number: deal_out(jax.random.fold_in(key_of[12], 2), own, number, TOK_DEV, EXPERTS, TOP, SLOTS, 2))(routes_keys, routes_turns).reshape((TOKENS, TOP))
    route_weights = jnp.clip(0.2 + 0.8 * jax.random.uniform(key_of[13], (TOKENS, TOP), jnp.float32) ** level_of(key_of[13], (TOKENS, TOP), ((0, 8),), -0.2, 0.2), 0.2, 1.0)
    w_gate = scatter_about(key_of[14], (EXPERTS, D, FF), D ** -0.5, 0.125, ((0, 8), (2, 4)))
    w_up = scatter_about(key_of[15], (EXPERTS, D, FF), D ** -0.5, 0.125, ((0, 8), (2, 4)))
    w_down = scatter_about(key_of[16], (EXPERTS, FF, D), FF ** -0.5, 0.125, ((0, 8), (1, 4)))
    return dict(tokens=tokens, input_heads=input_heads, z_gate=z_gate, b_proj=b_proj, c_proj=c_proj, step_size=step_size, decay_log=decay_log, skip_gain=skip_gain, init_state=init_state, norm_gain=norm_gain, out_weight=out_weight, moe_gain=moe_gain, routes=routes, route_weights=route_weights, w_gate=w_gate, w_up=w_up, w_down=w_down)


def rms_rows(values, scale_gain):
    wide_vals = values.astype(jnp.float32)
    mean_sq = lax.optimization_barrier(jnp.mean(wide_vals * wide_vals, axis=-1, keepdims=True))
    return (wide_vals * lax.rsqrt(mean_sq + 1e-05) * scale_gain).astype(jnp.bfloat16)

def reference(tokens, input_heads, z_gate, b_proj, c_proj, step_size, decay_log, skip_gain, init_state, norm_gain, out_weight, moe_gain, routes, route_weights, w_gate, w_up, w_down):
    highest = lax.Precision.HIGHEST
    block_count = TOKENS // TOK_DEV
    x_blocks = input_heads.astype(jnp.float32).reshape(block_count, TOK_DEV, SSM_CHANNEL_COUNT, HDIM)
    b_blocks = b_proj.astype(jnp.float32).reshape(block_count, TOK_DEV, STATE)
    c_blocks = c_proj.astype(jnp.float32).reshape(block_count, TOK_DEV, STATE)
    step_blocks = step_size.reshape(block_count, TOK_DEV, SSM_CHANNEL_COUNT)
    log_blocks = decay_log.reshape(block_count, TOK_DEV, SSM_CHANNEL_COUNT)
    positions = jnp.arange(TOK_DEV, dtype=jnp.int32)
    causal = positions[:, None] >= positions[None, :]

    def span_step(state, pieces):
        x_block, b_block, c_block, step_block, log_block = pieces
        cum_decay = jnp.cumsum(log_block, axis=0)
        end_decay = cum_decay[-1]
        scores = jnp.einsum('in,jn->ij', c_block, b_block, precision=highest)
        cum_heads = cum_decay.T
        log_gap = cum_heads[:, :, None] - cum_heads[:, None, :]
        decay_mat = jnp.where(causal, jnp.exp(jnp.where(causal, log_gap, 0.0)), 0.0)
        mix_weights = decay_mat * scores[None] * step_block.T[:, None, :]
        intra_part = jnp.einsum('hij,jhp->ihp', mix_weights, x_block, precision=highest)
        inter_part = jnp.einsum('in,hpn->ihp', c_block, state, precision=highest) * jnp.exp(cum_decay)[:, :, None]
        weighted = (jnp.exp(end_decay[None, :] - cum_decay) * step_block)[:, :, None] * x_block
        new_state = jnp.exp(end_decay)[:, None, None] * state + jnp.einsum('jhp,jn->hpn', weighted, b_block, precision=highest)
        return (new_state, intra_part + inter_part)
    last_state, dual_scan_blocks = lax.scan(span_step, init_state, (x_blocks, b_blocks, c_blocks, step_blocks, log_blocks))
    x_wide = input_heads.astype(jnp.float32).reshape(TOKENS, SSM_CHANNEL_COUNT, HDIM)
    ssd_out = dual_scan_blocks.reshape(TOKENS, SSM_CHANNEL_COUNT, HDIM) + skip_gain[None, :, None] * x_wide
    z_wide = z_gate.astype(jnp.float32).reshape(TOKENS, SSM_CHANNEL_COUNT, HDIM)
    gated_vals = ssd_out * jax.nn.silu(z_wide)
    gated_vals = gated_vals * lax.rsqrt(lax.optimization_barrier(jnp.mean(gated_vals * gated_vals, axis=2, keepdims=True)) + 1e-05)
    normed = (gated_vals.reshape(TOKENS, INNER) * norm_gain).astype(jnp.bfloat16)
    projected = jnp.dot(normed, out_weight, preferred_element_type=jnp.float32)
    hidden = (tokens.astype(jnp.float32) + projected).astype(jnp.bfloat16)
    moe_in = rms_rows(hidden, moe_gain)
    flat_expert = routes.reshape(block_count, TOP * TOK_DEV).astype(jnp.int32)
    onehot = (flat_expert[:, :, None] == jnp.arange(EXPERTS, dtype=jnp.int32)[None, None, :]).astype(jnp.int32)
    earlier_count = (jnp.cumsum(onehot, axis=1) - onehot).astype(jnp.int32)
    slot_rank = lax.optimization_barrier(jnp.sum(earlier_count * onehot, axis=2)).astype(jnp.int32)
    block_base = (jnp.arange(block_count, dtype=jnp.int32) * SLOTS)[:, None]
    placed = (flat_expert * CAP + block_base + slot_rank).reshape(-1).astype(jnp.int32)
    owners = (jnp.arange(TOP * TOKENS, dtype=jnp.int32) // TOP).astype(jnp.int32)
    source = jnp.full((EXPERTS * CAP,), TOKENS, jnp.int32).at[placed].set(owners).reshape(EXPERTS, CAP)

    def expert_run(pieces):
        index_rows, gate_mat, up_mat, down_mat = pieces
        rows_in = jnp.take(moe_in, index_rows, axis=0, mode='fill', fill_value=0)
        gate_val = jnp.dot(rows_in, gate_mat, preferred_element_type=jnp.float32)
        up_val = jnp.dot(rows_in, up_mat, preferred_element_type=jnp.float32)
        act_vals = (jax.nn.silu(gate_val) * up_val).astype(jnp.bfloat16)
        act_groups = act_vals.astype(jnp.float32).reshape(CAP, N_TP, FF // N_TP)
        down_weight_groups = down_mat.astype(jnp.float32).reshape(N_TP, FF // N_TP, D)
        partials = jnp.einsum('rqf,qfd->qrd', act_groups, down_weight_groups, precision=highest)
        partials = partials.astype(jnp.bfloat16).astype(jnp.float32)
        return lax.optimization_barrier(jnp.sum(partials, axis=0)).astype(jnp.bfloat16)
    expert_outs = lax.map(expert_run, (source, w_gate, w_up, w_down))
    chosen_indices = jnp.take(expert_outs.reshape(EXPERTS * CAP, D), placed, axis=0).reshape(TOKENS, TOP, D)
    mixed_out = hidden.astype(jnp.float32) + lax.optimization_barrier(jnp.sum(route_weights[:, :, None] * chosen_indices.astype(jnp.float32), axis=1))
    return mixed_out.astype(jnp.bfloat16)
```

```python
import jax
import jax.numpy as jnp
from jax import lax
from jax.sharding import PartitionSpec as P

BF = jnp.bfloat16
F32 = jnp.float32


def swap(value, bit):
    count = lax.axis_size("tp")
    return lax.ppermute(value, "tp", [(i, i ^ bit) for i in range(count)])


def sum_share(part):
    place = lax.axis_index("tp")
    rows, width = part.shape
    share = width // 4
    quarters = [part[:, k * share : (k + 1) * share] for k in range(4)]
    low = (place & 1) == 0
    keep = [jnp.where(low, quarters[0], quarters[1]), jnp.where(low, quarters[2], quarters[3])]
    give = [jnp.where(low, quarters[1], quarters[0]), jnp.where(low, quarters[3], quarters[2])]
    got = swap(jnp.stack(give).astype(BF), 1)
    first = keep[0] + got[0].astype(F32)
    second = keep[1] + got[1].astype(F32)
    near = place < 2
    last = swap(jnp.where(near, second, first).astype(BF), 2)
    return jnp.where(near, first, second) + last.astype(F32)


def join_shares(own):
    place = lax.axis_index("tp")
    far = swap(own, 2)
    near = place < 2
    pair = jnp.stack([jnp.where(near, own, far), jnp.where(near, far, own)])
    other = swap(pair, 1)
    low = (place & 1) == 0
    return jnp.concatenate(
        [
            jnp.where(low, pair[0], other[0]),
            jnp.where(low, other[0], pair[0]),
            jnp.where(low, pair[1], other[1]),
            jnp.where(low, other[1], pair[1]),
        ],
        axis=1,
    )


def exchange(value):
    return lax.all_to_all(value, "seq", split_axis=0, concat_axis=0, tiled=True)


def entering_state(local_state, block_decay, init_state):
    count = lax.axis_size("seq")
    place = lax.axis_index("seq")
    rows, width = local_state.shape
    heads = block_decay.shape[0]
    part = rows // count
    if count <= heads:
        held = heads // count
        decays = block_decay.reshape(count, held)
    else:
        held = 1
        decays = jnp.repeat(block_decay, count // heads).reshape(count, 1)
    high = decays.astype(BF)
    low = (decays - high.astype(F32)).astype(BF)
    pad = ((0, 0), (0, 8 - held))
    extra = jnp.concatenate([jnp.pad(high, pad), jnp.pad(low, pad)], axis=1)
    extra = jnp.broadcast_to(extra[:, :, None], (count, 16, width))
    out = jnp.concatenate([local_state.astype(BF).reshape(count, part, width), extra], axis=1)
    got = exchange(out)
    states = got[:, :part].astype(F32).reshape(count, held, part // held, width)
    scale = got[:, part : part + held].astype(F32) + got[:, part + 8 : part + 8 + held].astype(F32)
    carry = lax.dynamic_slice_in_dim(init_state.reshape(rows, width), place * part, part, 0)
    carry = carry.reshape(held, part // held, width)
    entering = []
    for turn in range(count):
        entering.append(carry.astype(BF))
        carry = scale[turn][:, None, :] * carry + states[turn]
    back = jnp.stack(entering).reshape(count, part, width)
    return exchange(back).reshape(rows, width)


def body(
    tokens,
    input_heads,
    z_gate,
    b_proj,
    c_proj,
    step_size,
    decay_log,
    skip_gain,
    init_state,
    norm_gain,
    out_weight,
    moe_gain,
    routes,
    route_weights,
    w_gate,
    w_up,
    w_down,
):
    highest = lax.Precision.HIGHEST
    tok_rows = input_heads.shape[0]
    head_count = step_size.shape[1]
    head_size = init_state.shape[1]
    state_size = init_state.shape[2]
    x_heads = input_heads.reshape(tok_rows, head_count, head_size)
    x_wide = x_heads.astype(F32)
    positions = jnp.arange(tok_rows, dtype=jnp.int32)
    causal = positions[:, None] >= positions[None, :]
    cum_decay = jnp.dot(causal.astype(F32), decay_log, precision=highest)
    end_decay = cum_decay[-1]
    weighted = (jnp.exp(end_decay[None, :] - cum_decay) * step_size)[:, :, None] * x_wide
    weighted = weighted.astype(BF).reshape(tok_rows, head_count * head_size)
    local_state = lax.dot_general(
        weighted, b_proj, (((0,), (0,)), ((), ())), preferred_element_type=F32
    )
    arriving = entering_state(local_state, jnp.exp(end_decay), init_state)
    scores = jnp.einsum("in,jn->ij", c_proj, b_proj, preferred_element_type=F32)
    cum_heads = cum_decay.T
    log_gap = cum_heads[:, :, None] - cum_heads[:, None, :]
    decay_mat = jnp.where(causal, jnp.exp(jnp.where(causal, log_gap, 0.0)), 0.0)
    mix_weights = (decay_mat * scores[None] * step_size.T[:, None, :]).astype(BF)
    intra_part = jnp.einsum("hij,jhp->ihp", mix_weights, x_heads, preferred_element_type=F32)
    direct = intra_part + skip_gain[None, :, None] * x_wide
    inter = lax.dot_general(
        c_proj, arriving, (((1,), (1,)), ((), ())), preferred_element_type=F32
    ).reshape(tok_rows, head_count, head_size)
    ssd_out = direct + inter * jnp.exp(cum_decay)[:, :, None]
    z_wide = z_gate.astype(F32).reshape(tok_rows, head_count, head_size)
    gated_vals = ssd_out * jax.nn.silu(z_wide)
    gated_vals = gated_vals * lax.rsqrt(
        jnp.mean(gated_vals * gated_vals, axis=2, keepdims=True) + 1e-05
    )
    normed = (gated_vals.reshape(tok_rows, head_count * head_size) * norm_gain).astype(BF)
    partial_value = jnp.dot(normed, out_weight, preferred_element_type=F32)

    model_width = out_weight.shape[1]
    share = model_width // lax.axis_size("tp")
    seq_count = lax.axis_size("seq")
    expert_count = w_gate.shape[0] * seq_count
    slot_count = 4 * tok_rows // seq_count
    top_count = routes.shape[1]
    items = top_count * tok_rows
    slots = expert_count * slot_count
    flat_expert = routes.T.reshape(-1)
    onehot = flat_expert[:, None] == jnp.arange(expert_count, dtype=jnp.int32)[None, :]
    before = jnp.arange(items)[:, None] > jnp.arange(items)[None, :]
    earlier = jnp.dot(before.astype(BF), onehot.astype(BF), preferred_element_type=F32)
    rank = jnp.sum(jnp.where(onehot, earlier, 0.0), axis=1).astype(jnp.int32)
    placed = flat_expert * slot_count + rank
    spots = placed[:, None] == jnp.arange(slots, dtype=jnp.int32)[None, :]
    pick = spots.astype(BF)
    fill = jnp.any(spots.reshape(top_count, tok_rows, slots), axis=0).astype(BF)

    place = lax.axis_index("tp")
    own_tokens = lax.dynamic_slice_in_dim(tokens, place * share, share, 1)
    hidden = (own_tokens.astype(F32) + sum_share(partial_value)).astype(BF)
    outgoing = lax.dot_general(
        fill, hidden, (((0,), (0,)), ((), ())), preferred_element_type=F32
    ).astype(BF)
    arrived = exchange(outgoing.reshape(expert_count, slot_count, share))
    rows = join_shares(arrived.reshape(slots, share))
    wide = rows.astype(F32)
    mean_sq = jnp.mean(wide * wide, axis=-1, keepdims=True)
    moe_rows = (wide * lax.rsqrt(mean_sq + 1e-05) * moe_gain).astype(BF)
    gate_val = jnp.dot(moe_rows, w_gate[0], preferred_element_type=F32)
    up_val = jnp.dot(moe_rows, w_up[0], preferred_element_type=F32)
    act_vals = (jax.nn.silu(gate_val) * up_val).astype(BF)
    down_val = jnp.dot(act_vals, w_down[0], preferred_element_type=F32)
    results = sum_share(down_val).astype(BF)
    returned = exchange(results.reshape(expert_count, slot_count, share)).reshape(slots, share)
    chosen = jnp.dot(pick, returned, preferred_element_type=F32).reshape(
        top_count, tok_rows, share
    )
    mixed_out = hidden.astype(F32) + jnp.sum(route_weights.T[:, :, None] * chosen, axis=0)
    return mixed_out.astype(BF)


def solution(mesh):
    in_specs = (
        P("seq", None),
        P("seq", "tp"),
        P("seq", "tp"),
        P("seq", None),
        P("seq", None),
        P("seq", "tp"),
        P("seq", "tp"),
        P("tp"),
        P("tp", None, None),
        P("tp"),
        P("tp", None),
        P(),
        P("seq", None),
        P("seq", None),
        P("seq", None, "tp"),
        P("seq", None, "tp"),
        P("seq", "tp", None),
    )
    out_specs = P("seq", "tp")
    return jax.shard_map(body, mesh=mesh, in_specs=in_specs, out_specs=out_specs, check_vma=False)
```

```python
import jax
import jax.numpy as jnp
from jax import lax
from jax.experimental import pallas as pl
from jax.experimental.pallas import tpu as pltpu
from jax.sharding import PartitionSpec as P

BF = jnp.bfloat16
F32 = jnp.float32


def swap(value, bit):
    count = lax.axis_size("tp")
    return lax.ppermute(value, "tp", [(i, i ^ bit) for i in range(count)])


def sum_share(part):
    place = lax.axis_index("tp")
    rows, width = part.shape
    share = width // 4
    quarters = [part[:, k * share : (k + 1) * share] for k in range(4)]
    low = (place & 1) == 0
    keep = [jnp.where(low, quarters[0], quarters[1]), jnp.where(low, quarters[2], quarters[3])]
    give = [jnp.where(low, quarters[1], quarters[0]), jnp.where(low, quarters[3], quarters[2])]
    got = swap(jnp.stack(give).astype(BF), 1)
    first = keep[0] + got[0].astype(F32)
    second = keep[1] + got[1].astype(F32)
    near = place < 2
    last = swap(jnp.where(near, second, first).astype(BF), 2)
    return jnp.where(near, first, second) + last.astype(F32)


def exchange(value):
    return lax.all_to_all(value, "seq", split_axis=0, concat_axis=0, tiled=True)


def entering_state(local_state, block_decay, init_state):
    count = lax.axis_size("seq")
    place = lax.axis_index("seq")
    rows, width = local_state.shape
    heads = block_decay.shape[0]
    part = rows // count
    if count <= heads:
        held = heads // count
        decays = block_decay.reshape(count, held)
    else:
        held = 1
        decays = jnp.repeat(block_decay, count // heads).reshape(count, 1)
    high = decays.astype(BF)
    low = (decays - high.astype(F32)).astype(BF)
    pad = ((0, 0), (0, 8 - held))
    extra = jnp.concatenate([jnp.pad(high, pad), jnp.pad(low, pad)], axis=1)
    extra = jnp.broadcast_to(extra[:, :, None], (count, 16, width))
    out = jnp.concatenate([local_state.astype(BF).reshape(count, part, width), extra], axis=1)
    got = exchange(out)
    start = lax.dynamic_slice_in_dim(init_state.reshape(rows, width), place * part, part, 0)

    def prefix(got_ref, start_ref, back_ref):
        group = part // held
        carries = [start_ref[pl.ds(h * group, group), :] for h in range(held)]
        for turn in range(count):
            scale = got_ref[turn, pl.ds(part, 16), :].astype(F32)
            scale = scale[:8] + scale[8:]
            for h in range(held):
                spot = pl.ds(h * group, group)
                back_ref[turn, spot, :] = carries[h].astype(BF)
                state = got_ref[turn, spot, :].astype(F32)
                carries[h] = scale[h : h + 1] * carries[h] + state

    back = pl.pallas_call(
        prefix,
        out_shape=jax.ShapeDtypeStruct((count, part, width), BF),
        name="prefix",
    )(got, start)
    return exchange(back).reshape(rows, width)


def expert_kernel(place_ref, own, near, far, last, gain, wg, wu, wd, give, keep, rows, total):
    place = place_ref[0]
    step = pl.program_id(0)
    share = own.shape[1]
    spots = [pl.ds(pl.multiple_of((place ^ k) * share, share), share) for k in range(4)]
    parts = [own, near, far, last]

    @pl.when(step == 0)
    def _():
        wide = [p[...].astype(F32) for p in parts]
        square = sum(jnp.sum(w * w, axis=1, keepdims=True) for w in wide)
        scale = lax.rsqrt(square * (1.0 / (4 * share)) + 1e-05)
        for k in range(4):
            rows[k] = (wide[k] * scale * gain[:, spots[k]]).astype(BF)

    gate = up = 0.0
    for k in range(4):
        gate += jnp.dot(rows[k], wg[spots[k], :], preferred_element_type=F32)
        up += jnp.dot(rows[k], wu[spots[k], :], preferred_element_type=F32)
    act = (gate * (1.0 / (1.0 + jnp.exp(-gate))) * up).astype(BF)
    for k in range(4):
        down = jnp.dot(act, wd[:, spots[k]], preferred_element_type=F32)

        @pl.when(step == 0)
        def _():
            total[k] = down

        @pl.when(step > 0)
        def _():
            total[k] += down

    @pl.when(step == pl.num_programs(0) - 1)
    def _():
        give[0] = total[1].astype(BF)
        give[1] = total[3].astype(BF)
        keep[0] = total[0]
        keep[1] = total[2]


def run_expert(place, own, near, far, last, gain, wg, wu, wd):
    rows, share = own.shape
    width, inner = wg.shape
    tile = inner // 2

    def whole(j, _):
        return (0, 0)

    part = pl.BlockSpec((rows, share), whole)
    return pl.pallas_call(
        expert_kernel,
        grid_spec=pltpu.PrefetchScalarGridSpec(
            num_scalar_prefetch=1,
            grid=(inner // tile,),
            in_specs=[
                part,
                part,
                part,
                part,
                pl.BlockSpec((1, width), whole),
                pl.BlockSpec((width, tile), lambda j, _: (0, j)),
                pl.BlockSpec((width, tile), lambda j, _: (0, j)),
                pl.BlockSpec((tile, width), lambda j, _: (j, 0)),
            ],
            out_specs=[pl.BlockSpec((2, rows, share), lambda j, _: (0, 0, 0))] * 2,
            scratch_shapes=[pltpu.VMEM((4, rows, share), BF), pltpu.VMEM((4, rows, share), F32)],
        ),
        out_shape=[
            jax.ShapeDtypeStruct((2, rows, share), BF),
            jax.ShapeDtypeStruct((2, rows, share), F32),
        ],
        compiler_params=pltpu.CompilerParams(vmem_limit_bytes=40 * 1024 * 1024),
        cost_estimate=pl.CostEstimate(
            flops=6 * rows * width * inner,
            bytes_accessed=6 * width * inner + 14 * rows * width,
            transcendentals=rows * inner,
        ),
        name="expert",
    )(place.reshape(1), own, near, far, last, gain.reshape(1, width), wg, wu, wd)


def body(
    tokens,
    input_heads,
    z_gate,
    b_proj,
    c_proj,
    step_size,
    decay_log,
    skip_gain,
    init_state,
    norm_gain,
    out_weight,
    moe_gain,
    routes,
    route_weights,
    w_gate,
    w_up,
    w_down,
):
    highest = lax.Precision.HIGHEST
    tok_rows = input_heads.shape[0]
    head_count = step_size.shape[1]
    head_size = init_state.shape[1]
    state_size = init_state.shape[2]
    x_heads = input_heads.reshape(tok_rows, head_count, head_size)
    x_wide = x_heads.astype(F32)
    positions = jnp.arange(tok_rows, dtype=jnp.int32)
    causal = positions[:, None] >= positions[None, :]
    cum_decay = jnp.dot(causal.astype(F32), decay_log, precision=highest)
    end_decay = cum_decay[-1]
    weighted = (jnp.exp(end_decay[None, :] - cum_decay) * step_size)[:, :, None] * x_wide
    weighted = weighted.astype(BF).reshape(tok_rows, head_count * head_size)
    local_state = lax.dot_general(
        weighted, b_proj, (((0,), (0,)), ((), ())), preferred_element_type=F32
    )
    arriving = entering_state(local_state, jnp.exp(end_decay), init_state)
    scores = jnp.einsum("in,jn->ij", c_proj, b_proj, preferred_element_type=F32)
    cum_heads = cum_decay.T
    log_gap = cum_heads[:, :, None] - cum_heads[:, None, :]
    decay_mat = jnp.where(causal, jnp.exp(jnp.where(causal, log_gap, 0.0)), 0.0)
    mix_weights = (decay_mat * scores[None] * step_size.T[:, None, :]).astype(BF)
    intra_part = jnp.einsum("hij,jhp->ihp", mix_weights, x_heads, preferred_element_type=F32)
    direct = intra_part + skip_gain[None, :, None] * x_wide
    inter = lax.dot_general(
        c_proj, arriving, (((1,), (1,)), ((), ())), preferred_element_type=F32
    ).reshape(tok_rows, head_count, head_size)
    ssd_out = direct + inter * jnp.exp(cum_decay)[:, :, None]
    z_wide = z_gate.astype(F32).reshape(tok_rows, head_count, head_size)
    gated_vals = ssd_out * jax.nn.silu(z_wide)
    gated_vals = gated_vals * lax.rsqrt(
        jnp.mean(gated_vals * gated_vals, axis=2, keepdims=True) + 1e-05
    )
    normed = (gated_vals.reshape(tok_rows, head_count * head_size) * norm_gain).astype(BF)
    partial_value = jnp.dot(normed, out_weight, preferred_element_type=F32)

    model_width = out_weight.shape[1]
    share = model_width // lax.axis_size("tp")
    seq_count = lax.axis_size("seq")
    expert_count = w_gate.shape[0] * seq_count
    slot_count = 4 * tok_rows // seq_count
    top_count = routes.shape[1]
    items = top_count * tok_rows
    slots = expert_count * slot_count
    flat_expert = routes.T.reshape(-1)
    onehot = flat_expert[:, None] == jnp.arange(expert_count, dtype=jnp.int32)[None, :]
    before = jnp.arange(items)[:, None] > jnp.arange(items)[None, :]
    earlier = jnp.dot(before.astype(BF), onehot.astype(BF), preferred_element_type=F32)
    rank = jnp.sum(jnp.where(onehot, earlier, 0.0), axis=1).astype(jnp.int32)
    placed = flat_expert * slot_count + rank
    spots = placed[:, None] == jnp.arange(slots, dtype=jnp.int32)[None, :]
    pick = spots.astype(BF)
    fill = jnp.any(spots.reshape(top_count, tok_rows, slots), axis=0).astype(BF)

    place = lax.axis_index("tp")
    own_tokens = lax.dynamic_slice_in_dim(tokens, place * share, share, 1)
    hidden = (own_tokens.astype(F32) + sum_share(partial_value)).astype(BF)
    outgoing = lax.dot_general(
        fill, hidden, (((0,), (0,)), ((), ())), preferred_element_type=F32
    ).astype(BF)
    outgoing = outgoing.reshape(expert_count, slot_count, share)
    cuts = 2 if slot_count % 32 == 0 else 1
    cut = slot_count // cuts
    returned = []
    for turn in range(cuts):
        own = exchange(outgoing[:, turn * cut : (turn + 1) * cut]).reshape(-1, share)
        far = swap(own, 2)
        near = swap(own, 1)
        last = swap(far, 1)
        give, keep = run_expert(
            place, own, near, far, last, moe_gain, w_gate[0], w_up[0], w_down[0]
        )
        got = swap(give, 1)
        passing = swap((keep[1] + got[1].astype(F32)).astype(BF), 2)
        result = (keep[0] + got[0].astype(F32) + passing.astype(F32)).astype(BF)
        returned.append(exchange(result.reshape(expert_count, cut, share)))
    returned = jnp.concatenate(returned, axis=1).reshape(slots, share)
    chosen = jnp.dot(pick, returned, preferred_element_type=F32).reshape(
        top_count, tok_rows, share
    )
    mixed_out = hidden.astype(F32) + jnp.sum(route_weights.T[:, :, None] * chosen, axis=0)
    return mixed_out.astype(BF)


def solution(mesh):
    in_specs = (
        P("seq", None),
        P("seq", "tp"),
        P("seq", "tp"),
        P("seq", None),
        P("seq", None),
        P("seq", "tp"),
        P("seq", "tp"),
        P("tp"),
        P("tp", None, None),
        P("tp"),
        P("tp", None),
        P(),
        P("seq", None),
        P("seq", None),
        P("seq", None, "tp"),
        P("seq", None, "tp"),
        P("seq", "tp", None),
    )
    out_specs = P("seq", "tp")
    return jax.shard_map(body, mesh=mesh, in_specs=in_specs, out_specs=out_specs, check_vma=False)
```

```python
import jax
import jax.numpy as jnp
from jax import lax
from jax.experimental import pallas as pl
from jax.experimental.pallas import tpu as pltpu
from jax.sharding import PartitionSpec as P

BF = jnp.bfloat16
F32 = jnp.float32
MIB = 1024 * 1024
LANES = 128


def swap(value, bit):
    count = lax.axis_size("tp")
    return lax.ppermute(value, "tp", [(i, i ^ bit) for i in range(count)])


def exchange(value):
    return lax.all_to_all(value, "seq", split_axis=0, concat_axis=0, tiled=True)


def after(value, *others):
    return lax.optimization_barrier((value, *others))[0]


def params(mib):
    return pltpu.CompilerParams(vmem_limit_bytes=mib * MIB)


def whole(*shape):
    return pl.BlockSpec(shape, lambda *_: (0,) * len(shape))


def by_pair(left, right, size):
    lane = lax.broadcasted_iota(jnp.int32, (size, LANES), 1)
    return jnp.where(lane < LANES // 2, left, right)


def state_kernel(x, step_t, decay_t, b, out, cum_out):
    count, rows, _ = out.shape
    part = rows - 16
    heads, toks = decay_t.shape
    row = lax.broadcasted_iota(jnp.int32, (toks, toks), 0)
    col = lax.broadcasted_iota(jnp.int32, (toks, toks), 1)
    upper = (row <= col).astype(F32)
    cum_t = jnp.dot(
        decay_t[...], upper, precision=lax.Precision.HIGHEST, preferred_element_type=F32
    )
    cum_out[...] = cum_t
    end = cum_t[:, toks - 1 : toks]
    scale = (jnp.exp(end - cum_t) * step_t[...]).T
    decay = jnp.broadcast_to(jnp.exp(end), (heads, LANES))
    high = decay.astype(BF).astype(F32)
    extra = by_pair(high, decay - high, heads).astype(BF)
    for k in range(count):
        out[k, pl.ds(part, 16), :] = extra
    for p in range(heads // 2):
        pair = x[:, p * LANES : (p + 1) * LANES].astype(F32)
        factor = by_pair(scale[:, 2 * p : 2 * p + 1], scale[:, 2 * p + 1 : 2 * p + 2], toks)
        state = lax.dot_general(
            (pair * factor).astype(BF),
            b[...],
            (((0,), (0,)), ((), ())),
            preferred_element_type=F32,
        ).astype(BF)
        for k in range(LANES // part):
            out[p * (LANES // part) + k, pl.ds(0, part), :] = state[k * part : (k + 1) * part]


def own_state(x, step_t, decay_t, b, count):
    heads, toks = decay_t.shape
    part = x.shape[1] // count
    return pl.pallas_call(
        state_kernel,
        out_shape=[
            jax.ShapeDtypeStruct((count, part + 16, b.shape[1]), BF),
            jax.ShapeDtypeStruct((heads, toks), F32),
        ],
        compiler_params=params(8),
        name="own_state",
    )(x, step_t, decay_t, b)


def prefix_kernel(place_ref, got, start, back):
    count, part, _ = back.shape
    heads = 16
    held = max(1, heads // count)
    group = part // held
    first = place_ref[0] * heads // count
    row = lax.broadcasted_iota(jnp.int32, (heads, LANES), 0)
    carries = [start[pl.ds(h * group, group), :] for h in range(held)]
    for turn in range(count):
        extra = got[turn, pl.ds(part, 16), :].astype(F32)
        scale = extra[:, :1] + extra[:, LANES // 2 : LANES // 2 + 1]
        for h in range(held):
            spot = pl.ds(h * group, group)
            back[turn, spot, :] = carries[h].astype(BF)
            factor = jnp.sum(jnp.where(row == first + h, scale, 0.0), axis=0, keepdims=True)
            carries[h] = factor * carries[h] + got[turn, spot, :].astype(F32)


def entering_state(place, got, init_rows):
    count, rows, width = got.shape
    part = rows - 16
    return pl.pallas_call(
        prefix_kernel,
        grid_spec=pltpu.PrefetchScalarGridSpec(
            num_scalar_prefetch=1,
            grid=(1,),
            in_specs=[
                whole(count, rows, width),
                pl.BlockSpec((part, width), lambda _, place: (place[0], 0)),
            ],
            out_specs=whole(count, part, width),
        ),
        out_shape=jax.ShapeDtypeStruct((count, part, width), BF),
        compiler_params=params(8),
        name="prefix",
    )(place.reshape(1), got, init_rows)


def within_kernel(skip, x, step_t, cum_t, b, c, out):
    heads, toks = cum_t.shape
    row = lax.broadcasted_iota(jnp.int32, (toks, toks), 0)
    col = lax.broadcasted_iota(jnp.int32, (toks, toks), 1)
    causal = row >= col
    nt = (((1,), (1,)), ((), ()))
    scores = lax.dot_general(c[...], b[...], nt, preferred_element_type=F32)
    cum = cum_t[...].T
    for p in range(heads // 2):
        pair = x[:, p * LANES : (p + 1) * LANES]
        sums = []
        for h in (2 * p, 2 * p + 1):
            gap = cum[:, h : h + 1] - cum_t[h : h + 1, :]
            decay = jnp.where(causal, jnp.exp(jnp.where(causal, gap, 0.0)), 0.0)
            weights = (decay * scores * step_t[h : h + 1, :]).astype(BF)
            sums.append(jnp.dot(weights, pair, preferred_element_type=F32))
        gain = by_pair(skip[2 * p], skip[2 * p + 1], toks)
        out[:, p * LANES : (p + 1) * LANES] = (
            by_pair(sums[0], sums[1], toks) + gain * pair.astype(F32)
        )


def within_block(skip, x, step_t, cum_t, b, c):
    toks, inner = x.shape
    heads = cum_t.shape[0]
    vmem = pl.BlockSpec(memory_space=pltpu.VMEM)
    return pl.pallas_call(
        within_kernel,
        in_specs=[pl.BlockSpec(memory_space=pltpu.SMEM)] + [vmem] * 5,
        out_shape=jax.ShapeDtypeStruct((toks, inner), F32),
        compiler_params=params(8),
        cost_estimate=pl.CostEstimate(
            flops=4 * heads * toks * toks * LANES,
            bytes_accessed=6 * toks * inner,
            transcendentals=heads * toks * toks,
        ),
        name="within_block",
    )(skip, x, step_t, cum_t, b, c)


def tail_kernel(place_ref, c, arriving, cum_t, direct, z, gain, weight, give, keep, normed):
    step = pl.program_id(0)
    heads, toks = cum_t.shape

    @pl.when(step == 0)
    def _():
        grown = jnp.exp(cum_t[...]).T
        lane = lax.broadcasted_iota(jnp.int32, (toks, LANES), 1)
        left = lane < LANES // 2
        nt = (((1,), (1,)), ((), ()))
        for p in range(heads // 2):
            spot = pl.ds(p * LANES, LANES)
            inter = lax.dot_general(
                c[...], arriving[spot, :], nt, preferred_element_type=F32
            )
            factor = by_pair(grown[:, 2 * p : 2 * p + 1], grown[:, 2 * p + 1 : 2 * p + 2], toks)
            wide = z[:, spot].astype(F32)
            gated = (direct[:, spot] + inter * factor) * (wide * (1.0 / (1.0 + jnp.exp(-wide))))
            square = gated * gated
            first = jnp.sum(jnp.where(left, square, 0.0), axis=1, keepdims=True)
            second = jnp.sum(jnp.where(left, 0.0, square), axis=1, keepdims=True)
            mean = by_pair(first, second, toks) * (2.0 / LANES)
            normed[:, spot] = (gated * lax.rsqrt(mean + 1e-05) * gain[:, spot]).astype(BF)

    part = jnp.dot(normed[...], weight[...], preferred_element_type=F32)

    @pl.when(step < 2)
    def _():
        give[jnp.minimum(step, 1)] = part.astype(BF)

    @pl.when(step >= 2)
    def _():
        keep[jnp.maximum(step - 2, 0)] = part


def mixer_tail(place, c, arriving, cum_t, direct, z, gain, weight):
    heads, toks = cum_t.shape
    inner, width = weight.shape
    share = width // 4
    return pl.pallas_call(
        tail_kernel,
        grid_spec=pltpu.PrefetchScalarGridSpec(
            num_scalar_prefetch=1,
            grid=(4,),
            in_specs=[
                whole(*c.shape),
                whole(*arriving.shape),
                whole(heads, toks),
                whole(toks, inner),
                whole(toks, inner),
                whole(1, inner),
                pl.BlockSpec((inner, share), lambda j, place: (0, place[0] ^ ((2 * j + 1) % 5))),
            ],
            out_specs=[whole(2, toks, share)] * 2,
            scratch_shapes=[pltpu.VMEM((toks, inner), BF)],
        ),
        out_shape=[
            jax.ShapeDtypeStruct((2, toks, share), BF),
            jax.ShapeDtypeStruct((2, toks, share), F32),
        ],
        compiler_params=params(56),
        cost_estimate=pl.CostEstimate(
            flops=2 * toks * inner * width,
            bytes_accessed=2 * inner * width + 14 * toks * inner,
            transcendentals=toks * inner,
        ),
        name="mixer_tail",
    )(place.reshape(1), c, arriving, cum_t, direct, z, gain.reshape(1, inner), weight)


def expert_kernel(place_ref, own, near, far, last, gain, wg, wu, wd, give, keep, rows, total):
    place = place_ref[0]
    step = pl.program_id(0)
    share = own.shape[1]
    spots = [pl.ds(pl.multiple_of((place ^ k) * share, share), share) for k in range(4)]
    parts = [own, near, far, last]

    @pl.when(step == 0)
    def _():
        wide = [p[...].astype(F32) for p in parts]
        square = sum(jnp.sum(w * w, axis=1, keepdims=True) for w in wide)
        scale = lax.rsqrt(square * (1.0 / (4 * share)) + 1e-05)
        for k in range(4):
            rows[k] = (wide[k] * scale * gain[:, spots[k]]).astype(BF)

    gate = up = 0.0
    for k in range(4):
        gate += jnp.dot(rows[k], wg[spots[k], :], preferred_element_type=F32)
        up += jnp.dot(rows[k], wu[spots[k], :], preferred_element_type=F32)
    act = (gate * (1.0 / (1.0 + jnp.exp(-gate))) * up).astype(BF)
    for k in range(4):
        down = jnp.dot(act, wd[:, spots[k]], preferred_element_type=F32)

        @pl.when(step == 0)
        def _():
            total[k] = down

        @pl.when(step > 0)
        def _():
            total[k] += down

    @pl.when(step == pl.num_programs(0) - 1)
    def _():
        give[0] = total[1].astype(BF)
        give[1] = total[3].astype(BF)
        keep[0] = total[0]
        keep[1] = total[2]


def run_expert(place, own, near, far, last, gain, wg, wu, wd):
    rows, share = own.shape
    width, inner = wg.shape
    tile = inner // 2

    part = whole(rows, share)
    return pl.pallas_call(
        expert_kernel,
        grid_spec=pltpu.PrefetchScalarGridSpec(
            num_scalar_prefetch=1,
            grid=(inner // tile,),
            in_specs=[
                part,
                part,
                part,
                part,
                whole(1, width),
                pl.BlockSpec((width, tile), lambda j, _: (0, j)),
                pl.BlockSpec((width, tile), lambda j, _: (0, j)),
                pl.BlockSpec((tile, width), lambda j, _: (j, 0)),
            ],
            out_specs=[whole(2, rows, share)] * 2,
            scratch_shapes=[pltpu.VMEM((4, rows, share), BF), pltpu.VMEM((4, rows, share), F32)],
        ),
        out_shape=[
            jax.ShapeDtypeStruct((2, rows, share), BF),
            jax.ShapeDtypeStruct((2, rows, share), F32),
        ],
        compiler_params=params(56),
        cost_estimate=pl.CostEstimate(
            flops=6 * rows * width * inner,
            bytes_accessed=6 * width * inner + 14 * rows * width,
            transcendentals=rows * inner,
        ),
        name="expert",
    )(place.reshape(1), own, near, far, last, gain.reshape(1, width), wg, wu, wd)


def body(
    tokens,
    input_heads,
    z_gate,
    b_proj,
    c_proj,
    step_size,
    decay_log,
    skip_gain,
    init_state,
    norm_gain,
    out_weight,
    moe_gain,
    routes,
    route_weights,
    w_gate,
    w_up,
    w_down,
):
    tok_rows, inner = input_heads.shape
    state_size = init_state.shape[2]
    seq_count = lax.axis_size("seq")
    place = lax.axis_index("tp")
    step_t = step_size.T
    outgoing, cum_t = own_state(input_heads, step_t, decay_log.T, b_proj, seq_count)
    got = exchange(outgoing)
    direct = within_block(skip_gain, input_heads, step_t, cum_t, b_proj, c_proj)
    back = entering_state(lax.axis_index("seq"), got, init_state.reshape(inner, state_size))
    arriving = exchange(back).reshape(inner, state_size)
    give, keep = mixer_tail(
        place, c_proj, arriving, cum_t, direct, z_gate, norm_gain, out_weight
    )

    model_width = out_weight.shape[1]
    share = model_width // 4
    expert_count = w_gate.shape[0] * seq_count
    slot_count = 4 * tok_rows // seq_count
    top_count = routes.shape[1]
    items = top_count * tok_rows
    slots = expert_count * slot_count
    flat_expert = routes.T.reshape(-1)
    onehot = flat_expert[:, None] == jnp.arange(expert_count, dtype=jnp.int32)[None, :]
    before = jnp.arange(items)[:, None] > jnp.arange(items)[None, :]
    earlier = jnp.dot(before.astype(BF), onehot.astype(BF), preferred_element_type=F32)
    rank = jnp.sum(jnp.where(onehot, earlier, 0.0), axis=1).astype(jnp.int32)
    placed = flat_expert * slot_count + rank
    spots = placed[:, None] == jnp.arange(slots, dtype=jnp.int32)[None, :]
    pick = spots.astype(BF)
    fill = jnp.any(spots.reshape(top_count, tok_rows, slots), axis=0).astype(BF)

    got = swap(give, 1)
    passing = swap((keep[1] + got[1].astype(F32)).astype(BF), 2)
    own_tokens = lax.dynamic_slice_in_dim(tokens, place * share, share, 1)
    projected = keep[0] + got[0].astype(F32) + passing.astype(F32)
    hidden = (own_tokens.astype(F32) + projected).astype(BF)
    outgoing = lax.dot_general(
        fill, hidden, (((0,), (0,)), ((), ())), preferred_element_type=F32
    ).astype(BF)
    arrived = exchange(outgoing.reshape(expert_count, slot_count, share)).reshape(slots, share)

    cut = slots // 2
    own = [arrived[:cut], arrived[cut:]]
    far = [swap(own[0], 2), swap(own[1], 2)]
    near = [swap(own[0], 1), swap(own[1], 1)]
    weights = (moe_gain, w_gate[0], w_up[0], w_down[0])
    give0, keep0 = run_expert(place, own[0], near[0], far[0], swap(far[0], 1), *weights)
    pass_got0 = swap(give0[1], 1)
    last1 = swap(after(far[1], give0), 1)
    pass0 = (keep0[1] + pass_got0.astype(F32)).astype(BF)
    give1, keep1 = run_expert(
        place, after(own[1], pass0), near[1], far[1], last1, *weights
    )
    passed0 = swap(pass0, 2)
    kept_got0 = swap(give0[0], 1)
    pass_got1 = swap(give1[1], 1)
    kept_got1 = swap(give1[0], 1)
    passed1 = swap((keep1[1] + pass_got1.astype(F32)).astype(BF), 2)
    result0 = (keep0[0] + kept_got0.astype(F32) + passed0.astype(F32)).astype(BF)
    result1 = (keep1[0] + kept_got1.astype(F32) + passed1.astype(F32)).astype(BF)
    results = jnp.concatenate([result0, result1]).reshape(expert_count, slot_count, share)
    returned = exchange(results).reshape(slots, share)
    chosen = jnp.dot(pick, returned, preferred_element_type=F32).reshape(
        top_count, tok_rows, share
    )
    mixed_out = hidden.astype(F32) + jnp.sum(route_weights.T[:, :, None] * chosen, axis=0)
    return mixed_out.astype(BF)


def solution(mesh):
    in_specs = (
        P("seq", None),
        P("seq", "tp"),
        P("seq", "tp"),
        P("seq", None),
        P("seq", None),
        P("seq", "tp"),
        P("seq", "tp"),
        P("tp"),
        P("tp", None, None),
        P("tp"),
        P("tp", None),
        P(),
        P("seq", None),
        P("seq", None),
        P("seq", None, "tp"),
        P("seq", None, "tp"),
        P("seq", "tp", None),
    )
    out_specs = P("seq", "tp")
    return jax.shard_map(body, mesh=mesh, in_specs=in_specs, out_specs=out_specs, check_vma=False)
```

```python
import jax
import jax.numpy as jnp
from jax import lax
from jax.experimental import pallas as pl
from jax.experimental.pallas import tpu as pltpu
from jax.sharding import PartitionSpec as P

BF = jnp.bfloat16
F32 = jnp.float32
MIB = 1024 * 1024
LANES = 128


def swap(value, bit):
    count = lax.axis_size("tp")
    return lax.ppermute(value, "tp", [(i, i ^ bit) for i in range(count)])


def exchange(value):
    return lax.all_to_all(value, "seq", split_axis=0, concat_axis=0, tiled=True)


def params(mib):
    return pltpu.CompilerParams(vmem_limit_bytes=mib * MIB)


def whole(*shape):
    return pl.BlockSpec(shape, lambda *_: (0,) * len(shape))


def by_pair(left, right, size):
    lane = lax.broadcasted_iota(jnp.int32, (size, LANES), 1)
    return jnp.where(lane < LANES // 2, left, right)


def state_kernel(x, step_t, decay_t, b, out, cum_out):
    count, rows, _ = out.shape
    part = rows - 16
    heads, toks = decay_t.shape
    row = lax.broadcasted_iota(jnp.int32, (toks, toks), 0)
    col = lax.broadcasted_iota(jnp.int32, (toks, toks), 1)
    upper = (row <= col).astype(F32)
    cum_t = jnp.dot(
        decay_t[...], upper, precision=lax.Precision.HIGHEST, preferred_element_type=F32
    )
    cum_out[...] = cum_t
    end = cum_t[:, toks - 1 : toks]
    scale = (jnp.exp(end - cum_t) * step_t[...]).T
    decay = jnp.broadcast_to(jnp.exp(end), (heads, LANES))
    high = decay.astype(BF).astype(F32)
    extra = by_pair(high, decay - high, heads).astype(BF)
    for k in range(count):
        out[k, pl.ds(part, 16), :] = extra
    for p in range(heads // 2):
        pair = x[:, p * LANES : (p + 1) * LANES].astype(F32)
        factor = by_pair(scale[:, 2 * p : 2 * p + 1], scale[:, 2 * p + 1 : 2 * p + 2], toks)
        state = lax.dot_general(
            (pair * factor).astype(BF),
            b[...],
            (((0,), (0,)), ((), ())),
            preferred_element_type=F32,
        ).astype(BF)
        for k in range(LANES // part):
            out[p * (LANES // part) + k, pl.ds(0, part), :] = state[k * part : (k + 1) * part]


def own_state(x, step_t, decay_t, b, count):
    heads, toks = decay_t.shape
    part = x.shape[1] // count
    return pl.pallas_call(
        state_kernel,
        out_shape=[
            jax.ShapeDtypeStruct((count, part + 16, b.shape[1]), BF),
            jax.ShapeDtypeStruct((heads, toks), F32),
        ],
        compiler_params=params(56),
        name="own_state",
    )(x, step_t, decay_t, b)


def prefix_kernel(place_ref, got, start, back):
    count, part, _ = back.shape
    heads = 16
    held = max(1, heads // count)
    group = part // held
    first = place_ref[0] * heads // count
    row = lax.broadcasted_iota(jnp.int32, (heads, LANES), 0)
    carries = [start[pl.ds(h * group, group), :] for h in range(held)]
    for turn in range(count):
        extra = got[turn, pl.ds(part, 16), :].astype(F32)
        scale = extra[:, :1] + extra[:, LANES // 2 : LANES // 2 + 1]
        for h in range(held):
            spot = pl.ds(h * group, group)
            back[turn, spot, :] = carries[h].astype(BF)
            factor = jnp.sum(jnp.where(row == first + h, scale, 0.0), axis=0, keepdims=True)
            carries[h] = factor * carries[h] + got[turn, spot, :].astype(F32)


def entering_state(place, got, init_rows):
    count, rows, width = got.shape
    part = rows - 16
    return pl.pallas_call(
        prefix_kernel,
        grid_spec=pltpu.PrefetchScalarGridSpec(
            num_scalar_prefetch=1,
            grid=(1,),
            in_specs=[
                whole(count, rows, width),
                pl.BlockSpec((part, width), lambda _, place: (place[0], 0)),
            ],
            out_specs=whole(count, part, width),
        ),
        out_shape=jax.ShapeDtypeStruct((count, part, width), BF),
        compiler_params=params(56),
        name="prefix",
    )(place.reshape(1), got, init_rows)


def within_kernel(skip, x, step_t, cum_t, b, c, out):
    heads, toks = cum_t.shape
    row = lax.broadcasted_iota(jnp.int32, (toks, toks), 0)
    col = lax.broadcasted_iota(jnp.int32, (toks, toks), 1)
    causal = row >= col
    nt = (((1,), (1,)), ((), ()))
    scores = lax.dot_general(c[...], b[...], nt, preferred_element_type=F32)
    cum = cum_t[...].T
    for p in range(heads // 2):
        pair = x[:, p * LANES : (p + 1) * LANES]
        sums = []
        for h in (2 * p, 2 * p + 1):
            gap = cum[:, h : h + 1] - cum_t[h : h + 1, :]
            decay = jnp.where(causal, jnp.exp(jnp.where(causal, gap, 0.0)), 0.0)
            weights = (decay * scores * step_t[h : h + 1, :]).astype(BF)
            sums.append(jnp.dot(weights, pair, preferred_element_type=F32))
        gain = by_pair(skip[2 * p], skip[2 * p + 1], toks)
        out[:, p * LANES : (p + 1) * LANES] = (
            by_pair(sums[0], sums[1], toks) + gain * pair.astype(F32)
        )


def within_block(skip, x, step_t, cum_t, b, c):
    toks, inner = x.shape
    heads = cum_t.shape[0]
    vmem = pl.BlockSpec(memory_space=pltpu.VMEM)
    return pl.pallas_call(
        within_kernel,
        in_specs=[pl.BlockSpec(memory_space=pltpu.SMEM)] + [vmem] * 5,
        out_shape=jax.ShapeDtypeStruct((toks, inner), F32),
        compiler_params=params(56),
        cost_estimate=pl.CostEstimate(
            flops=4 * heads * toks * toks * LANES,
            bytes_accessed=6 * toks * inner,
            transcendentals=heads * toks * toks,
        ),
        name="within_block",
    )(skip, x, step_t, cum_t, b, c)


def fetch(sems, *pairs):
    copies = [pltpu.make_async_copy(src, dst, sems.at[i]) for i, (src, dst) in enumerate(pairs)]
    for copy in copies:
        copy.start()
    return copies


def cuts_of(ref, count):
    rows = ref.shape[0] // count
    return [ref.at[pl.ds(k * rows, rows)] for k in range(count)]


def quarters(place_ref, share):
    return [pl.ds(pl.multiple_of((place_ref[0] ^ k) * share, share), share) for k in range(4)]


def tail_kernel(
    place_ref, c_in, cum_in, gain_in, arriving_in, direct_in, z_in, weight_in,
    near, last, keep, passing,
    c, cum_t, gain, arriving, direct, z, weight, normed, sems,
):
    heads, toks = cum_t.shape
    share = near.shape[1]
    copies = fetch(
        sems,
        (cum_in, cum_t),
        (gain_in, gain),
        (c_in, c),
        (arriving_in, arriving),
        (z_in, z),
        (direct_in, direct),
        *zip(cuts_of(weight_in, 8), cuts_of(weight, 8)),
    )
    for copy in copies[:6]:
        copy.wait()
    grown = jnp.exp(cum_t[...]).T
    lane = lax.broadcasted_iota(jnp.int32, (toks, LANES), 1)
    left = lane < LANES // 2
    nt = (((1,), (1,)), ((), ()))
    for p in range(heads // 2):
        spot = pl.ds(p * LANES, LANES)
        inter = lax.dot_general(c[...], arriving[spot, :], nt, preferred_element_type=F32)
        factor = by_pair(grown[:, 2 * p : 2 * p + 1], grown[:, 2 * p + 1 : 2 * p + 2], toks)
        wide = z[:, spot].astype(F32)
        gated = (direct[:, spot] + inter * factor) * (wide * (1.0 / (1.0 + jnp.exp(-wide))))
        square = gated * gated
        first = jnp.sum(jnp.where(left, square, 0.0), axis=1, keepdims=True)
        second = jnp.sum(jnp.where(left, 0.0, square), axis=1, keepdims=True)
        mean = by_pair(first, second, toks) * (2.0 / LANES)
        normed[:, spot] = (gated * lax.rsqrt(mean + 1e-05) * gain[:, spot]).astype(BF)
    for copy in copies[6:]:
        copy.wait()
    spots = quarters(place_ref, share)
    for k, out in ((3, last), (1, near), (2, passing), (0, keep)):
        part = jnp.dot(normed[...], weight[:, spots[k]], preferred_element_type=F32)
        out[...] = part.astype(out.dtype)


def mixer_tail(place, c, arriving, cum_t, direct, z, gain, weight):
    heads, toks = cum_t.shape
    inner, width = weight.shape
    share = width // 4
    operands = (c, cum_t, gain.reshape(1, inner), arriving, direct, z, weight)
    return pl.pallas_call(
        tail_kernel,
        in_specs=[pl.BlockSpec(memory_space=pltpu.SMEM)]
        + [pl.BlockSpec(memory_space=pl.ANY)] * len(operands),
        out_shape=[jax.ShapeDtypeStruct((toks, share), kind) for kind in (BF, BF, F32, F32)],
        scratch_shapes=[pltpu.VMEM(a.shape, a.dtype) for a in operands]
        + [pltpu.VMEM((toks, inner), BF), pltpu.SemaphoreType.DMA((14,))],
        compiler_params=params(56),
        cost_estimate=pl.CostEstimate(
            flops=2 * toks * inner * width,
            bytes_accessed=2 * inner * width + 14 * toks * inner,
            transcendentals=toks * inner,
        ),
        name="mixer_tail",
    )(place.reshape(1), *operands)


def expert_kernel(
    place_ref, gain_in, own_in, near_in, far_in, last_in, wg_in, wu_in, wd_in,
    near_out, last_out, keep_out, pass_out,
    gain, own, near, far, last, wg, wu, wd, rows, act, sems,
):
    count, share = own.shape
    width = 4 * share
    tile = min(count, 256)
    copies = fetch(
        sems,
        (gain_in, gain),
        (own_in, own),
        (near_in, near),
        (far_in, far),
        (last_in, last),
        *zip(cuts_of(wg_in, 4), cuts_of(wg, 4)),
        *zip(cuts_of(wu_in, 4), cuts_of(wu, 4)),
        *zip(cuts_of(wd_in, 4), cuts_of(wd, 4)),
    )
    spots = quarters(place_ref, share)
    for copy in copies[:5]:
        copy.wait()

    @pl.loop(0, count, step=64)
    def _(start):
        spot = pl.ds(pl.multiple_of(start, 64), 64)
        wide = [p[spot, :].astype(F32) for p in (own, near, far, last)]
        square = sum(jnp.sum(w * w, axis=1, keepdims=True) for w in wide)
        scale = lax.rsqrt(square * (1.0 / width) + 1e-05)
        for k in range(4):
            rows[k, spot, :] = (wide[k] * scale * gain[:, spots[k]]).astype(BF)

    for copy in copies[5:13]:
        copy.wait()

    @pl.loop(0, count, step=tile)
    def _(start):
        spot = pl.ds(pl.multiple_of(start, tile), tile)
        gate = up = 0.0
        for k in range(4):
            part = rows[k, spot, :]
            gate += jnp.dot(part, wg[spots[k], :], preferred_element_type=F32)
            up += jnp.dot(part, wu[spots[k], :], preferred_element_type=F32)
        act[spot, :] = (gate * (1.0 / (1.0 + jnp.exp(-gate))) * up).astype(BF)

    for copy in copies[13:]:
        copy.wait()

    @pl.loop(0, count, step=tile)
    def _(start):
        spot = pl.ds(pl.multiple_of(start, tile), tile)
        part = act[spot, :]
        for k, out in ((3, last_out), (1, near_out), (2, pass_out), (0, keep_out)):
            down = jnp.dot(part, wd[:, spots[k]], preferred_element_type=F32)
            out[spot, :] = down.astype(BF)


def run_expert(place, gain, own, near, far, last, wg, wu, wd):
    rows, share = own.shape
    width, inner = wg.shape
    operands = (gain.reshape(1, width), own, near, far, last, wg, wu, wd)
    return pl.pallas_call(
        expert_kernel,
        in_specs=[pl.BlockSpec(memory_space=pltpu.SMEM)]
        + [pl.BlockSpec(memory_space=pl.ANY)] * len(operands),
        out_shape=[jax.ShapeDtypeStruct((rows, share), BF)] * 4,
        scratch_shapes=[pltpu.VMEM(a.shape, a.dtype) for a in operands]
        + [
            pltpu.VMEM((4, rows, share), BF),
            pltpu.VMEM((rows, inner), BF),
            pltpu.SemaphoreType.DMA((17,)),
        ],
        compiler_params=params(56),
        cost_estimate=pl.CostEstimate(
            flops=6 * rows * width * inner,
            bytes_accessed=6 * width * inner + 4 * rows * width,
            transcendentals=rows * inner,
        ),
        name="expert",
    )(place.reshape(1), *operands)


def body(
    tokens,
    input_heads,
    z_gate,
    b_proj,
    c_proj,
    step_size,
    decay_log,
    skip_gain,
    init_state,
    norm_gain,
    out_weight,
    moe_gain,
    routes,
    route_weights,
    w_gate,
    w_up,
    w_down,
):
    tok_rows, inner = input_heads.shape
    state_size = init_state.shape[2]
    seq_count = lax.axis_size("seq")
    place = lax.axis_index("tp")
    step_t = step_size.T
    outgoing, cum_t = own_state(input_heads, step_t, decay_log.T, b_proj, seq_count)
    got = exchange(outgoing)
    direct = within_block(skip_gain, input_heads, step_t, cum_t, b_proj, c_proj)
    back = entering_state(lax.axis_index("seq"), got, init_state.reshape(inner, state_size))
    arriving = exchange(back).reshape(inner, state_size)
    to_near, to_last, keep, passing = mixer_tail(
        place, c_proj, arriving, cum_t, direct, z_gate, norm_gain, out_weight
    )

    model_width = out_weight.shape[1]
    share = model_width // 4
    expert_count = w_gate.shape[0] * seq_count
    slot_count = 4 * tok_rows // seq_count
    top_count = routes.shape[1]
    items = top_count * tok_rows
    slots = expert_count * slot_count
    flat_expert = routes.T.reshape(-1)
    onehot = flat_expert[:, None] == jnp.arange(expert_count, dtype=jnp.int32)[None, :]
    before = jnp.arange(items)[:, None] > jnp.arange(items)[None, :]
    earlier = jnp.dot(before.astype(BF), onehot.astype(BF), preferred_element_type=F32)
    rank = jnp.sum(jnp.where(onehot, earlier, 0.0), axis=1).astype(jnp.int32)
    placed = flat_expert * slot_count + rank
    spots = placed[:, None] == jnp.arange(slots, dtype=jnp.int32)[None, :]
    pick = spots.astype(BF)
    fill = jnp.any(spots.reshape(top_count, tok_rows, slots), axis=0).astype(BF)

    from_last = swap(to_last, 1)
    from_near = swap(to_near, 1)
    from_far = swap((passing + from_last.astype(F32)).astype(BF), 2)
    own_tokens = lax.dynamic_slice_in_dim(tokens, place * share, share, 1)
    projected = keep + from_near.astype(F32) + from_far.astype(F32)
    hidden = (own_tokens.astype(F32) + projected).astype(BF)
    outgoing = lax.dot_general(
        fill, hidden, (((0,), (0,)), ((), ())), preferred_element_type=F32
    ).astype(BF)
    arrived = exchange(outgoing.reshape(expert_count, slot_count, share)).reshape(slots, share)

    far = swap(arrived, 2)
    near = swap(arrived, 1)
    last = swap(far, 1)
    to_near, to_last, keep, passing = run_expert(
        place, moe_gain, arrived, near, far, last, w_gate[0], w_up[0], w_down[0]
    )
    from_last = swap(to_last, 1)
    from_near = swap(to_near, 1)
    from_far = swap((passing.astype(F32) + from_last.astype(F32)).astype(BF), 2)
    results = (keep.astype(F32) + from_near.astype(F32) + from_far.astype(F32)).astype(BF)
    results = results.reshape(expert_count, slot_count, share)
    returned = exchange(results).reshape(slots, share)
    chosen = jnp.dot(pick, returned, preferred_element_type=F32).reshape(
        top_count, tok_rows, share
    )
    mixed_out = hidden.astype(F32) + jnp.sum(route_weights.T[:, :, None] * chosen, axis=0)
    return mixed_out.astype(BF)


def solution(mesh):
    in_specs = (
        P("seq", None),
        P("seq", "tp"),
        P("seq", "tp"),
        P("seq", None),
        P("seq", None),
        P("seq", "tp"),
        P("seq", "tp"),
        P("tp"),
        P("tp", None, None),
        P("tp"),
        P("tp", None),
        P(),
        P("seq", None),
        P("seq", None),
        P("seq", None, "tp"),
        P("seq", None, "tp"),
        P("seq", "tp", None),
    )
    out_specs = P("seq", "tp")
    return jax.shard_map(body, mesh=mesh, in_specs=in_specs, out_specs=out_specs, check_vma=False)
```

```python
import jax
import jax.numpy as jnp
from jax import lax
from jax.experimental import pallas as pl
from jax.experimental.pallas import tpu as pltpu
from jax.sharding import PartitionSpec as P

BF = jnp.bfloat16
F32 = jnp.float32
MIB = 1024 * 1024
LANES = 128


def swap(value, bit):
    count = lax.axis_size("tp")
    return lax.ppermute(value, "tp", [(i, i ^ bit) for i in range(count)])


def exchange(value):
    return lax.all_to_all(value, "seq", split_axis=0, concat_axis=0, tiled=True)


def after(value, *others):
    return lax.optimization_barrier((value, *others))[0]


def in_hbm(value):
    return pltpu.with_memory_space_constraint(value, pltpu.HBM)


def params(mib):
    return pltpu.CompilerParams(vmem_limit_bytes=mib * MIB)


def whole(*shape):
    return pl.BlockSpec(shape, lambda *_: (0,) * len(shape))


def by_pair(left, right, size):
    lane = lax.broadcasted_iota(jnp.int32, (size, LANES), 1)
    return jnp.where(lane < LANES // 2, left, right)


def state_kernel(x, step_t, decay_t, b, out, cum_out):
    count, rows, _ = out.shape
    part = rows - 16
    heads, toks = decay_t.shape
    row = lax.broadcasted_iota(jnp.int32, (toks, toks), 0)
    col = lax.broadcasted_iota(jnp.int32, (toks, toks), 1)
    upper = (row <= col).astype(F32)
    cum_t = jnp.dot(
        decay_t[...], upper, precision=lax.Precision.HIGHEST, preferred_element_type=F32
    )
    cum_out[...] = cum_t
    end = cum_t[:, toks - 1 : toks]
    scale = (jnp.exp(end - cum_t) * step_t[...]).T
    decay = jnp.broadcast_to(jnp.exp(end), (heads, LANES))
    high = decay.astype(BF).astype(F32)
    extra = by_pair(high, decay - high, heads).astype(BF)
    for k in range(count):
        out[k, pl.ds(part, 16), :] = extra
    for p in range(heads // 2):
        pair = x[:, p * LANES : (p + 1) * LANES].astype(F32)
        factor = by_pair(scale[:, 2 * p : 2 * p + 1], scale[:, 2 * p + 1 : 2 * p + 2], toks)
        state = lax.dot_general(
            (pair * factor).astype(BF),
            b[...],
            (((0,), (0,)), ((), ())),
            preferred_element_type=F32,
        ).astype(BF)
        for k in range(LANES // part):
            out[p * (LANES // part) + k, pl.ds(0, part), :] = state[k * part : (k + 1) * part]


def own_state(x, step_t, decay_t, b, count):
    heads, toks = decay_t.shape
    part = x.shape[1] // count
    return pl.pallas_call(
        state_kernel,
        out_shape=[
            jax.ShapeDtypeStruct((count, part + 16, b.shape[1]), BF),
            jax.ShapeDtypeStruct((heads, toks), F32),
        ],
        compiler_params=params(24),
        name="own_state",
    )(in_hbm(x), in_hbm(step_t), in_hbm(decay_t), in_hbm(b))


def prefix_kernel(place_ref, got, start, back):
    count, part, _ = back.shape
    heads = 16
    held = max(1, heads // count)
    group = part // held
    first = place_ref[0] * heads // count
    row = lax.broadcasted_iota(jnp.int32, (heads, LANES), 0)
    carries = [start[pl.ds(h * group, group), :] for h in range(held)]
    for turn in range(count):
        extra = got[turn, pl.ds(part, 16), :].astype(F32)
        scale = extra[:, :1] + extra[:, LANES // 2 : LANES // 2 + 1]
        for h in range(held):
            spot = pl.ds(h * group, group)
            back[turn, spot, :] = carries[h].astype(BF)
            factor = jnp.sum(jnp.where(row == first + h, scale, 0.0), axis=0, keepdims=True)
            carries[h] = factor * carries[h] + got[turn, spot, :].astype(F32)


def entering_state(got, init_rows):
    count, rows, width = got.shape
    part = rows - 16
    place = lax.axis_index("seq")
    start = lax.dynamic_slice_in_dim(init_rows, place * part, part, 0)
    vmem = pl.BlockSpec(memory_space=pltpu.VMEM)
    return pl.pallas_call(
        prefix_kernel,
        in_specs=[pl.BlockSpec(memory_space=pltpu.SMEM), vmem, vmem],
        out_shape=jax.ShapeDtypeStruct((count, part, width), BF),
        compiler_params=params(24),
        name="prefix",
    )(place.reshape(1), got, start)


def within_kernel(skip, x, step_t, cum_t, b, c, out):
    heads, toks = cum_t.shape
    row = lax.broadcasted_iota(jnp.int32, (toks, toks), 0)
    col = lax.broadcasted_iota(jnp.int32, (toks, toks), 1)
    causal = row >= col
    nt = (((1,), (1,)), ((), ()))
    scores = lax.dot_general(c[...], b[...], nt, preferred_element_type=F32)
    cum = cum_t[...].T
    for p in range(heads // 2):
        pair = x[:, p * LANES : (p + 1) * LANES]
        sums = []
        for h in (2 * p, 2 * p + 1):
            gap = cum[:, h : h + 1] - cum_t[h : h + 1, :]
            decay = jnp.where(causal, jnp.exp(jnp.where(causal, gap, 0.0)), 0.0)
            weights = (decay * scores * step_t[h : h + 1, :]).astype(BF)
            sums.append(jnp.dot(weights, pair, preferred_element_type=F32))
        gain = by_pair(skip[2 * p], skip[2 * p + 1], toks)
        out[:, p * LANES : (p + 1) * LANES] = (
            by_pair(sums[0], sums[1], toks) + gain * pair.astype(F32)
        )


def within_block(skip, x, step_t, cum_t, b, c):
    toks, inner = x.shape
    heads = cum_t.shape[0]
    vmem = pl.BlockSpec(memory_space=pltpu.VMEM)
    return pl.pallas_call(
        within_kernel,
        in_specs=[pl.BlockSpec(memory_space=pltpu.SMEM)] + [vmem] * 5,
        out_shape=jax.ShapeDtypeStruct((toks, inner), F32),
        compiler_params=params(24),
        cost_estimate=pl.CostEstimate(
            flops=4 * heads * toks * toks * LANES,
            bytes_accessed=6 * toks * inner,
            transcendentals=heads * toks * toks,
        ),
        name="within_block",
    )(skip, in_hbm(x), in_hbm(step_t), cum_t, in_hbm(b), in_hbm(c))


def fetch(sems, *pairs):
    copies = [pltpu.make_async_copy(src, dst, sems.at[i]) for i, (src, dst) in enumerate(pairs)]
    for copy in copies:
        copy.start()
    return copies


def cuts_of(ref, count):
    rows = ref.shape[0] // count
    return [ref.at[pl.ds(k * rows, rows)] for k in range(count)]


def quarters(place_ref, share):
    return [pl.ds(pl.multiple_of((place_ref[0] ^ k) * share, share), share) for k in range(4)]


def tail_kernel(
    place_ref, c_in, cum_in, gain_in, arriving_in, direct_in, z_in, weight_in,
    near, last, keep, passing,
    c, cum_t, gain, arriving, direct, z, weight, normed, sems,
):
    heads, toks = cum_t.shape
    share = near.shape[1]
    copies = fetch(
        sems,
        (cum_in, cum_t),
        (gain_in, gain),
        (c_in, c),
        (arriving_in, arriving),
        (z_in, z),
        (direct_in, direct),
        *zip(cuts_of(weight_in, 8), cuts_of(weight, 8)),
    )
    for copy in copies[:6]:
        copy.wait()
    grown = jnp.exp(cum_t[...]).T
    lane = lax.broadcasted_iota(jnp.int32, (toks, LANES), 1)
    left = lane < LANES // 2
    nt = (((1,), (1,)), ((), ()))
    for p in range(heads // 2):
        spot = pl.ds(p * LANES, LANES)
        inter = lax.dot_general(c[...], arriving[spot, :], nt, preferred_element_type=F32)
        factor = by_pair(grown[:, 2 * p : 2 * p + 1], grown[:, 2 * p + 1 : 2 * p + 2], toks)
        wide = z[:, spot].astype(F32)
        gated = (direct[:, spot] + inter * factor) * (wide * (1.0 / (1.0 + jnp.exp(-wide))))
        square = gated * gated
        first = jnp.sum(jnp.where(left, square, 0.0), axis=1, keepdims=True)
        second = jnp.sum(jnp.where(left, 0.0, square), axis=1, keepdims=True)
        mean = by_pair(first, second, toks) * (2.0 / LANES)
        normed[:, spot] = (gated * lax.rsqrt(mean + 1e-05) * gain[:, spot]).astype(BF)
    for copy in copies[6:]:
        copy.wait()
    spots = quarters(place_ref, share)
    for k, out in ((3, last), (1, near), (2, passing), (0, keep)):
        part = jnp.dot(normed[...], weight[:, spots[k]], preferred_element_type=F32)
        out[...] = part.astype(out.dtype)


def mixer_tail(place, c, arriving, cum_t, direct, z, gain, weight):
    heads, toks = cum_t.shape
    inner, width = weight.shape
    share = width // 4
    operands = (c, cum_t, gain.reshape(1, inner), arriving, direct, z, weight)
    fixed = (0, 2, 5, 6)
    operands = [in_hbm(a) if i in fixed else a for i, a in enumerate(operands)]
    return pl.pallas_call(
        tail_kernel,
        in_specs=[pl.BlockSpec(memory_space=pltpu.SMEM)]
        + [pl.BlockSpec(memory_space=pl.ANY)] * len(operands),
        out_shape=[jax.ShapeDtypeStruct((toks, share), kind) for kind in (BF, BF, F32, F32)],
        scratch_shapes=[pltpu.VMEM(a.shape, a.dtype) for a in operands]
        + [pltpu.VMEM((toks, inner), BF), pltpu.SemaphoreType.DMA((14,))],
        compiler_params=params(24),
        cost_estimate=pl.CostEstimate(
            flops=2 * toks * inner * width,
            bytes_accessed=2 * inner * width + 14 * toks * inner,
            transcendentals=toks * inner,
        ),
        name="mixer_tail",
    )(place.reshape(1), *operands)


def expert_kernel(
    place_ref, gain_in, own_in, near_in, far_in, last_in, wg_in, wu_in, wd_in,
    near_out, last_out, keep_out, pass_out,
    gain, own, near, far, last, wg, wu, wd, rows, sems,
):
    count, share = own.shape
    width = 4 * share
    spots = quarters(place_ref, share)
    copies = fetch(
        sems,
        (gain_in, gain),
        (own_in, own),
        (near_in, near),
        (far_in, far),
        (last_in, last),
        *((w_in.at[s], w.at[s]) for s in spots for w_in, w in ((wg_in, wg), (wu_in, wu))),
        *zip(cuts_of(wd_in, 4), cuts_of(wd, 4)),
    )
    for copy in copies[:5]:
        copy.wait()

    @pl.loop(0, count, step=64)
    def _(start):
        spot = pl.ds(pl.multiple_of(start, 64), 64)
        wide = [p[spot, :].astype(F32) for p in (own, near, far, last)]
        square = sum(jnp.sum(w * w, axis=1, keepdims=True) for w in wide)
        scale = lax.rsqrt(square * (1.0 / width) + 1e-05)
        for k in range(4):
            rows[k, spot, :] = (wide[k] * scale * gain[:, spots[k]]).astype(BF)

    gate = up = 0.0
    for k in range(4):
        copies[5 + 2 * k].wait()
        gate += jnp.dot(rows[k], wg[spots[k], :], preferred_element_type=F32)
        copies[6 + 2 * k].wait()
        up += jnp.dot(rows[k], wu[spots[k], :], preferred_element_type=F32)
    act = (gate * (1.0 / (1.0 + jnp.exp(-gate))) * up).astype(BF)
    for copy in copies[13:]:
        copy.wait()
    for k, out in ((3, last_out), (1, near_out), (2, pass_out), (0, keep_out)):
        out[...] = jnp.dot(act, wd[:, spots[k]], preferred_element_type=F32).astype(BF)


def run_expert(place, gain, own, near, far, last, wg, wu, wd):
    rows, share = own.shape
    width, inner = wg.shape
    weights = (in_hbm(wg), in_hbm(wu), in_hbm(wd))
    operands = (in_hbm(gain.reshape(1, width)), own, near, far, last, *weights)
    return pl.pallas_call(
        expert_kernel,
        in_specs=[pl.BlockSpec(memory_space=pltpu.SMEM)]
        + [pl.BlockSpec(memory_space=pl.ANY)] * len(operands),
        out_shape=[jax.ShapeDtypeStruct((rows, share), BF)] * 4,
        scratch_shapes=[pltpu.VMEM(a.shape, a.dtype) for a in operands]
        + [
            pltpu.VMEM((4, rows, share), BF),
            pltpu.SemaphoreType.DMA((17,)),
        ],
        compiler_params=params(24),
        cost_estimate=pl.CostEstimate(
            flops=6 * rows * width * inner,
            bytes_accessed=6 * width * inner + 4 * rows * width,
            transcendentals=rows * inner,
        ),
        name="expert",
    )(place.reshape(1), *operands)


def body(
    tokens,
    input_heads,
    z_gate,
    b_proj,
    c_proj,
    step_size,
    decay_log,
    skip_gain,
    init_state,
    norm_gain,
    out_weight,
    moe_gain,
    routes,
    route_weights,
    w_gate,
    w_up,
    w_down,
):
    tok_rows, inner = input_heads.shape
    state_size = init_state.shape[2]
    seq_count = lax.axis_size("seq")
    place = lax.axis_index("tp")
    step_t = step_size.T
    outgoing, cum_t = own_state(input_heads, step_t, decay_log.T, b_proj, seq_count)
    got = exchange(outgoing)
    direct = within_block(skip_gain, input_heads, step_t, cum_t, b_proj, c_proj)
    back = entering_state(got, init_state.reshape(inner, state_size))
    arriving = exchange(back).reshape(inner, state_size)
    to_near, to_last, keep, passing = mixer_tail(
        place, c_proj, arriving, cum_t, direct, z_gate, norm_gain, out_weight
    )

    model_width = out_weight.shape[1]
    share = model_width // 4
    expert_count = w_gate.shape[0] * seq_count
    slot_count = 4 * tok_rows // seq_count
    top_count = routes.shape[1]
    items = top_count * tok_rows
    slots = expert_count * slot_count
    flat_expert = routes.T.reshape(-1)
    onehot = flat_expert[:, None] == jnp.arange(expert_count, dtype=jnp.int32)[None, :]
    before = jnp.arange(items)[:, None] > jnp.arange(items)[None, :]
    earlier = jnp.dot(before.astype(BF), onehot.astype(BF), preferred_element_type=F32)
    rank = jnp.sum(jnp.where(onehot, earlier, 0.0), axis=1).astype(jnp.int32)
    placed = flat_expert * slot_count + rank
    spots = placed[:, None] == jnp.arange(slots, dtype=jnp.int32)[None, :]
    pick = spots.astype(BF)
    fill = jnp.any(spots.reshape(top_count, tok_rows, slots), axis=0).astype(BF)

    from_last = swap(to_last, 1)
    from_near = swap(to_near, 1)
    from_far = swap((passing + from_last.astype(F32)).astype(BF), 2)
    own_tokens = lax.dynamic_slice_in_dim(tokens, place * share, share, 1)
    projected = keep + from_near.astype(F32) + from_far.astype(F32)
    hidden = (own_tokens.astype(F32) + projected).astype(BF)
    outgoing = lax.dot_general(
        fill, hidden, (((0,), (0,)), ((), ())), preferred_element_type=F32
    ).astype(BF)
    arrived = exchange(outgoing.reshape(expert_count, slot_count, share)).reshape(slots, share)

    cut = slots // 2
    own = [arrived[:cut], arrived[cut:]]
    far = [swap(part, 2) for part in own]
    near = [swap(part, 1) for part in own]
    weights = (w_gate[0], w_up[0], w_down[0])
    last = swap(far[0], 1)
    to_near0, to_last0, keep0, pass0 = run_expert(
        place, moe_gain, own[0], near[0], far[0], last, *weights
    )
    from_last0 = swap(to_last0, 1)
    last = swap(after(far[1], to_last0), 1)
    pass0 = (pass0.astype(F32) + from_last0.astype(F32)).astype(BF)
    from_far0 = swap(pass0, 2)
    to_near1, to_last1, keep1, pass1 = run_expert(
        place, moe_gain, after(own[1], pass0), near[1], far[1], last, *weights
    )
    from_near0 = swap(to_near0, 1)
    from_last1 = swap(after(to_last1, from_far0), 1)
    from_near1 = swap(to_near1, 1)
    from_far1 = swap((pass1.astype(F32) + from_last1.astype(F32)).astype(BF), 2)
    results = [
        (keep.astype(F32) + from_near.astype(F32) + from_far.astype(F32)).astype(BF)
        for keep, from_near, from_far in (
            (keep0, from_near0, from_far0),
            (keep1, from_near1, from_far1),
        )
    ]
    results = jnp.concatenate(results).reshape(expert_count, slot_count, share)
    returned = exchange(results).reshape(slots, share)
    chosen = jnp.dot(pick, returned, preferred_element_type=F32).reshape(
        top_count, tok_rows, share
    )
    mixed_out = hidden.astype(F32) + jnp.sum(route_weights.T[:, :, None] * chosen, axis=0)
    return mixed_out.astype(BF)


def solution(mesh):
    in_specs = (
        P("seq", None),
        P("seq", "tp"),
        P("seq", "tp"),
        P("seq", None),
        P("seq", None),
        P("seq", "tp"),
        P("seq", "tp"),
        P("tp"),
        P("tp", None, None),
        P("tp"),
        P("tp", None),
        P(),
        P("seq", None),
        P("seq", None),
        P("seq", None, "tp"),
        P("seq", None, "tp"),
        P("seq", "tp", None),
    )
    out_specs = P("seq", "tp")
    return jax.shard_map(body, mesh=mesh, in_specs=in_specs, out_specs=out_specs, check_vma=False)
```

```python
import jax
import jax.numpy as jnp
from jax import lax
from jax.experimental import pallas as pl
from jax.experimental.pallas import tpu as pltpu
from jax.sharding import PartitionSpec as P

BF = jnp.bfloat16
F32 = jnp.float32
MIB = 1024 * 1024
LANES = 128


def swap(value, bit):
    count = lax.axis_size("tp")
    return lax.ppermute(value, "tp", [(i, i ^ bit) for i in range(count)])


def exchange(value):
    return lax.all_to_all(value, "seq", split_axis=0, concat_axis=0, tiled=True)


def after(value, *others):
    return lax.optimization_barrier((value, *others))[0]


def in_hbm(value):
    return pltpu.with_memory_space_constraint(value, pltpu.HBM)


def params(mib):
    return pltpu.CompilerParams(vmem_limit_bytes=mib * MIB)


def whole(*shape):
    return pl.BlockSpec(shape, lambda *_: (0,) * len(shape))


def by_pair(left, right, size):
    lane = lax.broadcasted_iota(jnp.int32, (size, LANES), 1)
    return jnp.where(lane < LANES // 2, left, right)


def state_kernel(x, step_t, decay_t, b, out, cum_out):
    count, rows, _ = out.shape
    part = rows - 16
    heads, toks = decay_t.shape
    row = lax.broadcasted_iota(jnp.int32, (toks, toks), 0)
    col = lax.broadcasted_iota(jnp.int32, (toks, toks), 1)
    upper = (row <= col).astype(F32)
    cum_t = jnp.dot(
        decay_t[...], upper, precision=lax.Precision.HIGHEST, preferred_element_type=F32
    )
    cum_out[...] = cum_t
    end = cum_t[:, toks - 1 : toks]
    scale = (jnp.exp(end - cum_t) * step_t[...]).T
    decay = jnp.broadcast_to(jnp.exp(end), (heads, LANES))
    high = decay.astype(BF).astype(F32)
    extra = by_pair(high, decay - high, heads).astype(BF)
    for k in range(count):
        out[k, pl.ds(part, 16), :] = extra
    for p in range(heads // 2):
        pair = x[:, p * LANES : (p + 1) * LANES].astype(F32)
        factor = by_pair(scale[:, 2 * p : 2 * p + 1], scale[:, 2 * p + 1 : 2 * p + 2], toks)
        state = lax.dot_general(
            (pair * factor).astype(BF),
            b[...],
            (((0,), (0,)), ((), ())),
            preferred_element_type=F32,
        ).astype(BF)
        for k in range(LANES // part):
            out[p * (LANES // part) + k, pl.ds(0, part), :] = state[k * part : (k + 1) * part]


def own_state(x, step_t, decay_t, b, count):
    heads, toks = decay_t.shape
    part = x.shape[1] // count
    return pl.pallas_call(
        state_kernel,
        out_shape=[
            jax.ShapeDtypeStruct((count, part + 16, b.shape[1]), BF),
            jax.ShapeDtypeStruct((heads, toks), F32),
        ],
        compiler_params=params(24),
        name="own_state",
    )(in_hbm(x), in_hbm(step_t), in_hbm(decay_t), in_hbm(b))


def prefix_kernel(place_ref, got, start, back):
    count, part, _ = back.shape
    heads = 16
    held = max(1, heads // count)
    group = part // held
    first = place_ref[0] * heads // count
    row = lax.broadcasted_iota(jnp.int32, (heads, LANES), 0)
    carries = [start[pl.ds(h * group, group), :] for h in range(held)]
    for turn in range(count):
        extra = got[turn, pl.ds(part, 16), :].astype(F32)
        scale = extra[:, :1] + extra[:, LANES // 2 : LANES // 2 + 1]
        for h in range(held):
            spot = pl.ds(h * group, group)
            back[turn, spot, :] = carries[h].astype(BF)
            factor = jnp.sum(jnp.where(row == first + h, scale, 0.0), axis=0, keepdims=True)
            carries[h] = factor * carries[h] + got[turn, spot, :].astype(F32)


def entering_state(got, init_rows):
    count, rows, width = got.shape
    part = rows - 16
    place = lax.axis_index("seq")
    start = lax.dynamic_slice_in_dim(init_rows, place * part, part, 0)
    vmem = pl.BlockSpec(memory_space=pltpu.VMEM)
    return pl.pallas_call(
        prefix_kernel,
        in_specs=[pl.BlockSpec(memory_space=pltpu.SMEM), vmem, vmem],
        out_shape=jax.ShapeDtypeStruct((count, part, width), BF),
        compiler_params=params(24),
        name="prefix",
    )(place.reshape(1), got, start)


def within_kernel(skip, x, step_t, cum_t, b, c, out):
    heads, toks = cum_t.shape
    row = lax.broadcasted_iota(jnp.int32, (toks, toks), 0)
    col = lax.broadcasted_iota(jnp.int32, (toks, toks), 1)
    causal = row >= col
    nt = (((1,), (1,)), ((), ()))
    scores = lax.dot_general(c[...], b[...], nt, preferred_element_type=F32)
    cum = cum_t[...].T
    for p in range(heads // 2):
        pair = x[:, p * LANES : (p + 1) * LANES]
        sums = []
        for h in (2 * p, 2 * p + 1):
            gap = cum[:, h : h + 1] - cum_t[h : h + 1, :]
            decay = jnp.where(causal, jnp.exp(jnp.where(causal, gap, 0.0)), 0.0)
            weights = (decay * scores * step_t[h : h + 1, :]).astype(BF)
            sums.append(jnp.dot(weights, pair, preferred_element_type=F32))
        gain = by_pair(skip[2 * p], skip[2 * p + 1], toks)
        out[:, p * LANES : (p + 1) * LANES] = (
            by_pair(sums[0], sums[1], toks) + gain * pair.astype(F32)
        )


def within_block(skip, x, step_t, cum_t, b, c):
    toks, inner = x.shape
    heads = cum_t.shape[0]
    vmem = pl.BlockSpec(memory_space=pltpu.VMEM)
    return pl.pallas_call(
        within_kernel,
        in_specs=[pl.BlockSpec(memory_space=pltpu.SMEM)] + [vmem] * 5,
        out_shape=jax.ShapeDtypeStruct((toks, inner), F32),
        compiler_params=params(24),
        cost_estimate=pl.CostEstimate(
            flops=4 * heads * toks * toks * LANES,
            bytes_accessed=6 * toks * inner,
            transcendentals=heads * toks * toks,
        ),
        name="within_block",
    )(skip, in_hbm(x), in_hbm(step_t), cum_t, in_hbm(b), in_hbm(c))


def fetch(sems, *pairs):
    copies = [pltpu.make_async_copy(src, dst, sems.at[i]) for i, (src, dst) in enumerate(pairs)]
    for copy in copies:
        copy.start()
    return copies


def cuts_of(ref, count):
    rows = ref.shape[0] // count
    return [ref.at[pl.ds(k * rows, rows)] for k in range(count)]


def quarters(place_ref, share):
    return [pl.ds(pl.multiple_of((place_ref[0] ^ k) * share, share), share) for k in range(4)]


def tail_kernel(
    place_ref, c_in, cum_in, gain_in, arriving_in, direct_in, z_in, weight_in, tokens_in,
    near, last, keep, passing,
    c, cum_t, gain, arriving, direct, z, weight, tokens, normed, sems,
):
    heads, toks = cum_t.shape
    share = near.shape[1]
    spots = quarters(place_ref, share)
    copies = fetch(
        sems,
        (cum_in, cum_t),
        (gain_in, gain),
        (c_in, c),
        (arriving_in, arriving),
        (z_in, z),
        (direct_in, direct),
        *zip(cuts_of(weight_in, 8), cuts_of(weight, 8)),
        (tokens_in.at[:, spots[0]], tokens),
    )
    for copy in copies[:6]:
        copy.wait()
    grown = jnp.exp(cum_t[...]).T
    lane = lax.broadcasted_iota(jnp.int32, (toks, LANES), 1)
    left = lane < LANES // 2
    nt = (((1,), (1,)), ((), ()))
    for p in range(heads // 2):
        spot = pl.ds(p * LANES, LANES)
        inter = lax.dot_general(c[...], arriving[spot, :], nt, preferred_element_type=F32)
        factor = by_pair(grown[:, 2 * p : 2 * p + 1], grown[:, 2 * p + 1 : 2 * p + 2], toks)
        wide = z[:, spot].astype(F32)
        gated = (direct[:, spot] + inter * factor) * (wide * (1.0 / (1.0 + jnp.exp(-wide))))
        square = gated * gated
        first = jnp.sum(jnp.where(left, square, 0.0), axis=1, keepdims=True)
        second = jnp.sum(jnp.where(left, 0.0, square), axis=1, keepdims=True)
        mean = by_pair(first, second, toks) * (2.0 / LANES)
        normed[:, spot] = (gated * lax.rsqrt(mean + 1e-05) * gain[:, spot]).astype(BF)
    for copy in copies[6:]:
        copy.wait()
    for k, out in ((3, last), (1, near), (2, passing), (0, keep)):
        part = jnp.dot(normed[...], weight[:, spots[k]], preferred_element_type=F32)
        if k == 0:
            part += tokens[...].astype(F32)
        out[...] = part.astype(out.dtype)


def mixer_tail(place, c, arriving, cum_t, direct, z, gain, weight, tokens):
    heads, toks = cum_t.shape
    inner, width = weight.shape
    share = width // 4
    operands = (c, cum_t, gain.reshape(1, inner), arriving, direct, z, weight, tokens)
    fixed = (0, 2, 5, 6, 7)
    operands = [in_hbm(a) if i in fixed else a for i, a in enumerate(operands)]
    return pl.pallas_call(
        tail_kernel,
        in_specs=[pl.BlockSpec(memory_space=pltpu.SMEM)]
        + [pl.BlockSpec(memory_space=pl.ANY)] * len(operands),
        out_shape=[jax.ShapeDtypeStruct((toks, share), kind) for kind in (BF, BF, F32, F32)],
        scratch_shapes=[pltpu.VMEM(a.shape, a.dtype) for a in operands[:-1]]
        + [
            pltpu.VMEM((toks, share), BF),
            pltpu.VMEM((toks, inner), BF),
            pltpu.SemaphoreType.DMA((15,)),
        ],
        compiler_params=params(24),
        cost_estimate=pl.CostEstimate(
            flops=2 * toks * inner * width,
            bytes_accessed=2 * inner * width + 14 * toks * inner,
            transcendentals=toks * inner,
        ),
        name="mixer_tail",
    )(place.reshape(1), *operands)


def expert_kernel(
    place_ref, gain_in, own_in, near_in, far_in, last_in, wg_in, wu_in, wd_in,
    near_out, last_out, keep_out, pass_out,
    gain, own, near, far, last, wg, wu, wd, rows, sems,
):
    count, share = own.shape
    width = 4 * share
    spots = quarters(place_ref, share)
    copies = fetch(
        sems,
        (gain_in, gain),
        (own_in, own),
        (near_in, near),
        (far_in, far),
        (last_in, last),
        *((w_in.at[s], w.at[s]) for s in spots for w_in, w in ((wg_in, wg), (wu_in, wu))),
        *zip(cuts_of(wd_in, 4), cuts_of(wd, 4)),
    )
    for copy in copies[:5]:
        copy.wait()

    @pl.loop(0, count, step=64)
    def _(start):
        spot = pl.ds(pl.multiple_of(start, 64), 64)
        wide = [p[spot, :].astype(F32) for p in (own, near, far, last)]
        square = sum(jnp.sum(w * w, axis=1, keepdims=True) for w in wide)
        scale = lax.rsqrt(square * (1.0 / width) + 1e-05)
        for k in range(4):
            rows[k, spot, :] = (wide[k] * scale * gain[:, spots[k]]).astype(BF)

    gate = up = 0.0
    for k in range(4):
        copies[5 + 2 * k].wait()
        gate += jnp.dot(rows[k], wg[spots[k], :], preferred_element_type=F32)
        copies[6 + 2 * k].wait()
        up += jnp.dot(rows[k], wu[spots[k], :], preferred_element_type=F32)
    act = (gate * (1.0 / (1.0 + jnp.exp(-gate))) * up).astype(BF)
    for copy in copies[13:]:
        copy.wait()
    for k, out in ((3, last_out), (1, near_out), (2, pass_out), (0, keep_out)):
        out[...] = jnp.dot(act, wd[:, spots[k]], preferred_element_type=F32).astype(BF)


def run_expert(place, gain, own, near, far, last, wg, wu, wd):
    rows, share = own.shape
    width, inner = wg.shape
    weights = (in_hbm(wg), in_hbm(wu), in_hbm(wd))
    operands = (in_hbm(gain.reshape(1, width)), own, near, far, last, *weights)
    return pl.pallas_call(
        expert_kernel,
        in_specs=[pl.BlockSpec(memory_space=pltpu.SMEM)]
        + [pl.BlockSpec(memory_space=pl.ANY)] * len(operands),
        out_shape=[jax.ShapeDtypeStruct((rows, share), BF)] * 4,
        scratch_shapes=[pltpu.VMEM(a.shape, a.dtype) for a in operands]
        + [
            pltpu.VMEM((4, rows, share), BF),
            pltpu.SemaphoreType.DMA((17,)),
        ],
        compiler_params=params(24),
        cost_estimate=pl.CostEstimate(
            flops=6 * rows * width * inner,
            bytes_accessed=6 * width * inner + 4 * rows * width,
            transcendentals=rows * inner,
        ),
        name="expert",
    )(place.reshape(1), *operands)


def body(
    tokens,
    input_heads,
    z_gate,
    b_proj,
    c_proj,
    step_size,
    decay_log,
    skip_gain,
    init_state,
    norm_gain,
    out_weight,
    moe_gain,
    routes,
    route_weights,
    w_gate,
    w_up,
    w_down,
):
    tok_rows, inner = input_heads.shape
    state_size = init_state.shape[2]
    seq_count = lax.axis_size("seq")
    place = lax.axis_index("tp")
    step_t = step_size.T
    outgoing, cum_t = own_state(input_heads, step_t, decay_log.T, b_proj, seq_count)
    got = exchange(outgoing)
    direct = within_block(skip_gain, input_heads, step_t, cum_t, b_proj, c_proj)
    back = entering_state(got, init_state.reshape(inner, state_size))
    arriving = exchange(back).reshape(inner, state_size)
    to_near, to_last, keep, passing = mixer_tail(
        place, c_proj, arriving, cum_t, direct, z_gate, norm_gain, out_weight, tokens
    )

    model_width = out_weight.shape[1]
    share = model_width // 4
    expert_count = w_gate.shape[0] * seq_count
    slot_count = 4 * tok_rows // seq_count
    top_count = routes.shape[1]
    items = top_count * tok_rows
    slots = expert_count * slot_count
    flat_expert = routes.T.reshape(-1)
    onehot = flat_expert[:, None] == jnp.arange(expert_count, dtype=jnp.int32)[None, :]
    before = jnp.arange(items)[:, None] > jnp.arange(items)[None, :]
    earlier = jnp.dot(before.astype(BF), onehot.astype(BF), preferred_element_type=F32)
    rank = jnp.sum(jnp.where(onehot, earlier, 0.0), axis=1).astype(jnp.int32)
    cut = slot_count // 2
    half = slots // 2
    late = (rank >= cut).astype(jnp.int32)
    placed = late * half + flat_expert * cut + rank - late * cut
    spots = placed[:, None] == jnp.arange(slots, dtype=jnp.int32)[None, :]
    spots = spots.reshape(top_count, tok_rows, slots)
    fill = jnp.any(spots, axis=0).astype(BF)
    combine = jnp.sum(jnp.where(spots, route_weights.T[:, :, None], 0.0), axis=0)

    from_last = swap(to_last, 1)
    from_near = swap(to_near, 1)
    from_far = swap((passing + from_last.astype(F32)).astype(BF), 2)
    hidden = (keep + from_near.astype(F32) + from_far.astype(F32)).astype(BF)

    def dispatch(turn):
        outgoing = lax.dot_general(
            fill[:, turn * half : (turn + 1) * half],
            hidden,
            (((0,), (0,)), ((), ())),
            preferred_element_type=F32,
        ).astype(BF)
        return outgoing.reshape(expert_count, cut, share)

    def combined(turn, results):
        returned = exchange(results.reshape(expert_count, cut, share)).reshape(half, share)
        return jnp.dot(
            combine[:, turn * half : (turn + 1) * half],
            returned.astype(F32),
            precision=lax.Precision.HIGHEST,
            preferred_element_type=F32,
        )

    weights = (w_gate[0], w_up[0], w_down[0])
    own0 = exchange(dispatch(0)).reshape(half, share)
    far0 = swap(own0, 2)
    near0 = swap(own0, 1)
    own1 = exchange(after(dispatch(1), near0)).reshape(half, share)
    last0 = swap(far0, 1)
    to_near0, to_last0, keep0, pass0 = run_expert(
        place, moe_gain, own0, near0, far0, last0, *weights
    )
    own1 = after(own1, to_last0)
    far1 = swap(own1, 2)
    near1 = swap(own1, 1)
    from_last0 = swap(to_last0, 1)
    from_near0 = swap(to_near0, 1)
    pass0 = (pass0.astype(F32) + from_last0.astype(F32)).astype(BF)
    from_far0 = swap(pass0, 2)
    last1 = swap(far1, 1)
    to_near1, to_last1, keep1, pass1 = run_expert(
        place, moe_gain, after(own1, pass0), near1, far1, last1, *weights
    )
    result0 = (keep0.astype(F32) + from_near0.astype(F32) + from_far0.astype(F32)).astype(BF)
    mixed = hidden.astype(F32) + combined(0, result0)
    from_last1 = swap(to_last1, 1)
    from_near1 = swap(to_near1, 1)
    from_far1 = swap((pass1.astype(F32) + from_last1.astype(F32)).astype(BF), 2)
    result1 = (keep1.astype(F32) + from_near1.astype(F32) + from_far1.astype(F32)).astype(BF)
    mixed = mixed + combined(1, result1)
    return mixed.astype(BF)


def solution(mesh):
    in_specs = (
        P("seq", None),
        P("seq", "tp"),
        P("seq", "tp"),
        P("seq", None),
        P("seq", None),
        P("seq", "tp"),
        P("seq", "tp"),
        P("tp"),
        P("tp", None, None),
        P("tp"),
        P("tp", None),
        P(),
        P("seq", None),
        P("seq", None),
        P("seq", None, "tp"),
        P("seq", None, "tp"),
        P("seq", "tp", None),
    )
    out_specs = P("seq", "tp")
    return jax.shard_map(body, mesh=mesh, in_specs=in_specs, out_specs=out_specs, check_vma=False)
```

```python
import jax
import jax.numpy as jnp
from jax import lax
from jax.experimental import pallas as pl
from jax.experimental.pallas import tpu as pltpu
from jax.sharding import PartitionSpec as P

BF = jnp.bfloat16
F32 = jnp.float32
MIB = 1024 * 1024
LANES = 128


def swap(value, bit):
    count = lax.axis_size("tp")
    return lax.ppermute(value, "tp", [(i, i ^ bit) for i in range(count)])


def exchange(value):
    return lax.all_to_all(value, "seq", split_axis=0, concat_axis=0, tiled=True)


def after(value, *others):
    return lax.optimization_barrier((value, *others))[0]


def in_hbm(value):
    return pltpu.with_memory_space_constraint(value, pltpu.HBM)


def params(mib):
    return pltpu.CompilerParams(vmem_limit_bytes=mib * MIB)


def whole(*shape):
    return pl.BlockSpec(shape, lambda *_: (0,) * len(shape))


def by_pair(left, right, size):
    lane = lax.broadcasted_iota(jnp.int32, (size, LANES), 1)
    return jnp.where(lane < LANES // 2, left, right)


def state_kernel(x, step_t, decay_t, b, out, cum_out):
    count, rows, _ = out.shape
    part = rows - 16
    heads, toks = decay_t.shape
    row = lax.broadcasted_iota(jnp.int32, (toks, toks), 0)
    col = lax.broadcasted_iota(jnp.int32, (toks, toks), 1)
    upper = (row <= col).astype(F32)
    cum_t = jnp.dot(
        decay_t[...], upper, precision=lax.Precision.HIGHEST, preferred_element_type=F32
    )
    cum_out[...] = cum_t
    end = cum_t[:, toks - 1 : toks]
    scale = (jnp.exp(end - cum_t) * step_t[...]).T
    decay = jnp.broadcast_to(jnp.exp(end), (heads, LANES))
    high = decay.astype(BF).astype(F32)
    extra = by_pair(high, decay - high, heads).astype(BF)
    for k in range(count):
        out[k, pl.ds(part, 16), :] = extra
    for p in range(heads // 2):
        pair = x[:, p * LANES : (p + 1) * LANES].astype(F32)
        factor = by_pair(scale[:, 2 * p : 2 * p + 1], scale[:, 2 * p + 1 : 2 * p + 2], toks)
        state = lax.dot_general(
            (pair * factor).astype(BF),
            b[...],
            (((0,), (0,)), ((), ())),
            preferred_element_type=F32,
        ).astype(BF)
        for k in range(LANES // part):
            out[p * (LANES // part) + k, pl.ds(0, part), :] = state[k * part : (k + 1) * part]


def own_state(x, step_t, decay_t, b, count):
    heads, toks = decay_t.shape
    part = x.shape[1] // count
    return pl.pallas_call(
        state_kernel,
        out_shape=[
            jax.ShapeDtypeStruct((count, part + 16, b.shape[1]), BF),
            jax.ShapeDtypeStruct((heads, toks), F32),
        ],
        compiler_params=params(8),
        name="own_state",
    )(in_hbm(x), in_hbm(step_t), in_hbm(decay_t), in_hbm(b))


def prefix_kernel(place_ref, got, start, back):
    count, part, _ = back.shape
    heads = 16
    held = max(1, heads // count)
    group = part // held
    first = place_ref[0] * heads // count
    row = lax.broadcasted_iota(jnp.int32, (heads, LANES), 0)
    carries = [start[pl.ds(h * group, group), :] for h in range(held)]
    for turn in range(count):
        extra = got[turn, pl.ds(part, 16), :].astype(F32)
        scale = extra[:, :1] + extra[:, LANES // 2 : LANES // 2 + 1]
        for h in range(held):
            spot = pl.ds(h * group, group)
            back[turn, spot, :] = carries[h].astype(BF)
            factor = jnp.sum(jnp.where(row == first + h, scale, 0.0), axis=0, keepdims=True)
            carries[h] = factor * carries[h] + got[turn, spot, :].astype(F32)


def entering_state(got, init_rows):
    count, rows, width = got.shape
    part = rows - 16
    place = lax.axis_index("seq")
    start = lax.dynamic_slice_in_dim(init_rows, place * part, part, 0)
    vmem = pl.BlockSpec(memory_space=pltpu.VMEM)
    return pl.pallas_call(
        prefix_kernel,
        in_specs=[pl.BlockSpec(memory_space=pltpu.SMEM), vmem, vmem],
        out_shape=jax.ShapeDtypeStruct((count, part, width), BF),
        compiler_params=params(8),
        name="prefix",
    )(place.reshape(1), got, start)


def within_kernel(skip, x, step_t, cum_t, b, c, out):
    heads, toks = cum_t.shape
    row = lax.broadcasted_iota(jnp.int32, (toks, toks), 0)
    col = lax.broadcasted_iota(jnp.int32, (toks, toks), 1)
    causal = row >= col
    nt = (((1,), (1,)), ((), ()))
    scores = lax.dot_general(c[...], b[...], nt, preferred_element_type=F32)
    cum = cum_t[...].T
    for p in range(heads // 2):
        pair = x[:, p * LANES : (p + 1) * LANES]
        sums = []
        for h in (2 * p, 2 * p + 1):
            gap = cum[:, h : h + 1] - cum_t[h : h + 1, :]
            decay = jnp.where(causal, jnp.exp(jnp.where(causal, gap, 0.0)), 0.0)
            weights = (decay * scores * step_t[h : h + 1, :]).astype(BF)
            sums.append(jnp.dot(weights, pair, preferred_element_type=F32))
        gain = by_pair(skip[2 * p], skip[2 * p + 1], toks)
        out[:, p * LANES : (p + 1) * LANES] = (
            by_pair(sums[0], sums[1], toks) + gain * pair.astype(F32)
        )


def within_block(skip, x, step_t, cum_t, b, c):
    toks, inner = x.shape
    heads = cum_t.shape[0]
    vmem = pl.BlockSpec(memory_space=pltpu.VMEM)
    return pl.pallas_call(
        within_kernel,
        in_specs=[pl.BlockSpec(memory_space=pltpu.SMEM)] + [vmem] * 5,
        out_shape=jax.ShapeDtypeStruct((toks, inner), F32),
        compiler_params=params(24),
        cost_estimate=pl.CostEstimate(
            flops=4 * heads * toks * toks * LANES,
            bytes_accessed=6 * toks * inner,
            transcendentals=heads * toks * toks,
        ),
        name="within_block",
    )(skip, in_hbm(x), in_hbm(step_t), cum_t, in_hbm(b), in_hbm(c))


def fetch(sems, *pairs):
    copies = [pltpu.make_async_copy(src, dst, sems.at[i]) for i, (src, dst) in enumerate(pairs)]
    for copy in copies:
        copy.start()
    return copies


def cuts_of(ref, count):
    rows = ref.shape[0] // count
    return [ref.at[pl.ds(k * rows, rows)] for k in range(count)]


def quarters(place_ref, share):
    return [pl.ds(pl.multiple_of((place_ref[0] ^ k) * share, share), share) for k in range(4)]


def tail_kernel(
    place_ref, c_in, cum_in, gain_in, arriving_in, direct_in, z_in, weight_in, tokens_in,
    near, last, keep, passing,
    c, cum_t, gain, arriving, direct, z, weight, tokens, normed, sems,
):
    heads, toks = cum_t.shape
    share = near.shape[1]
    spots = quarters(place_ref, share)
    copies = fetch(
        sems,
        (cum_in, cum_t),
        (gain_in, gain),
        (c_in, c),
        (arriving_in, arriving),
        (z_in, z),
        (direct_in, direct),
        *zip(cuts_of(weight_in, 8), cuts_of(weight, 8)),
        (tokens_in.at[:, spots[0]], tokens),
    )
    for copy in copies[:6]:
        copy.wait()
    grown = jnp.exp(cum_t[...]).T
    lane = lax.broadcasted_iota(jnp.int32, (toks, LANES), 1)
    left = lane < LANES // 2
    nt = (((1,), (1,)), ((), ()))
    for p in range(heads // 2):
        spot = pl.ds(p * LANES, LANES)
        inter = lax.dot_general(c[...], arriving[spot, :], nt, preferred_element_type=F32)
        factor = by_pair(grown[:, 2 * p : 2 * p + 1], grown[:, 2 * p + 1 : 2 * p + 2], toks)
        wide = z[:, spot].astype(F32)
        gated = (direct[:, spot] + inter * factor) * (wide * (1.0 / (1.0 + jnp.exp(-wide))))
        square = gated * gated
        first = jnp.sum(jnp.where(left, square, 0.0), axis=1, keepdims=True)
        second = jnp.sum(jnp.where(left, 0.0, square), axis=1, keepdims=True)
        mean = by_pair(first, second, toks) * (2.0 / LANES)
        normed[:, spot] = (gated * lax.rsqrt(mean + 1e-05) * gain[:, spot]).astype(BF)
    for copy in copies[6:]:
        copy.wait()
    for k, out in ((3, last), (1, near), (2, passing), (0, keep)):
        part = jnp.dot(normed[...], weight[:, spots[k]], preferred_element_type=F32)
        if k == 0:
            part += tokens[...].astype(F32)
        out[...] = part.astype(out.dtype)


def mixer_tail(place, c, arriving, cum_t, direct, z, gain, weight, tokens):
    heads, toks = cum_t.shape
    inner, width = weight.shape
    share = width // 4
    operands = (c, cum_t, gain.reshape(1, inner), arriving, direct, z, weight, tokens)
    fixed = (0, 2, 5, 6, 7)
    operands = [in_hbm(a) if i in fixed else a for i, a in enumerate(operands)]
    return pl.pallas_call(
        tail_kernel,
        in_specs=[pl.BlockSpec(memory_space=pltpu.SMEM)]
        + [pl.BlockSpec(memory_space=pl.ANY)] * len(operands),
        out_shape=[jax.ShapeDtypeStruct((toks, share), kind) for kind in (BF, BF, F32, F32)],
        scratch_shapes=[pltpu.VMEM(a.shape, a.dtype) for a in operands[:-1]]
        + [
            pltpu.VMEM((toks, share), BF),
            pltpu.VMEM((toks, inner), BF),
            pltpu.SemaphoreType.DMA((15,)),
        ],
        compiler_params=params(24),
        cost_estimate=pl.CostEstimate(
            flops=2 * toks * inner * width,
            bytes_accessed=2 * inner * width + 14 * toks * inner,
            transcendentals=toks * inner,
        ),
        name="mixer_tail",
    )(place.reshape(1), *operands)


def expert_kernel(
    place_ref, gain_in, own_in, near_in, far_in, last_in, wg_in, wu_in, wd_in,
    near_out, last_out, keep_out, pass_out,
    gain, own, near, far, last, wg, wu, wd, rows, sems,
):
    count, share = own.shape
    width = 4 * share
    spots = quarters(place_ref, share)
    copies = fetch(
        sems,
        (gain_in, gain),
        (own_in, own),
        (near_in, near),
        (far_in, far),
        (last_in, last),
        *((w_in.at[s], w.at[s]) for s in spots for w_in, w in ((wg_in, wg), (wu_in, wu))),
        *zip(cuts_of(wd_in, 4), cuts_of(wd, 4)),
    )
    for copy in copies[:5]:
        copy.wait()

    @pl.loop(0, count, step=64)
    def _(start):
        spot = pl.ds(pl.multiple_of(start, 64), 64)
        wide = [p[spot, :].astype(F32) for p in (own, near, far, last)]
        square = sum(jnp.sum(w * w, axis=1, keepdims=True) for w in wide)
        scale = lax.rsqrt(square * (1.0 / width) + 1e-05)
        for k in range(4):
            rows[k, spot, :] = (wide[k] * scale * gain[:, spots[k]]).astype(BF)

    gate = up = 0.0
    for k in range(4):
        copies[5 + 2 * k].wait()
        gate += jnp.dot(rows[k], wg[spots[k], :], preferred_element_type=F32)
        copies[6 + 2 * k].wait()
        up += jnp.dot(rows[k], wu[spots[k], :], preferred_element_type=F32)
    act = (gate * (1.0 / (1.0 + jnp.exp(-gate))) * up).astype(BF)
    for copy in copies[13:]:
        copy.wait()
    for k, out in ((3, last_out), (1, near_out), (2, pass_out), (0, keep_out)):
        out[...] = jnp.dot(act, wd[:, spots[k]], preferred_element_type=F32).astype(BF)


def run_expert(place, gain, own, near, far, last, wg, wu, wd):
    rows, share = own.shape
    width, inner = wg.shape
    weights = (in_hbm(wg), in_hbm(wu), in_hbm(wd))
    operands = (in_hbm(gain.reshape(1, width)), own, near, far, last, *weights)
    return pl.pallas_call(
        expert_kernel,
        in_specs=[pl.BlockSpec(memory_space=pltpu.SMEM)]
        + [pl.BlockSpec(memory_space=pl.ANY)] * len(operands),
        out_shape=[jax.ShapeDtypeStruct((rows, share), BF)] * 4,
        scratch_shapes=[pltpu.VMEM(a.shape, a.dtype) for a in operands]
        + [
            pltpu.VMEM((4, rows, share), BF),
            pltpu.SemaphoreType.DMA((17,)),
        ],
        compiler_params=params(24),
        cost_estimate=pl.CostEstimate(
            flops=6 * rows * width * inner,
            bytes_accessed=6 * width * inner + 4 * rows * width,
            transcendentals=rows * inner,
        ),
        name="expert",
    )(place.reshape(1), *operands)


def body(
    tokens,
    input_heads,
    z_gate,
    b_proj,
    c_proj,
    step_size,
    decay_log,
    skip_gain,
    init_state,
    norm_gain,
    out_weight,
    moe_gain,
    routes,
    route_weights,
    w_gate,
    w_up,
    w_down,
):
    tok_rows, inner = input_heads.shape
    state_size = init_state.shape[2]
    seq_count = lax.axis_size("seq")
    place = lax.axis_index("tp")
    step_t = step_size.T
    outgoing, cum_t = own_state(input_heads, step_t, decay_log.T, b_proj, seq_count)
    got = exchange(outgoing)
    direct = within_block(skip_gain, input_heads, step_t, cum_t, b_proj, c_proj)
    back = entering_state(got, init_state.reshape(inner, state_size))
    arriving = exchange(back).reshape(inner, state_size)
    to_near, to_last, keep, passing = mixer_tail(
        place, c_proj, arriving, cum_t, direct, z_gate, norm_gain, out_weight, tokens
    )

    model_width = out_weight.shape[1]
    share = model_width // 4
    expert_count = w_gate.shape[0] * seq_count
    slot_count = 4 * tok_rows // seq_count
    top_count = routes.shape[1]
    items = top_count * tok_rows
    slots = expert_count * slot_count
    flat_expert = routes.T.reshape(-1)
    onehot = flat_expert[:, None] == jnp.arange(expert_count, dtype=jnp.int32)[None, :]
    before = jnp.arange(items)[:, None] > jnp.arange(items)[None, :]
    earlier = jnp.dot(before.astype(BF), onehot.astype(BF), preferred_element_type=F32)
    rank = jnp.sum(jnp.where(onehot, earlier, 0.0), axis=1).astype(jnp.int32)
    cut = slot_count // 2
    half = slots // 2
    late = (rank >= cut).astype(jnp.int32)
    placed = late * half + flat_expert * cut + rank - late * cut
    spots = placed[:, None] == jnp.arange(slots, dtype=jnp.int32)[None, :]
    spots = spots.reshape(top_count, tok_rows, slots)
    fill = jnp.any(spots, axis=0).astype(BF)
    combine = jnp.sum(jnp.where(spots, route_weights.T[:, :, None], 0.0), axis=0)

    from_last = swap(to_last, 1)
    from_near = swap(to_near, 1)
    from_far = swap((passing + from_last.astype(F32)).astype(BF), 2)
    hidden = (keep + from_near.astype(F32) + from_far.astype(F32)).astype(BF)

    def dispatch(turn):
        outgoing = lax.dot_general(
            fill[:, turn * half : (turn + 1) * half],
            hidden,
            (((0,), (0,)), ((), ())),
            preferred_element_type=F32,
        ).astype(BF)
        return outgoing.reshape(expert_count, cut, share)

    def combined(turn, results):
        returned = exchange(results.reshape(expert_count, cut, share)).reshape(half, share)
        return jnp.dot(
            combine[:, turn * half : (turn + 1) * half],
            returned.astype(F32),
            precision=lax.Precision.HIGHEST,
            preferred_element_type=F32,
        )

    weights = (w_gate[0], w_up[0], w_down[0])
    own0 = exchange(dispatch(0)).reshape(half, share)
    far0 = swap(own0, 2)
    near0 = swap(own0, 1)
    own1 = exchange(after(dispatch(1), near0)).reshape(half, share)
    last0 = swap(far0, 1)
    to_near0, to_last0, keep0, pass0 = run_expert(
        place, moe_gain, own0, near0, far0, last0, *weights
    )
    own1 = after(own1, to_last0)
    far1 = swap(own1, 2)
    near1 = swap(own1, 1)
    from_last0 = swap(to_last0, 1)
    from_near0 = swap(to_near0, 1)
    pass0 = (pass0.astype(F32) + from_last0.astype(F32)).astype(BF)
    from_far0 = swap(pass0, 2)
    last1 = swap(after(far1, pass0), 1)
    to_near1, to_last1, keep1, pass1 = run_expert(
        place, moe_gain, after(own1, pass0), near1, far1, last1, *weights
    )
    result0 = (keep0.astype(F32) + from_near0.astype(F32) + from_far0.astype(F32)).astype(BF)
    mixed = hidden.astype(F32) + combined(0, result0)
    from_last1 = swap(after(to_last1, from_far0), 1)
    from_near1 = swap(to_near1, 1)
    from_far1 = swap((pass1.astype(F32) + from_last1.astype(F32)).astype(BF), 2)
    result1 = (keep1.astype(F32) + from_near1.astype(F32) + from_far1.astype(F32)).astype(BF)
    mixed = mixed + combined(1, result1)
    return mixed.astype(BF)


def solution(mesh):
    in_specs = (
        P("seq", None),
        P("seq", "tp"),
        P("seq", "tp"),
        P("seq", None),
        P("seq", None),
        P("seq", "tp"),
        P("seq", "tp"),
        P("tp"),
        P("tp", None, None),
        P("tp"),
        P("tp", None),
        P(),
        P("seq", None),
        P("seq", None),
        P("seq", None, "tp"),
        P("seq", None, "tp"),
        P("seq", "tp", None),
    )
    out_specs = P("seq", "tp")
    return jax.shard_map(body, mesh=mesh, in_specs=in_specs, out_specs=out_specs, check_vma=False)
```

```python
import jax
import jax.numpy as jnp
from jax import lax
from jax.experimental import pallas as pl
from jax.experimental.pallas import tpu as pltpu
from jax.sharding import PartitionSpec as P

BF = jnp.bfloat16
F32 = jnp.float32
MIB = 1024 * 1024
LANES = 128


def swap(value, bit):
    count = lax.axis_size("tp")
    return lax.ppermute(value, "tp", [(i, i ^ bit) for i in range(count)])


def exchange(value):
    return lax.all_to_all(value, "seq", split_axis=0, concat_axis=0, tiled=True)


def after(value, *others):
    return lax.optimization_barrier((value, *others))[0]


def in_hbm(value):
    return pltpu.with_memory_space_constraint(value, pltpu.HBM)


def params(mib):
    return pltpu.CompilerParams(vmem_limit_bytes=mib * MIB)


def whole(*shape):
    return pl.BlockSpec(shape, lambda *_: (0,) * len(shape))


def by_pair(left, right, size):
    lane = lax.broadcasted_iota(jnp.int32, (size, LANES), 1)
    return jnp.where(lane < LANES // 2, left, right)


def state_kernel(x, step_t, decay_t, b, out, cum_out):
    count, rows, _ = out.shape
    part = rows - 16
    heads, toks = decay_t.shape
    row = lax.broadcasted_iota(jnp.int32, (toks, toks), 0)
    col = lax.broadcasted_iota(jnp.int32, (toks, toks), 1)
    upper = (row <= col).astype(F32)
    cum_t = jnp.dot(
        decay_t[...], upper, precision=lax.Precision.HIGHEST, preferred_element_type=F32
    )
    cum_out[...] = cum_t
    end = cum_t[:, toks - 1 : toks]
    scale = (jnp.exp(end - cum_t) * step_t[...]).T
    decay = jnp.broadcast_to(jnp.exp(end), (heads, LANES))
    high = decay.astype(BF).astype(F32)
    extra = by_pair(high, decay - high, heads).astype(BF)
    for k in range(count):
        out[k, pl.ds(part, 16), :] = extra
    for p in range(heads // 2):
        pair = x[:, p * LANES : (p + 1) * LANES].astype(F32)
        factor = by_pair(scale[:, 2 * p : 2 * p + 1], scale[:, 2 * p + 1 : 2 * p + 2], toks)
        state = lax.dot_general(
            (pair * factor).astype(BF),
            b[...],
            (((0,), (0,)), ((), ())),
            preferred_element_type=F32,
        ).astype(BF)
        for k in range(LANES // part):
            out[p * (LANES // part) + k, pl.ds(0, part), :] = state[k * part : (k + 1) * part]


def own_state(x, step_t, decay_t, b, count):
    heads, toks = decay_t.shape
    part = x.shape[1] // count
    return pl.pallas_call(
        state_kernel,
        out_shape=[
            jax.ShapeDtypeStruct((count, part + 16, b.shape[1]), BF),
            jax.ShapeDtypeStruct((heads, toks), F32),
        ],
        compiler_params=params(8),
        name="own_state",
    )(in_hbm(x), in_hbm(step_t), in_hbm(decay_t), in_hbm(b))


def prefix_kernel(place_ref, got, start, back):
    count, part, _ = back.shape
    heads = 16
    held = max(1, heads // count)
    group = part // held
    first = place_ref[0] * heads // count
    row = lax.broadcasted_iota(jnp.int32, (heads, LANES), 0)
    carries = [start[pl.ds(h * group, group), :] for h in range(held)]
    for turn in range(count):
        extra = got[turn, pl.ds(part, 16), :].astype(F32)
        scale = extra[:, :1] + extra[:, LANES // 2 : LANES // 2 + 1]
        for h in range(held):
            spot = pl.ds(h * group, group)
            back[turn, spot, :] = carries[h].astype(BF)
            factor = jnp.sum(jnp.where(row == first + h, scale, 0.0), axis=0, keepdims=True)
            carries[h] = factor * carries[h] + got[turn, spot, :].astype(F32)


def entering_state(got, init_rows):
    count, rows, width = got.shape
    part = rows - 16
    place = lax.axis_index("seq")
    start = lax.dynamic_slice_in_dim(init_rows, place * part, part, 0)
    vmem = pl.BlockSpec(memory_space=pltpu.VMEM)
    return pl.pallas_call(
        prefix_kernel,
        in_specs=[pl.BlockSpec(memory_space=pltpu.SMEM), vmem, vmem],
        out_shape=jax.ShapeDtypeStruct((count, part, width), BF),
        compiler_params=params(8),
        name="prefix",
    )(place.reshape(1), got, start)


def within_kernel(skip, x, step_t, cum_t, b, c, out):
    heads, toks = cum_t.shape
    row = lax.broadcasted_iota(jnp.int32, (toks, toks), 0)
    col = lax.broadcasted_iota(jnp.int32, (toks, toks), 1)
    causal = row >= col
    nt = (((1,), (1,)), ((), ()))
    scores = lax.dot_general(c[...], b[...], nt, preferred_element_type=F32)
    cum = cum_t[...].T
    for p in range(heads // 2):
        pair = x[:, p * LANES : (p + 1) * LANES]
        sums = []
        for h in (2 * p, 2 * p + 1):
            gap = cum[:, h : h + 1] - cum_t[h : h + 1, :]
            decay = jnp.where(causal, jnp.exp(jnp.where(causal, gap, 0.0)), 0.0)
            weights = (decay * scores * step_t[h : h + 1, :]).astype(BF)
            sums.append(jnp.dot(weights, pair, preferred_element_type=F32))
        gain = by_pair(skip[2 * p], skip[2 * p + 1], toks)
        out[:, p * LANES : (p + 1) * LANES] = (
            by_pair(sums[0], sums[1], toks) + gain * pair.astype(F32)
        )


def within_block(skip, x, step_t, cum_t, b, c):
    toks, inner = x.shape
    heads = cum_t.shape[0]
    vmem = pl.BlockSpec(memory_space=pltpu.VMEM)
    return pl.pallas_call(
        within_kernel,
        in_specs=[pl.BlockSpec(memory_space=pltpu.SMEM)] + [vmem] * 5,
        out_shape=jax.ShapeDtypeStruct((toks, inner), F32),
        compiler_params=params(24),
        cost_estimate=pl.CostEstimate(
            flops=4 * heads * toks * toks * LANES,
            bytes_accessed=6 * toks * inner,
            transcendentals=heads * toks * toks,
        ),
        name="within_block",
    )(skip, in_hbm(x), in_hbm(step_t), cum_t, in_hbm(b), in_hbm(c))


def fetch(sems, *pairs):
    copies = [pltpu.make_async_copy(src, dst, sems.at[i]) for i, (src, dst) in enumerate(pairs)]
    for copy in copies:
        copy.start()
    return copies


def cuts_of(ref, count):
    rows = ref.shape[0] // count
    return [ref.at[pl.ds(k * rows, rows)] for k in range(count)]


def quarters(place_ref, share):
    return [pl.ds(pl.multiple_of((place_ref[0] ^ k) * share, share), share) for k in range(4)]


def tail_kernel(
    place_ref, c_in, cum_in, gain_in, arriving_in, direct_in, z_in, weight_in, tokens_in,
    near, last, keep, passing,
    c, cum_t, gain, arriving, direct, z, weight, tokens, normed, sems,
):
    heads, toks = cum_t.shape
    share = near.shape[1]
    spots = quarters(place_ref, share)
    copies = fetch(
        sems,
        (cum_in, cum_t),
        (gain_in, gain),
        (c_in, c),
        (arriving_in, arriving),
        (z_in, z),
        (direct_in, direct),
        *zip(cuts_of(weight_in, 8), cuts_of(weight, 8)),
        (tokens_in.at[:, spots[0]], tokens),
    )
    for copy in copies[:6]:
        copy.wait()
    grown = jnp.exp(cum_t[...]).T
    lane = lax.broadcasted_iota(jnp.int32, (toks, LANES), 1)
    left = lane < LANES // 2
    nt = (((1,), (1,)), ((), ()))
    for p in range(heads // 2):
        spot = pl.ds(p * LANES, LANES)
        inter = lax.dot_general(c[...], arriving[spot, :], nt, preferred_element_type=F32)
        factor = by_pair(grown[:, 2 * p : 2 * p + 1], grown[:, 2 * p + 1 : 2 * p + 2], toks)
        wide = z[:, spot].astype(F32)
        gated = (direct[:, spot] + inter * factor) * (wide * (1.0 / (1.0 + jnp.exp(-wide))))
        square = gated * gated
        first = jnp.sum(jnp.where(left, square, 0.0), axis=1, keepdims=True)
        second = jnp.sum(jnp.where(left, 0.0, square), axis=1, keepdims=True)
        mean = by_pair(first, second, toks) * (2.0 / LANES)
        normed[:, spot] = (gated * lax.rsqrt(mean + 1e-05) * gain[:, spot]).astype(BF)
    for copy in copies[6:]:
        copy.wait()
    for k, out in ((3, last), (1, near), (2, passing), (0, keep)):
        part = jnp.dot(normed[...], weight[:, spots[k]], preferred_element_type=F32)
        if k == 0:
            part += tokens[...].astype(F32)
        out[...] = part.astype(out.dtype)


def mixer_tail(place, c, arriving, cum_t, direct, z, gain, weight, tokens):
    heads, toks = cum_t.shape
    inner, width = weight.shape
    share = width // 4
    operands = (c, cum_t, gain.reshape(1, inner), arriving, direct, z, weight, tokens)
    fixed = (0, 2, 5, 6, 7)
    operands = [in_hbm(a) if i in fixed else a for i, a in enumerate(operands)]
    return pl.pallas_call(
        tail_kernel,
        in_specs=[pl.BlockSpec(memory_space=pltpu.SMEM)]
        + [pl.BlockSpec(memory_space=pl.ANY)] * len(operands),
        out_shape=[jax.ShapeDtypeStruct((toks, share), kind) for kind in (BF, BF, F32, F32)],
        scratch_shapes=[pltpu.VMEM(a.shape, a.dtype) for a in operands[:-1]]
        + [
            pltpu.VMEM((toks, share), BF),
            pltpu.VMEM((toks, inner), BF),
            pltpu.SemaphoreType.DMA((15,)),
        ],
        compiler_params=params(24),
        cost_estimate=pl.CostEstimate(
            flops=2 * toks * inner * width,
            bytes_accessed=2 * inner * width + 14 * toks * inner,
            transcendentals=toks * inner,
        ),
        name="mixer_tail",
    )(place.reshape(1), *operands)


def expert_kernel(
    place_ref, gain_in, own_in, near_in, far_in, last_in, wg_in, wu_in, wd_in,
    near_out, last_out, keep_out, pass_out,
    gain, own, near, far, last, wg, wu, wd, rows, sems,
):
    count, share = own.shape
    width = 4 * share
    spots = quarters(place_ref, share)
    copies = fetch(
        sems,
        (gain_in, gain),
        (own_in, own),
        (near_in, near),
        (far_in, far),
        (last_in, last),
        *((w_in.at[s], w.at[s]) for s in spots for w_in, w in ((wg_in, wg), (wu_in, wu))),
        *zip(cuts_of(wd_in, 4), cuts_of(wd, 4)),
    )
    for copy in copies[:5]:
        copy.wait()

    @pl.loop(0, count, step=64)
    def _(start):
        spot = pl.ds(pl.multiple_of(start, 64), 64)
        wide = [p[spot, :].astype(F32) for p in (own, near, far, last)]
        square = sum(jnp.sum(w * w, axis=1, keepdims=True) for w in wide)
        scale = lax.rsqrt(square * (1.0 / width) + 1e-05)
        for k in range(4):
            rows[k, spot, :] = (wide[k] * scale * gain[:, spots[k]]).astype(BF)

    gate = up = 0.0
    for k in range(4):
        copies[5 + 2 * k].wait()
        gate += jnp.dot(rows[k], wg[spots[k], :], preferred_element_type=F32)
        copies[6 + 2 * k].wait()
        up += jnp.dot(rows[k], wu[spots[k], :], preferred_element_type=F32)
    act = (gate * (1.0 / (1.0 + jnp.exp(-gate))) * up).astype(BF)
    for copy in copies[13:]:
        copy.wait()
    for k, out in ((3, last_out), (1, near_out), (2, pass_out), (0, keep_out)):
        out[...] = jnp.dot(act, wd[:, spots[k]], preferred_element_type=F32).astype(BF)


def run_expert(place, gain, own, near, far, last, wg, wu, wd):
    rows, share = own.shape
    width, inner = wg.shape
    weights = (in_hbm(wg), in_hbm(wu), in_hbm(wd))
    operands = (in_hbm(gain.reshape(1, width)), own, near, far, last, *weights)
    return pl.pallas_call(
        expert_kernel,
        in_specs=[pl.BlockSpec(memory_space=pltpu.SMEM)]
        + [pl.BlockSpec(memory_space=pl.ANY)] * len(operands),
        out_shape=[jax.ShapeDtypeStruct((rows, share), BF)] * 4,
        scratch_shapes=[pltpu.VMEM(a.shape, a.dtype) for a in operands]
        + [
            pltpu.VMEM((4, rows, share), BF),
            pltpu.SemaphoreType.DMA((17,)),
        ],
        compiler_params=params(24),
        cost_estimate=pl.CostEstimate(flops=1, bytes_accessed=1, transcendentals=0),
        name="expert",
    )(place.reshape(1), *operands)


def body(
    tokens,
    input_heads,
    z_gate,
    b_proj,
    c_proj,
    step_size,
    decay_log,
    skip_gain,
    init_state,
    norm_gain,
    out_weight,
    moe_gain,
    routes,
    route_weights,
    w_gate,
    w_up,
    w_down,
):
    tok_rows, inner = input_heads.shape
    state_size = init_state.shape[2]
    seq_count = lax.axis_size("seq")
    place = lax.axis_index("tp")
    step_t = step_size.T
    outgoing, cum_t = own_state(input_heads, step_t, decay_log.T, b_proj, seq_count)
    got = exchange(outgoing)
    direct = within_block(skip_gain, input_heads, step_t, cum_t, b_proj, c_proj)
    back = entering_state(got, init_state.reshape(inner, state_size))
    arriving = exchange(back).reshape(inner, state_size)
    to_near, to_last, keep, passing = mixer_tail(
        place, c_proj, arriving, cum_t, direct, z_gate, norm_gain, out_weight, tokens
    )

    model_width = out_weight.shape[1]
    share = model_width // 4
    expert_count = w_gate.shape[0] * seq_count
    slot_count = 4 * tok_rows // seq_count
    top_count = routes.shape[1]
    items = top_count * tok_rows
    slots = expert_count * slot_count
    flat_expert = routes.T.reshape(-1)
    onehot = flat_expert[:, None] == jnp.arange(expert_count, dtype=jnp.int32)[None, :]
    before = jnp.arange(items)[:, None] > jnp.arange(items)[None, :]
    earlier = jnp.dot(before.astype(BF), onehot.astype(BF), preferred_element_type=F32)
    rank = jnp.sum(jnp.where(onehot, earlier, 0.0), axis=1).astype(jnp.int32)
    placed = flat_expert * slot_count + rank
    spots = placed[:, None] == jnp.arange(slots, dtype=jnp.int32)[None, :]
    spots = spots.reshape(top_count, tok_rows, slots)
    fill = jnp.any(spots, axis=0).astype(BF)
    combine = jnp.sum(jnp.where(spots, route_weights.T[:, :, None], 0.0), axis=0)

    from_last = swap(to_last, 1)
    from_near = swap(to_near, 1)
    from_far = swap((passing + from_last.astype(F32)).astype(BF), 2)
    hidden = (keep + from_near.astype(F32) + from_far.astype(F32)).astype(BF)

    outgoing = lax.dot_general(
        fill, hidden, (((0,), (0,)), ((), ())), preferred_element_type=F32
    ).astype(BF)
    arrived = exchange(outgoing.reshape(expert_count, slot_count, share)).reshape(slots, share)

    cut = slots // 2
    own = [arrived[:cut], arrived[cut:]]
    far = [swap(part, 2) for part in own]
    near = [swap(part, 1) for part in own]
    weights = (w_gate[0], w_up[0], w_down[0])
    last = swap(far[0], 1)
    to_near0, to_last0, keep0, pass0 = run_expert(
        place, moe_gain, own[0], near[0], far[0], last, *weights
    )
    from_last0 = swap(to_last0, 1)
    last = swap(after(far[1], to_last0), 1)
    pass0 = (pass0.astype(F32) + from_last0.astype(F32)).astype(BF)
    from_far0 = swap(pass0, 2)
    to_near1, to_last1, keep1, pass1 = run_expert(
        place, moe_gain, after(own[1], pass0), near[1], far[1], last, *weights
    )
    from_near0 = swap(to_near0, 1)
    from_last1 = swap(to_last1, 1)
    from_near1 = swap(after(to_near1, from_far0), 1)
    pass1 = (pass1.astype(F32) + from_last1.astype(F32)).astype(BF)
    from_far1 = swap(pass1, 2)
    results = [
        (keep.astype(F32) + from_near.astype(F32) + from_far.astype(F32)).astype(BF)
        for keep, from_near, from_far in (
            (keep0, from_near0, from_far0),
            (keep1, from_near1, from_far1),
        )
    ]
    results = jnp.concatenate(results).reshape(expert_count, slot_count, share)
    returned = exchange(results).reshape(slots, share)
    mixed = hidden.astype(F32) + jnp.dot(
        combine,
        returned.astype(F32),
        precision=lax.Precision.HIGHEST,
        preferred_element_type=F32,
    )
    return mixed.astype(BF)


def solution(mesh):
    in_specs = (
        P("seq", None),
        P("seq", "tp"),
        P("seq", "tp"),
        P("seq", None),
        P("seq", None),
        P("seq", "tp"),
        P("seq", "tp"),
        P("tp"),
        P("tp", None, None),
        P("tp"),
        P("tp", None),
        P(),
        P("seq", None),
        P("seq", None),
        P("seq", None, "tp"),
        P("seq", None, "tp"),
        P("seq", "tp", None),
    )
    out_specs = P("seq", "tp")
    return jax.shard_map(body, mesh=mesh, in_specs=in_specs, out_specs=out_specs, check_vma=False)
```

```python
import jax
import jax.numpy as jnp
from jax import lax
from jax.experimental import pallas as pl
from jax.experimental.pallas import tpu as pltpu
from jax.sharding import PartitionSpec as P

BF = jnp.bfloat16
F32 = jnp.float32
MIB = 1024 * 1024
LANES = 128


def swap(value, bit):
    count = lax.axis_size("tp")
    return lax.ppermute(value, "tp", [(i, i ^ bit) for i in range(count)])


def exchange(value):
    return lax.all_to_all(value, "seq", split_axis=0, concat_axis=0, tiled=True)


def after(value, *others):
    return lax.optimization_barrier((value, *others))[0]


def in_hbm(value):
    return pltpu.with_memory_space_constraint(value, pltpu.HBM)


def params(mib):
    return pltpu.CompilerParams(vmem_limit_bytes=mib * MIB)


def whole(*shape):
    return pl.BlockSpec(shape, lambda *_: (0,) * len(shape))


def by_pair(left, right, size):
    lane = lax.broadcasted_iota(jnp.int32, (size, LANES), 1)
    return jnp.where(lane < LANES // 2, left, right)


def state_kernel(x, step_t, decay_t, b, out, cum_out):
    count, rows, _ = out.shape
    part = rows - 16
    heads, toks = decay_t.shape
    row = lax.broadcasted_iota(jnp.int32, (toks, toks), 0)
    col = lax.broadcasted_iota(jnp.int32, (toks, toks), 1)
    upper = (row <= col).astype(F32)
    cum_t = jnp.dot(
        decay_t[...], upper, precision=lax.Precision.HIGHEST, preferred_element_type=F32
    )
    cum_out[...] = cum_t
    end = cum_t[:, toks - 1 : toks]
    scale = (jnp.exp(end - cum_t) * step_t[...]).T
    decay = jnp.broadcast_to(jnp.exp(end), (heads, LANES))
    high = decay.astype(BF).astype(F32)
    extra = by_pair(high, decay - high, heads).astype(BF)
    for k in range(count):
        out[k, pl.ds(part, 16), :] = extra
    for p in range(heads // 2):
        pair = x[:, p * LANES : (p + 1) * LANES].astype(F32)
        factor = by_pair(scale[:, 2 * p : 2 * p + 1], scale[:, 2 * p + 1 : 2 * p + 2], toks)
        state = lax.dot_general(
            (pair * factor).astype(BF),
            b[...],
            (((0,), (0,)), ((), ())),
            preferred_element_type=F32,
        ).astype(BF)
        for k in range(LANES // part):
            out[p * (LANES // part) + k, pl.ds(0, part), :] = state[k * part : (k + 1) * part]


def own_state(x, step_t, decay_t, b, count):
    heads, toks = decay_t.shape
    part = x.shape[1] // count
    return pl.pallas_call(
        state_kernel,
        out_shape=[
            jax.ShapeDtypeStruct((count, part + 16, b.shape[1]), BF),
            jax.ShapeDtypeStruct((heads, toks), F32),
        ],
        compiler_params=params(8),
        name="own_state",
    )(in_hbm(x), in_hbm(step_t), in_hbm(decay_t), in_hbm(b))


def prefix_kernel(place_ref, got, start, back):
    count, part, _ = back.shape
    heads = 16
    held = max(1, heads // count)
    group = part // held
    first = place_ref[0] * heads // count
    row = lax.broadcasted_iota(jnp.int32, (heads, LANES), 0)
    carries = [start[pl.ds(h * group, group), :] for h in range(held)]
    for turn in range(count):
        extra = got[turn, pl.ds(part, 16), :].astype(F32)
        scale = extra[:, :1] + extra[:, LANES // 2 : LANES // 2 + 1]
        for h in range(held):
            spot = pl.ds(h * group, group)
            back[turn, spot, :] = carries[h].astype(BF)
            factor = jnp.sum(jnp.where(row == first + h, scale, 0.0), axis=0, keepdims=True)
            carries[h] = factor * carries[h] + got[turn, spot, :].astype(F32)


def entering_state(got, init_rows):
    count, rows, width = got.shape
    part = rows - 16
    place = lax.axis_index("seq")
    start = lax.dynamic_slice_in_dim(init_rows, place * part, part, 0)
    vmem = pl.BlockSpec(memory_space=pltpu.VMEM)
    return pl.pallas_call(
        prefix_kernel,
        in_specs=[pl.BlockSpec(memory_space=pltpu.SMEM), vmem, vmem],
        out_shape=jax.ShapeDtypeStruct((count, part, width), BF),
        compiler_params=params(8),
        name="prefix",
    )(place.reshape(1), got, start)


def within_kernel(skip, x, step_t, cum_t, b, c, out):
    heads, toks = cum_t.shape
    row = lax.broadcasted_iota(jnp.int32, (toks, toks), 0)
    col = lax.broadcasted_iota(jnp.int32, (toks, toks), 1)
    causal = row >= col
    nt = (((1,), (1,)), ((), ()))
    scores = lax.dot_general(c[...], b[...], nt, preferred_element_type=F32)
    cum = cum_t[...].T
    for p in range(heads // 2):
        pair = x[:, p * LANES : (p + 1) * LANES]
        sums = []
        for h in (2 * p, 2 * p + 1):
            gap = cum[:, h : h + 1] - cum_t[h : h + 1, :]
            decay = jnp.where(causal, jnp.exp(jnp.where(causal, gap, 0.0)), 0.0)
            weights = (decay * scores * step_t[h : h + 1, :]).astype(BF)
            sums.append(jnp.dot(weights, pair, preferred_element_type=F32))
        gain = by_pair(skip[2 * p], skip[2 * p + 1], toks)
        out[:, p * LANES : (p + 1) * LANES] = (
            by_pair(sums[0], sums[1], toks) + gain * pair.astype(F32)
        )


def within_block(skip, x, step_t, cum_t, b, c):
    toks, inner = x.shape
    heads = cum_t.shape[0]
    vmem = pl.BlockSpec(memory_space=pltpu.VMEM)
    return pl.pallas_call(
        within_kernel,
        in_specs=[pl.BlockSpec(memory_space=pltpu.SMEM)] + [vmem] * 5,
        out_shape=jax.ShapeDtypeStruct((toks, inner), F32),
        compiler_params=params(8),
        cost_estimate=pl.CostEstimate(
            flops=4 * heads * toks * toks * LANES,
            bytes_accessed=6 * toks * inner,
            transcendentals=heads * toks * toks,
        ),
        name="within_block",
    )(skip, in_hbm(x), in_hbm(step_t), cum_t, in_hbm(b), in_hbm(c))


def fetch(sems, *pairs):
    copies = [pltpu.make_async_copy(src, dst, sems.at[i]) for i, (src, dst) in enumerate(pairs)]
    for copy in copies:
        copy.start()
    return copies


def cuts_of(ref, count):
    rows = ref.shape[0] // count
    return [ref.at[pl.ds(k * rows, rows)] for k in range(count)]


def quarters(place_ref, share):
    return [pl.ds(pl.multiple_of((place_ref[0] ^ k) * share, share), share) for k in range(4)]


def tail_kernel(
    place_ref, c_in, cum_in, gain_in, arriving_in, direct_in, z_in, weight_in, tokens_in,
    near, last, keep, passing,
    c, cum_t, gain, arriving, direct, z, weight, tokens, normed, sems,
):
    heads, toks = cum_t.shape
    share = near.shape[1]
    spots = quarters(place_ref, share)
    copies = fetch(
        sems,
        (cum_in, cum_t),
        (gain_in, gain),
        (c_in, c),
        (arriving_in, arriving),
        (z_in, z),
        (direct_in, direct),
        *zip(cuts_of(weight_in, 8), cuts_of(weight, 8)),
        (tokens_in.at[:, spots[0]], tokens),
    )
    for copy in copies[:6]:
        copy.wait()
    grown = jnp.exp(cum_t[...]).T
    lane = lax.broadcasted_iota(jnp.int32, (toks, LANES), 1)
    left = lane < LANES // 2
    nt = (((1,), (1,)), ((), ()))
    for p in range(heads // 2):
        spot = pl.ds(p * LANES, LANES)
        inter = lax.dot_general(c[...], arriving[spot, :], nt, preferred_element_type=F32)
        factor = by_pair(grown[:, 2 * p : 2 * p + 1], grown[:, 2 * p + 1 : 2 * p + 2], toks)
        wide = z[:, spot].astype(F32)
        gated = (direct[:, spot] + inter * factor) * (wide * (1.0 / (1.0 + jnp.exp(-wide))))
        square = gated * gated
        first = jnp.sum(jnp.where(left, square, 0.0), axis=1, keepdims=True)
        second = jnp.sum(jnp.where(left, 0.0, square), axis=1, keepdims=True)
        mean = by_pair(first, second, toks) * (2.0 / LANES)
        normed[:, spot] = (gated * lax.rsqrt(mean + 1e-05) * gain[:, spot]).astype(BF)
    for copy in copies[6:]:
        copy.wait()
    for k, out in ((3, last), (1, near), (2, passing), (0, keep)):
        part = jnp.dot(normed[...], weight[:, spots[k]], preferred_element_type=F32)
        if k == 0:
            part += tokens[...].astype(F32)
        out[...] = part.astype(out.dtype)


def mixer_tail(place, c, arriving, cum_t, direct, z, gain, weight, tokens):
    heads, toks = cum_t.shape
    inner, width = weight.shape
    share = width // 4
    operands = (c, cum_t, gain.reshape(1, inner), arriving, direct, z, weight, tokens)
    fixed = (0, 2, 5, 6, 7)
    operands = [in_hbm(a) if i in fixed else a for i, a in enumerate(operands)]
    return pl.pallas_call(
        tail_kernel,
        in_specs=[pl.BlockSpec(memory_space=pltpu.SMEM)]
        + [pl.BlockSpec(memory_space=pl.ANY)] * len(operands),
        out_shape=[jax.ShapeDtypeStruct((toks, share), kind) for kind in (BF, BF, F32, F32)],
        scratch_shapes=[pltpu.VMEM(a.shape, a.dtype) for a in operands[:-1]]
        + [
            pltpu.VMEM((toks, share), BF),
            pltpu.VMEM((toks, inner), BF),
            pltpu.SemaphoreType.DMA((15,)),
        ],
        compiler_params=params(12),
        cost_estimate=pl.CostEstimate(
            flops=2 * toks * inner * width,
            bytes_accessed=2 * inner * width + 14 * toks * inner,
            transcendentals=toks * inner,
        ),
        name="mixer_tail",
    )(place.reshape(1), *operands)


def expert_kernel(
    place_ref, gain_in, own_in, near_in, far_in, last_in, wg_in, wu_in, wd_in,
    near_out, last_out, keep_out, pass_out,
    gain, own, near, far, last, wg, wu, wd, rows, sems,
):
    count, share = own.shape
    width = 4 * share
    spots = quarters(place_ref, share)
    copies = fetch(
        sems,
        (gain_in, gain),
        (own_in, own),
        (near_in, near),
        (far_in, far),
        (last_in, last),
        *((w_in.at[s], w.at[s]) for s in spots for w_in, w in ((wg_in, wg), (wu_in, wu))),
        *zip(cuts_of(wd_in, 4), cuts_of(wd, 4)),
    )
    for copy in copies[:5]:
        copy.wait()

    @pl.loop(0, count, step=64)
    def _(start):
        spot = pl.ds(pl.multiple_of(start, 64), 64)
        wide = [p[spot, :].astype(F32) for p in (own, near, far, last)]
        square = sum(jnp.sum(w * w, axis=1, keepdims=True) for w in wide)
        scale = lax.rsqrt(square * (1.0 / width) + 1e-05)
        for k in range(4):
            rows[k, spot, :] = (wide[k] * scale * gain[:, spots[k]]).astype(BF)

    gate = up = 0.0
    for k in range(4):
        copies[5 + 2 * k].wait()
        gate += jnp.dot(rows[k], wg[spots[k], :], preferred_element_type=F32)
        copies[6 + 2 * k].wait()
        up += jnp.dot(rows[k], wu[spots[k], :], preferred_element_type=F32)
    act = (gate * (1.0 / (1.0 + jnp.exp(-gate))) * up).astype(BF)
    for copy in copies[13:]:
        copy.wait()
    for k, out in ((3, last_out), (1, near_out), (2, pass_out), (0, keep_out)):
        out[...] = jnp.dot(act, wd[:, spots[k]], preferred_element_type=F32).astype(BF)


def run_expert(place, gain, own, near, far, last, wg, wu, wd):
    rows, share = own.shape
    width, inner = wg.shape
    weights = (in_hbm(wg), in_hbm(wu), in_hbm(wd))
    operands = (in_hbm(gain.reshape(1, width)), own, near, far, last, *weights)
    return pl.pallas_call(
        expert_kernel,
        in_specs=[pl.BlockSpec(memory_space=pltpu.SMEM)]
        + [pl.BlockSpec(memory_space=pl.ANY)] * len(operands),
        out_shape=[jax.ShapeDtypeStruct((rows, share), BF)] * 4,
        scratch_shapes=[pltpu.VMEM(a.shape, a.dtype) for a in operands]
        + [
            pltpu.VMEM((4, rows, share), BF),
            pltpu.SemaphoreType.DMA((17,)),
        ],
        compiler_params=params(16),
        cost_estimate=pl.CostEstimate(flops=1, bytes_accessed=1, transcendentals=0),
        name="expert",
    )(place.reshape(1), *operands)


def body(
    tokens,
    input_heads,
    z_gate,
    b_proj,
    c_proj,
    step_size,
    decay_log,
    skip_gain,
    init_state,
    norm_gain,
    out_weight,
    moe_gain,
    routes,
    route_weights,
    w_gate,
    w_up,
    w_down,
):
    tok_rows, inner = input_heads.shape
    state_size = init_state.shape[2]
    seq_count = lax.axis_size("seq")
    place = lax.axis_index("tp")
    step_t = step_size.T
    outgoing, cum_t = own_state(input_heads, step_t, decay_log.T, b_proj, seq_count)
    got = exchange(outgoing)
    direct = within_block(skip_gain, input_heads, step_t, cum_t, b_proj, c_proj)
    back = entering_state(got, init_state.reshape(inner, state_size))
    arriving = exchange(back).reshape(inner, state_size)
    to_near, to_last, keep, passing = mixer_tail(
        place, c_proj, arriving, cum_t, direct, z_gate, norm_gain, out_weight, tokens
    )

    model_width = out_weight.shape[1]
    share = model_width // 4
    expert_count = w_gate.shape[0] * seq_count
    slot_count = 4 * tok_rows // seq_count
    top_count = routes.shape[1]
    items = top_count * tok_rows
    slots = expert_count * slot_count
    flat_expert = routes.T.reshape(-1)
    onehot = flat_expert[:, None] == jnp.arange(expert_count, dtype=jnp.int32)[None, :]
    before = jnp.arange(items)[:, None] > jnp.arange(items)[None, :]
    earlier = jnp.dot(before.astype(BF), onehot.astype(BF), preferred_element_type=F32)
    rank = jnp.sum(jnp.where(onehot, earlier, 0.0), axis=1).astype(jnp.int32)
    placed = flat_expert * slot_count + rank
    spots = placed[:, None] == jnp.arange(slots, dtype=jnp.int32)[None, :]
    spots = spots.reshape(top_count, tok_rows, slots)
    fill = jnp.any(spots, axis=0).astype(BF)
    combine = jnp.sum(jnp.where(spots, route_weights.T[:, :, None], 0.0), axis=0)

    from_last = swap(to_last, 1)
    from_near = swap(to_near, 1)
    from_far = swap((passing + from_last.astype(F32)).astype(BF), 2)
    hidden = (keep + from_near.astype(F32) + from_far.astype(F32)).astype(BF)

    outgoing = lax.dot_general(
        fill, hidden, (((0,), (0,)), ((), ())), preferred_element_type=F32
    ).astype(BF)
    arrived = exchange(outgoing.reshape(expert_count, slot_count, share)).reshape(slots, share)

    cut = slots // 2
    own = [arrived[:cut], arrived[cut:]]
    far = [swap(part, 2) for part in own]
    near = [swap(part, 1) for part in own]
    weights = (w_gate[0], w_up[0], w_down[0])
    last = swap(far[0], 1)
    to_near0, to_last0, keep0, pass0 = run_expert(
        place, moe_gain, own[0], near[0], far[0], last, *weights
    )
    from_last0 = swap(to_last0, 1)
    last = swap(after(far[1], to_last0), 1)
    pass0 = (pass0.astype(F32) + from_last0.astype(F32)).astype(BF)
    from_far0 = swap(pass0, 2)
    to_near1, to_last1, keep1, pass1 = run_expert(
        place, moe_gain, after(own[1], pass0), near[1], far[1], last, *weights
    )
    from_last1 = swap(to_last1, 1)
    from_near0 = swap(after(to_near0, from_far0), 1)
    pass1 = (pass1.astype(F32) + from_last1.astype(F32)).astype(BF)
    from_far1 = swap(pass1, 2)
    from_near1 = swap(after(to_near1, pass1), 1)
    results = [
        (keep.astype(F32) + from_near.astype(F32) + from_far.astype(F32)).astype(BF)
        for keep, from_near, from_far in (
            (keep0, from_near0, from_far0),
            (keep1, from_near1, from_far1),
        )
    ]
    results = jnp.concatenate(results).reshape(expert_count, slot_count, share)
    returned = exchange(results).reshape(slots, share)
    mixed = hidden.astype(F32) + jnp.dot(
        combine,
        returned.astype(F32),
        precision=lax.Precision.HIGHEST,
        preferred_element_type=F32,
    )
    return mixed.astype(BF)


def solution(mesh):
    in_specs = (
        P("seq", None),
        P("seq", "tp"),
        P("seq", "tp"),
        P("seq", None),
        P("seq", None),
        P("seq", "tp"),
        P("seq", "tp"),
        P("tp"),
        P("tp", None, None),
        P("tp"),
        P("tp", None),
        P(),
        P("seq", None),
        P("seq", None),
        P("seq", None, "tp"),
        P("seq", None, "tp"),
        P("seq", "tp", None),
    )
    out_specs = P("seq", "tp")
    return jax.shard_map(body, mesh=mesh, in_specs=in_specs, out_specs=out_specs, check_vma=False)
```

```python
import jax
import jax.numpy as jnp
from jax import lax
from jax.experimental import pallas as pl
from jax.experimental.pallas import tpu as pltpu
from jax.sharding import PartitionSpec as P

BF = jnp.bfloat16
F32 = jnp.float32
MIB = 1024 * 1024
LANES = 128


def swap(value, bit):
    count = lax.axis_size("tp")
    return lax.ppermute(value, "tp", [(i, i ^ bit) for i in range(count)])


def exchange(value):
    return lax.all_to_all(value, "seq", split_axis=0, concat_axis=0, tiled=True)


def after(value, *others):
    return lax.optimization_barrier((value, *others))[0]


def in_hbm(value):
    return pltpu.with_memory_space_constraint(value, pltpu.HBM)


def params(mib):
    return pltpu.CompilerParams(vmem_limit_bytes=mib * MIB)


def whole(*shape):
    return pl.BlockSpec(shape, lambda *_: (0,) * len(shape))


def by_pair(left, right, size):
    lane = lax.broadcasted_iota(jnp.int32, (size, LANES), 1)
    return jnp.where(lane < LANES // 2, left, right)


def state_kernel(x, step_t, decay_t, b, out, cum_out):
    count, rows, _ = out.shape
    part = rows - 16
    heads, toks = decay_t.shape
    row = lax.broadcasted_iota(jnp.int32, (toks, toks), 0)
    col = lax.broadcasted_iota(jnp.int32, (toks, toks), 1)
    upper = (row <= col).astype(F32)
    cum_t = jnp.dot(
        decay_t[...], upper, precision=lax.Precision.HIGHEST, preferred_element_type=F32
    )
    cum_out[...] = cum_t
    end = cum_t[:, toks - 1 : toks]
    scale = (jnp.exp(end - cum_t) * step_t[...]).T
    decay = jnp.broadcast_to(jnp.exp(end), (heads, LANES))
    high = decay.astype(BF).astype(F32)
    extra = by_pair(high, decay - high, heads).astype(BF)
    for k in range(count):
        out[k, pl.ds(part, 16), :] = extra
    for p in range(heads // 2):
        pair = x[:, p * LANES : (p + 1) * LANES].astype(F32)
        factor = by_pair(scale[:, 2 * p : 2 * p + 1], scale[:, 2 * p + 1 : 2 * p + 2], toks)
        state = lax.dot_general(
            (pair * factor).astype(BF),
            b[...],
            (((0,), (0,)), ((), ())),
            preferred_element_type=F32,
        ).astype(BF)
        for k in range(LANES // part):
            out[p * (LANES // part) + k, pl.ds(0, part), :] = state[k * part : (k + 1) * part]


def own_state(x, step_t, decay_t, b, count):
    heads, toks = decay_t.shape
    part = x.shape[1] // count
    return pl.pallas_call(
        state_kernel,
        out_shape=[
            jax.ShapeDtypeStruct((count, part + 16, b.shape[1]), BF),
            jax.ShapeDtypeStruct((heads, toks), F32),
        ],
        compiler_params=params(8),
        name="own_state",
    )(in_hbm(x), in_hbm(step_t), in_hbm(decay_t), in_hbm(b))


def prefix_kernel(place_ref, got, start, back):
    count, part, _ = back.shape
    heads = 16
    held = max(1, heads // count)
    group = part // held
    first = place_ref[0] * heads // count
    row = lax.broadcasted_iota(jnp.int32, (heads, LANES), 0)
    carries = [start[pl.ds(h * group, group), :] for h in range(held)]
    for turn in range(count):
        extra = got[turn, pl.ds(part, 16), :].astype(F32)
        scale = extra[:, :1] + extra[:, LANES // 2 : LANES // 2 + 1]
        for h in range(held):
            spot = pl.ds(h * group, group)
            back[turn, spot, :] = carries[h].astype(BF)
            factor = jnp.sum(jnp.where(row == first + h, scale, 0.0), axis=0, keepdims=True)
            carries[h] = factor * carries[h] + got[turn, spot, :].astype(F32)


def exchange_halves(pieces):
    count = lax.axis_size("seq")
    halves = []
    for turn in range(2):
        got = []
        for k in range(turn * count // 2, (turn + 1) * count // 2):
            piece = pieces[turn][k - turn * count // 2]
            if k > 0:
                piece = lax.ppermute(piece, "seq", [(i, i ^ k) for i in range(count)])
            got.append(piece)
        halves.append(jnp.concatenate(got))
    return halves


def entering_state(got, init_rows):
    count, rows, width = got.shape
    part = rows - 16
    place = lax.axis_index("seq")
    start = lax.dynamic_slice_in_dim(init_rows, place * part, part, 0)
    vmem = pl.BlockSpec(memory_space=pltpu.VMEM)
    return pl.pallas_call(
        prefix_kernel,
        in_specs=[pl.BlockSpec(memory_space=pltpu.SMEM), vmem, vmem],
        out_shape=jax.ShapeDtypeStruct((count, part, width), BF),
        compiler_params=params(8),
        name="prefix",
    )(place.reshape(1), got, start)


def within_kernel(skip, x, step_t, cum_t, b, c, out):
    heads, toks = cum_t.shape
    row = lax.broadcasted_iota(jnp.int32, (toks, toks), 0)
    col = lax.broadcasted_iota(jnp.int32, (toks, toks), 1)
    causal = row >= col
    nt = (((1,), (1,)), ((), ()))
    scores = lax.dot_general(c[...], b[...], nt, preferred_element_type=F32)
    cum = cum_t[...].T
    for p in range(heads // 2):
        pair = x[:, p * LANES : (p + 1) * LANES]
        sums = []
        for h in (2 * p, 2 * p + 1):
            gap = cum[:, h : h + 1] - cum_t[h : h + 1, :]
            decay = jnp.where(causal, jnp.exp(jnp.where(causal, gap, 0.0)), 0.0)
            weights = (decay * scores * step_t[h : h + 1, :]).astype(BF)
            sums.append(jnp.dot(weights, pair, preferred_element_type=F32))
        gain = by_pair(skip[2 * p], skip[2 * p + 1], toks)
        out[:, p * LANES : (p + 1) * LANES] = (
            by_pair(sums[0], sums[1], toks) + gain * pair.astype(F32)
        )


def within_block(skip, x, step_t, cum_t, b, c):
    toks, inner = x.shape
    heads = cum_t.shape[0]
    vmem = pl.BlockSpec(memory_space=pltpu.VMEM)
    return pl.pallas_call(
        within_kernel,
        in_specs=[pl.BlockSpec(memory_space=pltpu.SMEM)] + [vmem] * 5,
        out_shape=jax.ShapeDtypeStruct((toks, inner), F32),
        compiler_params=params(8),
        cost_estimate=pl.CostEstimate(
            flops=4 * heads * toks * toks * LANES,
            bytes_accessed=6 * toks * inner,
            transcendentals=heads * toks * toks,
        ),
        name="within_block",
    )(skip, in_hbm(x), in_hbm(step_t), cum_t, in_hbm(b), in_hbm(c))


def fetch(sems, *pairs):
    copies = [pltpu.make_async_copy(src, dst, sems.at[i]) for i, (src, dst) in enumerate(pairs)]
    for copy in copies:
        copy.start()
    return copies


def cuts_of(ref, count):
    rows = ref.shape[0] // count
    return [ref.at[pl.ds(k * rows, rows)] for k in range(count)]


def quarters(place_ref, share):
    return [pl.ds(pl.multiple_of((place_ref[0] ^ k) * share, share), share) for k in range(4)]


def tail_kernel(
    place_ref, c_in, cum_in, gain_in, arriving_in, direct_in, z_in, weight_in, tokens_in,
    near, last, keep, passing,
    c, cum_t, gain, arriving, direct, z, weight, tokens, normed, sems,
):
    heads, toks = cum_t.shape
    share = near.shape[1]
    spots = quarters(place_ref, share)
    copies = fetch(
        sems,
        (cum_in, cum_t),
        (gain_in, gain),
        (c_in, c),
        (arriving_in, arriving),
        (z_in, z),
        (direct_in, direct),
        *zip(cuts_of(weight_in, 8), cuts_of(weight, 8)),
        (tokens_in.at[:, spots[0]], tokens),
    )
    for copy in copies[:6]:
        copy.wait()
    grown = jnp.exp(cum_t[...]).T
    lane = lax.broadcasted_iota(jnp.int32, (toks, LANES), 1)
    left = lane < LANES // 2
    nt = (((1,), (1,)), ((), ()))
    for p in range(heads // 2):
        spot = pl.ds(p * LANES, LANES)
        inter = lax.dot_general(c[...], arriving[spot, :], nt, preferred_element_type=F32)
        factor = by_pair(grown[:, 2 * p : 2 * p + 1], grown[:, 2 * p + 1 : 2 * p + 2], toks)
        wide = z[:, spot].astype(F32)
        gated = (direct[:, spot] + inter * factor) * (wide * (1.0 / (1.0 + jnp.exp(-wide))))
        square = gated * gated
        first = jnp.sum(jnp.where(left, square, 0.0), axis=1, keepdims=True)
        second = jnp.sum(jnp.where(left, 0.0, square), axis=1, keepdims=True)
        mean = by_pair(first, second, toks) * (2.0 / LANES)
        normed[:, spot] = (gated * lax.rsqrt(mean + 1e-05) * gain[:, spot]).astype(BF)
    for copy in copies[6:]:
        copy.wait()
    for k, out in ((3, last), (1, near), (2, passing), (0, keep)):
        part = jnp.dot(normed[...], weight[:, spots[k]], preferred_element_type=F32)
        if k == 0:
            part += tokens[...].astype(F32)
        out[...] = part.astype(out.dtype)


def mixer_tail(place, c, arriving, cum_t, direct, z, gain, weight, tokens):
    heads, toks = cum_t.shape
    inner, width = weight.shape
    share = width // 4
    operands = (c, cum_t, gain.reshape(1, inner), arriving, direct, z, weight, tokens)
    fixed = (0, 2, 5, 6, 7)
    operands = [in_hbm(a) if i in fixed else a for i, a in enumerate(operands)]
    return pl.pallas_call(
        tail_kernel,
        in_specs=[pl.BlockSpec(memory_space=pltpu.SMEM)]
        + [pl.BlockSpec(memory_space=pl.ANY)] * len(operands),
        out_shape=[jax.ShapeDtypeStruct((toks, share), kind) for kind in (BF, BF, F32, F32)],
        scratch_shapes=[pltpu.VMEM(a.shape, a.dtype) for a in operands[:-1]]
        + [
            pltpu.VMEM((toks, share), BF),
            pltpu.VMEM((toks, inner), BF),
            pltpu.SemaphoreType.DMA((15,)),
        ],
        compiler_params=params(12),
        cost_estimate=pl.CostEstimate(
            flops=2 * toks * inner * width,
            bytes_accessed=2 * inner * width + 14 * toks * inner,
            transcendentals=toks * inner,
        ),
        name="mixer_tail",
    )(place.reshape(1), *operands)


def expert_kernel(
    place_ref, gain_in, own_in, near_in, far_in, last_in, wg_in, wu_in, wd_in,
    near_out, last_out, keep_out, pass_out,
    gain, own, near, far, last, wg, wu, wd, rows, sems,
):
    count, share = own.shape
    width = 4 * share
    spots = quarters(place_ref, share)
    copies = fetch(
        sems,
        (gain_in, gain),
        (own_in, own),
        (near_in, near),
        (far_in, far),
        (last_in, last),
        *((w_in.at[s], w.at[s]) for s in spots for w_in, w in ((wg_in, wg), (wu_in, wu))),
        *zip(cuts_of(wd_in, 4), cuts_of(wd, 4)),
    )
    for copy in copies[:5]:
        copy.wait()

    @pl.loop(0, count, step=64)
    def _(start):
        spot = pl.ds(pl.multiple_of(start, 64), 64)
        wide = [p[spot, :].astype(F32) for p in (own, near, far, last)]
        square = sum(jnp.sum(w * w, axis=1, keepdims=True) for w in wide)
        scale = lax.rsqrt(square * (1.0 / width) + 1e-05)
        for k in range(4):
            rows[k, spot, :] = (wide[k] * scale * gain[:, spots[k]]).astype(BF)

    gate = up = 0.0
    for k in range(4):
        copies[5 + 2 * k].wait()
        gate += jnp.dot(rows[k], wg[spots[k], :], preferred_element_type=F32)
        copies[6 + 2 * k].wait()
        up += jnp.dot(rows[k], wu[spots[k], :], preferred_element_type=F32)
    act = (gate * (1.0 / (1.0 + jnp.exp(-gate))) * up).astype(BF)
    for copy in copies[13:]:
        copy.wait()
    for k, out in ((3, last_out), (1, near_out), (2, pass_out), (0, keep_out)):
        out[...] = jnp.dot(act, wd[:, spots[k]], preferred_element_type=F32).astype(BF)


def run_expert(place, gain, own, near, far, last, wg, wu, wd):
    rows, share = own.shape
    width, inner = wg.shape
    weights = (in_hbm(wg), in_hbm(wu), in_hbm(wd))
    operands = (in_hbm(gain.reshape(1, width)), own, near, far, last, *weights)
    return pl.pallas_call(
        expert_kernel,
        in_specs=[pl.BlockSpec(memory_space=pltpu.SMEM)]
        + [pl.BlockSpec(memory_space=pl.ANY)] * len(operands),
        out_shape=[jax.ShapeDtypeStruct((rows, share), BF)] * 4,
        scratch_shapes=[pltpu.VMEM(a.shape, a.dtype) for a in operands]
        + [
            pltpu.VMEM((4, rows, share), BF),
            pltpu.SemaphoreType.DMA((17,)),
        ],
        compiler_params=params(16),
        cost_estimate=pl.CostEstimate(flops=1, bytes_accessed=1, transcendentals=0),
        name="expert",
    )(place.reshape(1), *operands)


def body(
    tokens,
    input_heads,
    z_gate,
    b_proj,
    c_proj,
    step_size,
    decay_log,
    skip_gain,
    init_state,
    norm_gain,
    out_weight,
    moe_gain,
    routes,
    route_weights,
    w_gate,
    w_up,
    w_down,
):
    tok_rows, inner = input_heads.shape
    state_size = init_state.shape[2]
    seq_count = lax.axis_size("seq")
    place = lax.axis_index("tp")
    step_t = step_size.T
    outgoing, cum_t = own_state(input_heads, step_t, decay_log.T, b_proj, seq_count)
    got = exchange(outgoing)
    direct = within_block(skip_gain, input_heads, step_t, cum_t, b_proj, c_proj)
    back = entering_state(got, init_state.reshape(inner, state_size))
    arriving = exchange(back).reshape(inner, state_size)
    model_width = out_weight.shape[1]
    share = model_width // 4
    expert_count = w_gate.shape[0] * seq_count
    slot_count = 4 * tok_rows // seq_count
    top_count = routes.shape[1]
    items = top_count * tok_rows
    slots = expert_count * slot_count
    flat_expert = routes.T.reshape(-1)
    onehot = flat_expert[:, None] == jnp.arange(expert_count, dtype=jnp.int32)[None, :]
    before = jnp.arange(items)[:, None] > jnp.arange(items)[None, :]
    earlier = jnp.dot(before.astype(BF), onehot.astype(BF), preferred_element_type=F32)
    rank = jnp.sum(jnp.where(onehot, earlier, 0.0), axis=1).astype(jnp.int32)
    few = seq_count <= 8
    layout = flat_expert ^ lax.axis_index("seq") if few else flat_expert
    placed = layout * slot_count + rank
    spots = placed[:, None] == jnp.arange(slots, dtype=jnp.int32)[None, :]
    spots = spots.reshape(top_count, tok_rows, slots)
    fill = jnp.any(spots, axis=0).astype(BF)
    combine = jnp.sum(jnp.where(spots, route_weights.T[:, :, None], 0.0), axis=0)
    direct = after(direct, fill, combine)

    to_near, to_last, keep, passing = mixer_tail(
        place, c_proj, arriving, cum_t, direct, z_gate, norm_gain, out_weight, tokens
    )

    from_last = swap(to_last, 1)
    from_near = swap(to_near, 1)
    from_far = swap((passing + from_last.astype(F32)).astype(BF), 2)
    hidden = (keep + from_near.astype(F32) + from_far.astype(F32)).astype(BF)

    outgoing = lax.dot_general(
        fill, hidden, (((0,), (0,)), ((), ())), preferred_element_type=F32
    ).astype(BF)
    outgoing = outgoing.reshape(expert_count, slot_count, share)

    cut = slots // 2
    middle = expert_count // 2
    if few:
        own = exchange_halves((outgoing[:middle], outgoing[middle:]))
    else:
        arrived = exchange(outgoing).reshape(slots, share)
        own = [arrived[:cut], arrived[cut:]]
    far = [swap(part, 2) for part in own]
    near = [swap(part, 1) for part in own]
    weights = (w_gate[0], w_up[0], w_down[0])
    last = swap(far[0], 1)
    to_near0, to_last0, keep0, pass0 = run_expert(
        place, moe_gain, own[0], near[0], far[0], last, *weights
    )
    from_last0 = swap(to_last0, 1)
    last = swap(after(far[1], to_last0), 1)
    pass0 = (pass0.astype(F32) + from_last0.astype(F32)).astype(BF)
    from_far0 = swap(pass0, 2)
    to_near1, to_last1, keep1, pass1 = run_expert(
        place, moe_gain, after(own[1], pass0), near[1], far[1], last, *weights
    )
    from_last1 = swap(to_last1, 1)
    from_near0 = swap(after(to_near0, from_far0), 1)
    pass1 = (pass1.astype(F32) + from_last1.astype(F32)).astype(BF)
    from_far1 = swap(pass1, 2)
    from_near1 = swap(after(to_near1, pass1), 1)
    results = [
        (keep.astype(F32) + from_near.astype(F32) + from_far.astype(F32)).astype(BF)
        for keep, from_near, from_far in (
            (keep0, from_near0, from_far0),
            (keep1, from_near1, from_far1),
        )
    ]
    if few:
        results = [part.reshape(middle, slot_count, share) for part in results]
        returned = jnp.concatenate(exchange_halves(results))
    else:
        results = jnp.concatenate(results).reshape(expert_count, slot_count, share)
        returned = exchange(results).reshape(slots, share)
    mixed = hidden.astype(F32) + jnp.dot(
        combine,
        returned.astype(F32),
        precision=lax.Precision.HIGHEST,
        preferred_element_type=F32,
    )
    return mixed.astype(BF)


def solution(mesh):
    in_specs = (
        P("seq", None),
        P("seq", "tp"),
        P("seq", "tp"),
        P("seq", None),
        P("seq", None),
        P("seq", "tp"),
        P("seq", "tp"),
        P("tp"),
        P("tp", None, None),
        P("tp"),
        P("tp", None),
        P(),
        P("seq", None),
        P("seq", None),
        P("seq", None, "tp"),
        P("seq", None, "tp"),
        P("seq", "tp", None),
    )
    out_specs = P("seq", "tp")
    return jax.shard_map(body, mesh=mesh, in_specs=in_specs, out_specs=out_specs, check_vma=False)
```

```python
import jax
import jax.numpy as jnp
from jax import lax
from jax.experimental import pallas as pl
from jax.experimental.pallas import tpu as pltpu
from jax.sharding import PartitionSpec as P

BF = jnp.bfloat16
F32 = jnp.float32
MIB = 1024 * 1024
LANES = 128


def swap(value, bit):
    count = lax.axis_size("tp")
    return lax.ppermute(value, "tp", [(i, i ^ bit) for i in range(count)])


def exchange(value):
    return lax.all_to_all(value, "seq", split_axis=0, concat_axis=0, tiled=True)


def after(value, *others):
    return lax.optimization_barrier((value, *others))[0]


def in_hbm(value):
    return pltpu.with_memory_space_constraint(value, pltpu.HBM)


def params(mib):
    return pltpu.CompilerParams(vmem_limit_bytes=mib * MIB)


def whole(*shape):
    return pl.BlockSpec(shape, lambda *_: (0,) * len(shape))


def by_pair(left, right, size):
    lane = lax.broadcasted_iota(jnp.int32, (size, LANES), 1)
    return jnp.where(lane < LANES // 2, left, right)


def state_kernel(x, step_t, decay_t, b, out, cum_out):
    count, rows, _ = out.shape
    part = rows - 16
    heads, toks = decay_t.shape
    row = lax.broadcasted_iota(jnp.int32, (toks, toks), 0)
    col = lax.broadcasted_iota(jnp.int32, (toks, toks), 1)
    upper = (row <= col).astype(F32)
    cum_t = jnp.dot(
        decay_t[...], upper, precision=lax.Precision.HIGHEST, preferred_element_type=F32
    )
    cum_out[...] = cum_t
    end = cum_t[:, toks - 1 : toks]
    scale = (jnp.exp(end - cum_t) * step_t[...]).T
    decay = jnp.broadcast_to(jnp.exp(end), (heads, LANES))
    high = decay.astype(BF).astype(F32)
    extra = by_pair(high, decay - high, heads).astype(BF)
    for k in range(count):
        out[k, pl.ds(part, 16), :] = extra
    for p in range(heads // 2):
        pair = x[:, p * LANES : (p + 1) * LANES].astype(F32)
        factor = by_pair(scale[:, 2 * p : 2 * p + 1], scale[:, 2 * p + 1 : 2 * p + 2], toks)
        state = lax.dot_general(
            (pair * factor).astype(BF),
            b[...],
            (((0,), (0,)), ((), ())),
            preferred_element_type=F32,
        ).astype(BF)
        for k in range(LANES // part):
            out[p * (LANES // part) + k, pl.ds(0, part), :] = state[k * part : (k + 1) * part]


def own_state(x, step_t, decay_t, b, count):
    heads, toks = decay_t.shape
    part = x.shape[1] // count
    return pl.pallas_call(
        state_kernel,
        out_shape=[
            jax.ShapeDtypeStruct((count, part + 16, b.shape[1]), BF),
            jax.ShapeDtypeStruct((heads, toks), F32),
        ],
        compiler_params=params(8),
        name="own_state",
    )(in_hbm(x), in_hbm(step_t), in_hbm(decay_t), in_hbm(b))


def prefix_kernel(place_ref, got, start, back):
    count, part, _ = back.shape
    heads = 16
    held = max(1, heads // count)
    group = part // held
    first = place_ref[0] * heads // count
    row = lax.broadcasted_iota(jnp.int32, (heads, LANES), 0)
    carries = [start[pl.ds(h * group, group), :] for h in range(held)]
    for turn in range(count):
        extra = got[turn, pl.ds(part, 16), :].astype(F32)
        scale = extra[:, :1] + extra[:, LANES // 2 : LANES // 2 + 1]
        for h in range(held):
            spot = pl.ds(h * group, group)
            back[turn, spot, :] = carries[h].astype(BF)
            factor = jnp.sum(jnp.where(row == first + h, scale, 0.0), axis=0, keepdims=True)
            carries[h] = factor * carries[h] + got[turn, spot, :].astype(F32)


HALVES = ((0, 1, 4, 5), (2, 3, 6, 7))


def exchange_halves(pieces):
    halves = []
    for order, part in zip(HALVES, pieces):
        got = []
        for spot, k in enumerate(order):
            piece = part[spot]
            if k > 0:
                piece = lax.ppermute(piece, "seq", [(i, i ^ k) for i in range(8)])
            got.append(piece)
        halves.append(jnp.concatenate(got))
    return halves


def entering_state(got, init_rows):
    count, rows, width = got.shape
    part = rows - 16
    place = lax.axis_index("seq")
    start = lax.dynamic_slice_in_dim(init_rows, place * part, part, 0)
    vmem = pl.BlockSpec(memory_space=pltpu.VMEM)
    return pl.pallas_call(
        prefix_kernel,
        in_specs=[pl.BlockSpec(memory_space=pltpu.SMEM), vmem, vmem],
        out_shape=jax.ShapeDtypeStruct((count, part, width), BF),
        compiler_params=params(8),
        name="prefix",
    )(place.reshape(1), got, start)


def within_kernel(skip, x, step_t, cum_t, b, c, out):
    heads, toks = cum_t.shape
    row = lax.broadcasted_iota(jnp.int32, (toks, toks), 0)
    col = lax.broadcasted_iota(jnp.int32, (toks, toks), 1)
    causal = row >= col
    nt = (((1,), (1,)), ((), ()))
    scores = lax.dot_general(c[...], b[...], nt, preferred_element_type=F32)
    cum = cum_t[...].T
    for p in range(heads // 2):
        pair = x[:, p * LANES : (p + 1) * LANES]
        sums = []
        for h in (2 * p, 2 * p + 1):
            gap = cum[:, h : h + 1] - cum_t[h : h + 1, :]
            decay = jnp.where(causal, jnp.exp(jnp.where(causal, gap, 0.0)), 0.0)
            weights = (decay * scores * step_t[h : h + 1, :]).astype(BF)
            sums.append(jnp.dot(weights, pair, preferred_element_type=F32))
        gain = by_pair(skip[2 * p], skip[2 * p + 1], toks)
        out[:, p * LANES : (p + 1) * LANES] = (
            by_pair(sums[0], sums[1], toks) + gain * pair.astype(F32)
        )


def within_block(skip, x, step_t, cum_t, b, c):
    toks, inner = x.shape
    heads = cum_t.shape[0]
    vmem = pl.BlockSpec(memory_space=pltpu.VMEM)
    return pl.pallas_call(
        within_kernel,
        in_specs=[pl.BlockSpec(memory_space=pltpu.SMEM)] + [vmem] * 5,
        out_shape=jax.ShapeDtypeStruct((toks, inner), F32),
        compiler_params=params(8),
        cost_estimate=pl.CostEstimate(
            flops=4 * heads * toks * toks * LANES,
            bytes_accessed=6 * toks * inner,
            transcendentals=heads * toks * toks,
        ),
        name="within_block",
    )(skip, in_hbm(x), in_hbm(step_t), cum_t, in_hbm(b), in_hbm(c))


def fetch(sems, *pairs):
    copies = [pltpu.make_async_copy(src, dst, sems.at[i]) for i, (src, dst) in enumerate(pairs)]
    for copy in copies:
        copy.start()
    return copies


def cuts_of(ref, count):
    rows = ref.shape[0] // count
    return [ref.at[pl.ds(k * rows, rows)] for k in range(count)]


def quarters(place_ref, share):
    return [pl.ds(pl.multiple_of((place_ref[0] ^ k) * share, share), share) for k in range(4)]


def tail_kernel(
    place_ref, c_in, cum_in, gain_in, arriving_in, direct_in, z_in, weight_in, tokens_in,
    near, last, keep, passing,
    c, cum_t, gain, arriving, direct, z, weight, tokens, normed, sems,
):
    heads, toks = cum_t.shape
    share = near.shape[1]
    spots = quarters(place_ref, share)
    copies = fetch(
        sems,
        (cum_in, cum_t),
        (gain_in, gain),
        (c_in, c),
        (arriving_in, arriving),
        (z_in, z),
        (direct_in, direct),
        *zip(cuts_of(weight_in, 8), cuts_of(weight, 8)),
        (tokens_in.at[:, spots[0]], tokens),
    )
    for copy in copies[:6]:
        copy.wait()
    grown = jnp.exp(cum_t[...]).T
    lane = lax.broadcasted_iota(jnp.int32, (toks, LANES), 1)
    left = lane < LANES // 2
    nt = (((1,), (1,)), ((), ()))
    for p in range(heads // 2):
        spot = pl.ds(p * LANES, LANES)
        inter = lax.dot_general(c[...], arriving[spot, :], nt, preferred_element_type=F32)
        factor = by_pair(grown[:, 2 * p : 2 * p + 1], grown[:, 2 * p + 1 : 2 * p + 2], toks)
        wide = z[:, spot].astype(F32)
        gated = (direct[:, spot] + inter * factor) * (wide * (1.0 / (1.0 + jnp.exp(-wide))))
        square = gated * gated
        first = jnp.sum(jnp.where(left, square, 0.0), axis=1, keepdims=True)
        second = jnp.sum(jnp.where(left, 0.0, square), axis=1, keepdims=True)
        mean = by_pair(first, second, toks) * (2.0 / LANES)
        normed[:, spot] = (gated * lax.rsqrt(mean + 1e-05) * gain[:, spot]).astype(BF)
    for copy in copies[6:]:
        copy.wait()
    for k, out in ((3, last), (1, near), (2, passing), (0, keep)):
        part = jnp.dot(normed[...], weight[:, spots[k]], preferred_element_type=F32)
        if k == 0:
            part += tokens[...].astype(F32)
        out[...] = part.astype(out.dtype)


def mixer_tail(place, c, arriving, cum_t, direct, z, gain, weight, tokens):
    heads, toks = cum_t.shape
    inner, width = weight.shape
    share = width // 4
    operands = (c, cum_t, gain.reshape(1, inner), arriving, direct, z, weight, tokens)
    fixed = (0, 2, 5, 6, 7)
    operands = [in_hbm(a) if i in fixed else a for i, a in enumerate(operands)]
    return pl.pallas_call(
        tail_kernel,
        in_specs=[pl.BlockSpec(memory_space=pltpu.SMEM)]
        + [pl.BlockSpec(memory_space=pl.ANY)] * len(operands),
        out_shape=[jax.ShapeDtypeStruct((toks, share), kind) for kind in (BF, BF, F32, F32)],
        scratch_shapes=[pltpu.VMEM(a.shape, a.dtype) for a in operands[:-1]]
        + [
            pltpu.VMEM((toks, share), BF),
            pltpu.VMEM((toks, inner), BF),
            pltpu.SemaphoreType.DMA((15,)),
        ],
        compiler_params=params(12),
        cost_estimate=pl.CostEstimate(
            flops=2 * toks * inner * width,
            bytes_accessed=2 * inner * width + 14 * toks * inner,
            transcendentals=toks * inner,
        ),
        name="mixer_tail",
    )(place.reshape(1), *operands)


def expert_kernel(
    place_ref, gain_in, own_in, near_in, far_in, last_in, wg_in, wu_in, wd_in,
    near_out, last_out, keep_out, pass_out,
    gain, own, near, far, last, wg, wu, wd, rows, sems,
):
    count, share = own.shape
    width = 4 * share
    spots = quarters(place_ref, share)
    copies = fetch(
        sems,
        (gain_in, gain),
        (own_in, own),
        (near_in, near),
        (far_in, far),
        (last_in, last),
        *((w_in.at[s], w.at[s]) for s in spots for w_in, w in ((wg_in, wg), (wu_in, wu))),
        *zip(cuts_of(wd_in, 4), cuts_of(wd, 4)),
    )
    for copy in copies[:5]:
        copy.wait()

    @pl.loop(0, count, step=64)
    def _(start):
        spot = pl.ds(pl.multiple_of(start, 64), 64)
        wide = [p[spot, :].astype(F32) for p in (own, near, far, last)]
        square = sum(jnp.sum(w * w, axis=1, keepdims=True) for w in wide)
        scale = lax.rsqrt(square * (1.0 / width) + 1e-05)
        for k in range(4):
            rows[k, spot, :] = (wide[k] * scale * gain[:, spots[k]]).astype(BF)

    gate = up = 0.0
    for k in range(4):
        copies[5 + 2 * k].wait()
        gate += jnp.dot(rows[k], wg[spots[k], :], preferred_element_type=F32)
        copies[6 + 2 * k].wait()
        up += jnp.dot(rows[k], wu[spots[k], :], preferred_element_type=F32)
    act = (gate * (1.0 / (1.0 + jnp.exp(-gate))) * up).astype(BF)
    for copy in copies[13:]:
        copy.wait()
    for k, out in ((3, last_out), (1, near_out), (2, pass_out), (0, keep_out)):
        out[...] = jnp.dot(act, wd[:, spots[k]], preferred_element_type=F32).astype(BF)


def run_expert(place, gain, own, near, far, last, wg, wu, wd):
    rows, share = own.shape
    width, inner = wg.shape
    weights = (in_hbm(wg), in_hbm(wu), in_hbm(wd))
    operands = (in_hbm(gain.reshape(1, width)), own, near, far, last, *weights)
    return pl.pallas_call(
        expert_kernel,
        in_specs=[pl.BlockSpec(memory_space=pltpu.SMEM)]
        + [pl.BlockSpec(memory_space=pl.ANY)] * len(operands),
        out_shape=[jax.ShapeDtypeStruct((rows, share), BF)] * 4,
        scratch_shapes=[pltpu.VMEM(a.shape, a.dtype) for a in operands]
        + [
            pltpu.VMEM((4, rows, share), BF),
            pltpu.SemaphoreType.DMA((17,)),
        ],
        compiler_params=params(16),
        cost_estimate=pl.CostEstimate(flops=1, bytes_accessed=1, transcendentals=0),
        name="expert",
    )(place.reshape(1), *operands)


def body(
    tokens,
    input_heads,
    z_gate,
    b_proj,
    c_proj,
    step_size,
    decay_log,
    skip_gain,
    init_state,
    norm_gain,
    out_weight,
    moe_gain,
    routes,
    route_weights,
    w_gate,
    w_up,
    w_down,
):
    tok_rows, inner = input_heads.shape
    state_size = init_state.shape[2]
    seq_count = lax.axis_size("seq")
    place = lax.axis_index("tp")
    step_t = step_size.T
    outgoing, cum_t = own_state(input_heads, step_t, decay_log.T, b_proj, seq_count)
    got = exchange(outgoing)
    direct = within_block(skip_gain, input_heads, step_t, cum_t, b_proj, c_proj)
    back = entering_state(got, init_state.reshape(inner, state_size))
    arriving = exchange(back).reshape(inner, state_size)
    model_width = out_weight.shape[1]
    share = model_width // 4
    expert_count = w_gate.shape[0] * seq_count
    slot_count = 4 * tok_rows // seq_count
    top_count = routes.shape[1]
    items = top_count * tok_rows
    slots = expert_count * slot_count
    flat_expert = routes.T.reshape(-1)
    onehot = flat_expert[:, None] == jnp.arange(expert_count, dtype=jnp.int32)[None, :]
    before = jnp.arange(items)[:, None] > jnp.arange(items)[None, :]
    earlier = jnp.dot(before.astype(BF), onehot.astype(BF), preferred_element_type=F32)
    rank = jnp.sum(jnp.where(onehot, earlier, 0.0), axis=1).astype(jnp.int32)
    few = seq_count == 8
    layout = flat_expert
    if few:
        layout = flat_expert ^ lax.axis_index("seq")
        layout = (layout & 1) | ((layout & 2) << 1) | ((layout & 4) >> 1)
    placed = layout * slot_count + rank
    spots = placed[:, None] == jnp.arange(slots, dtype=jnp.int32)[None, :]
    spots = spots.reshape(top_count, tok_rows, slots)
    fill = jnp.any(spots, axis=0).astype(BF)
    combine = jnp.sum(jnp.where(spots, route_weights.T[:, :, None], 0.0), axis=0)
    direct = after(direct, fill, combine)

    to_near, to_last, keep, passing = mixer_tail(
        place, c_proj, arriving, cum_t, direct, z_gate, norm_gain, out_weight, tokens
    )

    from_last = swap(to_last, 1)
    from_near = swap(to_near, 1)
    from_far = swap((passing + from_last.astype(F32)).astype(BF), 2)
    hidden = (keep + from_near.astype(F32) + from_far.astype(F32)).astype(BF)

    outgoing = lax.dot_general(
        fill, hidden, (((0,), (0,)), ((), ())), preferred_element_type=F32
    ).astype(BF)
    outgoing = outgoing.reshape(expert_count, slot_count, share)

    cut = slots // 2
    middle = expert_count // 2
    if few:
        own = exchange_halves((outgoing[:middle], outgoing[middle:]))
    else:
        arrived = exchange(outgoing).reshape(slots, share)
        own = [arrived[:cut], arrived[cut:]]
    far = [swap(part, 2) for part in own]
    near = [swap(part, 1) for part in own]
    weights = (w_gate[0], w_up[0], w_down[0])
    last = swap(far[0], 1)
    to_near0, to_last0, keep0, pass0 = run_expert(
        place, moe_gain, own[0], near[0], far[0], last, *weights
    )
    from_last0 = swap(to_last0, 1)
    last = swap(after(far[1], to_last0), 1)
    pass0 = (pass0.astype(F32) + from_last0.astype(F32)).astype(BF)
    from_far0 = swap(pass0, 2)
    to_near1, to_last1, keep1, pass1 = run_expert(
        place, moe_gain, after(own[1], pass0), near[1], far[1], last, *weights
    )
    from_last1 = swap(to_last1, 1)
    from_near0 = swap(after(to_near0, from_far0), 1)
    pass1 = (pass1.astype(F32) + from_last1.astype(F32)).astype(BF)
    from_far1 = swap(pass1, 2)
    from_near1 = swap(after(to_near1, pass1), 1)
    results = [
        (keep.astype(F32) + from_near.astype(F32) + from_far.astype(F32)).astype(BF)
        for keep, from_near, from_far in (
            (keep0, from_near0, from_far0),
            (keep1, from_near1, from_far1),
        )
    ]
    if few:
        results = [part.reshape(middle, slot_count, share) for part in results]
        returned = jnp.concatenate(exchange_halves(results))
    else:
        results = jnp.concatenate(results).reshape(expert_count, slot_count, share)
        returned = exchange(results).reshape(slots, share)
    mixed = hidden.astype(F32) + jnp.dot(
        combine,
        returned.astype(F32),
        precision=lax.Precision.HIGHEST,
        preferred_element_type=F32,
    )
    return mixed.astype(BF)


def solution(mesh):
    in_specs = (
        P("seq", None),
        P("seq", "tp"),
        P("seq", "tp"),
        P("seq", None),
        P("seq", None),
        P("seq", "tp"),
        P("seq", "tp"),
        P("tp"),
        P("tp", None, None),
        P("tp"),
        P("tp", None),
        P(),
        P("seq", None),
        P("seq", None),
        P("seq", None, "tp"),
        P("seq", None, "tp"),
        P("seq", "tp", None),
    )
    out_specs = P("seq", "tp")
    return jax.shard_map(body, mesh=mesh, in_specs=in_specs, out_specs=out_specs, check_vma=False)
```

```python
import jax
import jax.numpy as jnp
from jax import lax
from jax.experimental import pallas as pl
from jax.experimental.pallas import tpu as pltpu
from jax.sharding import PartitionSpec as P

BF = jnp.bfloat16
F32 = jnp.float32
MIB = 1024 * 1024
LANES = 128


def swap(value, bit):
    count = lax.axis_size("tp")
    return lax.ppermute(value, "tp", [(i, i ^ bit) for i in range(count)])


def exchange(value):
    return lax.all_to_all(value, "seq", split_axis=0, concat_axis=0, tiled=True)


def after(value, *others):
    return lax.optimization_barrier((value, *others))[0]


def in_hbm(value):
    return pltpu.with_memory_space_constraint(value, pltpu.HBM)


def params(mib):
    return pltpu.CompilerParams(vmem_limit_bytes=mib * MIB)


def whole(*shape):
    return pl.BlockSpec(shape, lambda *_: (0,) * len(shape))


def by_pair(left, right, size):
    lane = lax.broadcasted_iota(jnp.int32, (size, LANES), 1)
    return jnp.where(lane < LANES // 2, left, right)


def state_kernel(x, step_t, decay_t, b, out, cum_out):
    count, rows, _ = out.shape
    part = rows - 16
    heads, toks = decay_t.shape
    row = lax.broadcasted_iota(jnp.int32, (toks, toks), 0)
    col = lax.broadcasted_iota(jnp.int32, (toks, toks), 1)
    upper = (row <= col).astype(F32)
    cum_t = jnp.dot(
        decay_t[...], upper, precision=lax.Precision.HIGHEST, preferred_element_type=F32
    )
    cum_out[...] = cum_t
    end = cum_t[:, toks - 1 : toks]
    scale = (jnp.exp(end - cum_t) * step_t[...]).T
    decay = jnp.broadcast_to(jnp.exp(end), (heads, LANES))
    high = decay.astype(BF).astype(F32)
    extra = by_pair(high, decay - high, heads).astype(BF)
    for k in range(count):
        out[k, pl.ds(part, 16), :] = extra
    for p in range(heads // 2):
        pair = x[:, p * LANES : (p + 1) * LANES].astype(F32)
        factor = by_pair(scale[:, 2 * p : 2 * p + 1], scale[:, 2 * p + 1 : 2 * p + 2], toks)
        state = lax.dot_general(
            (pair * factor).astype(BF),
            b[...],
            (((0,), (0,)), ((), ())),
            preferred_element_type=F32,
        ).astype(BF)
        for k in range(LANES // part):
            out[p * (LANES // part) + k, pl.ds(0, part), :] = state[k * part : (k + 1) * part]


def own_state(x, step_t, decay_t, b, count):
    heads, toks = decay_t.shape
    part = x.shape[1] // count
    return pl.pallas_call(
        state_kernel,
        out_shape=[
            jax.ShapeDtypeStruct((count, part + 16, b.shape[1]), BF),
            jax.ShapeDtypeStruct((heads, toks), F32),
        ],
        compiler_params=params(8),
        name="own_state",
    )(in_hbm(x), in_hbm(step_t), in_hbm(decay_t), in_hbm(b))


def prefix_kernel(place_ref, got, start, back):
    count, part, _ = back.shape
    heads = 16
    held = max(1, heads // count)
    group = part // held
    first = place_ref[0] * heads // count
    row = lax.broadcasted_iota(jnp.int32, (heads, LANES), 0)
    carries = [start[pl.ds(h * group, group), :] for h in range(held)]
    for turn in range(count):
        extra = got[turn, pl.ds(part, 16), :].astype(F32)
        scale = extra[:, :1] + extra[:, LANES // 2 : LANES // 2 + 1]
        for h in range(held):
            spot = pl.ds(h * group, group)
            back[turn, spot, :] = carries[h].astype(BF)
            factor = jnp.sum(jnp.where(row == first + h, scale, 0.0), axis=0, keepdims=True)
            carries[h] = factor * carries[h] + got[turn, spot, :].astype(F32)


PARTS = ((2, 3, 5, 6, 7), (0, 1, 4))


def exchange_parts(pieces):
    parts = []
    for order, part in zip(PARTS, pieces):
        got = []
        for spot, k in enumerate(order):
            piece = part[spot]
            if k > 0:
                piece = lax.ppermute(piece, "seq", [(i, i ^ k) for i in range(8)])
            got.append(piece)
        parts.append(jnp.concatenate(got))
    return parts


def entering_state(got, init_rows):
    count, rows, width = got.shape
    part = rows - 16
    place = lax.axis_index("seq")
    start = lax.dynamic_slice_in_dim(init_rows, place * part, part, 0)
    vmem = pl.BlockSpec(memory_space=pltpu.VMEM)
    return pl.pallas_call(
        prefix_kernel,
        in_specs=[pl.BlockSpec(memory_space=pltpu.SMEM), vmem, vmem],
        out_shape=jax.ShapeDtypeStruct((count, part, width), BF),
        compiler_params=params(8),
        name="prefix",
    )(place.reshape(1), got, start)


def within_kernel(skip, x, step_t, cum_t, b, c, out):
    heads, toks = cum_t.shape
    row = lax.broadcasted_iota(jnp.int32, (toks, toks), 0)
    col = lax.broadcasted_iota(jnp.int32, (toks, toks), 1)
    causal = row >= col
    nt = (((1,), (1,)), ((), ()))
    scores = lax.dot_general(c[...], b[...], nt, preferred_element_type=F32)
    cum = cum_t[...].T
    for p in range(heads // 2):
        pair = x[:, p * LANES : (p + 1) * LANES]
        sums = []
        for h in (2 * p, 2 * p + 1):
            gap = cum[:, h : h + 1] - cum_t[h : h + 1, :]
            decay = jnp.where(causal, jnp.exp(jnp.where(causal, gap, 0.0)), 0.0)
            weights = (decay * scores * step_t[h : h + 1, :]).astype(BF)
            sums.append(jnp.dot(weights, pair, preferred_element_type=F32))
        gain = by_pair(skip[2 * p], skip[2 * p + 1], toks)
        out[:, p * LANES : (p + 1) * LANES] = (
            by_pair(sums[0], sums[1], toks) + gain * pair.astype(F32)
        )


def within_block(skip, x, step_t, cum_t, b, c):
    toks, inner = x.shape
    heads = cum_t.shape[0]
    vmem = pl.BlockSpec(memory_space=pltpu.VMEM)
    return pl.pallas_call(
        within_kernel,
        in_specs=[pl.BlockSpec(memory_space=pltpu.SMEM)] + [vmem] * 5,
        out_shape=jax.ShapeDtypeStruct((toks, inner), F32),
        compiler_params=params(8),
        cost_estimate=pl.CostEstimate(
            flops=4 * heads * toks * toks * LANES,
            bytes_accessed=6 * toks * inner,
            transcendentals=heads * toks * toks,
        ),
        name="within_block",
    )(skip, in_hbm(x), in_hbm(step_t), cum_t, in_hbm(b), in_hbm(c))


def fetch(sems, *pairs):
    copies = [pltpu.make_async_copy(src, dst, sems.at[i]) for i, (src, dst) in enumerate(pairs)]
    for copy in copies:
        copy.start()
    return copies


def cuts_of(ref, count):
    rows = ref.shape[0] // count
    return [ref.at[pl.ds(k * rows, rows)] for k in range(count)]


def quarters(place_ref, share):
    return [pl.ds(pl.multiple_of((place_ref[0] ^ k) * share, share), share) for k in range(4)]


def tail_kernel(
    place_ref, c_in, cum_in, gain_in, arriving_in, direct_in, z_in, weight_in, tokens_in,
    near, last, keep, passing,
    c, cum_t, gain, arriving, direct, z, weight, tokens, normed, sems,
):
    heads, toks = cum_t.shape
    share = near.shape[1]
    spots = quarters(place_ref, share)
    copies = fetch(
        sems,
        (cum_in, cum_t),
        (gain_in, gain),
        (c_in, c),
        (arriving_in, arriving),
        (z_in, z),
        (direct_in, direct),
        *zip(cuts_of(weight_in, 8), cuts_of(weight, 8)),
        (tokens_in.at[:, spots[0]], tokens),
    )
    for copy in copies[:6]:
        copy.wait()
    grown = jnp.exp(cum_t[...]).T
    lane = lax.broadcasted_iota(jnp.int32, (toks, LANES), 1)
    left = lane < LANES // 2
    nt = (((1,), (1,)), ((), ()))
    for p in range(heads // 2):
        spot = pl.ds(p * LANES, LANES)
        inter = lax.dot_general(c[...], arriving[spot, :], nt, preferred_element_type=F32)
        factor = by_pair(grown[:, 2 * p : 2 * p + 1], grown[:, 2 * p + 1 : 2 * p + 2], toks)
        wide = z[:, spot].astype(F32)
        gated = (direct[:, spot] + inter * factor) * (wide * (1.0 / (1.0 + jnp.exp(-wide))))
        square = gated * gated
        first = jnp.sum(jnp.where(left, square, 0.0), axis=1, keepdims=True)
        second = jnp.sum(jnp.where(left, 0.0, square), axis=1, keepdims=True)
        mean = by_pair(first, second, toks) * (2.0 / LANES)
        normed[:, spot] = (gated * lax.rsqrt(mean + 1e-05) * gain[:, spot]).astype(BF)
    for copy in copies[6:]:
        copy.wait()
    for k, out in ((3, last), (1, near), (2, passing), (0, keep)):
        part = jnp.dot(normed[...], weight[:, spots[k]], preferred_element_type=F32)
        if k == 0:
            part += tokens[...].astype(F32)
        out[...] = part.astype(out.dtype)


def mixer_tail(place, c, arriving, cum_t, direct, z, gain, weight, tokens):
    heads, toks = cum_t.shape
    inner, width = weight.shape
    share = width // 4
    operands = (c, cum_t, gain.reshape(1, inner), arriving, direct, z, weight, tokens)
    fixed = (0, 2, 5, 6, 7)
    operands = [in_hbm(a) if i in fixed else a for i, a in enumerate(operands)]
    return pl.pallas_call(
        tail_kernel,
        in_specs=[pl.BlockSpec(memory_space=pltpu.SMEM)]
        + [pl.BlockSpec(memory_space=pl.ANY)] * len(operands),
        out_shape=[jax.ShapeDtypeStruct((toks, share), kind) for kind in (BF, BF, F32, F32)],
        scratch_shapes=[pltpu.VMEM(a.shape, a.dtype) for a in operands[:-1]]
        + [
            pltpu.VMEM((toks, share), BF),
            pltpu.VMEM((toks, inner), BF),
            pltpu.SemaphoreType.DMA((15,)),
        ],
        compiler_params=params(12),
        cost_estimate=pl.CostEstimate(
            flops=2 * toks * inner * width,
            bytes_accessed=2 * inner * width + 14 * toks * inner,
            transcendentals=toks * inner,
        ),
        name="mixer_tail",
    )(place.reshape(1), *operands)


def expert_kernel(
    place_ref, gain_in, own_in, near_in, far_in, last_in, wg_in, wu_in, wd_in,
    near_out, last_out, keep_out, pass_out,
    gain, own, near, far, last, wg, wu, wd, rows, sems,
):
    count, share = own.shape
    width = 4 * share
    spots = quarters(place_ref, share)
    copies = fetch(
        sems,
        (gain_in, gain),
        (own_in, own),
        (near_in, near),
        (far_in, far),
        (last_in, last),
        *((w_in.at[s], w.at[s]) for s in spots for w_in, w in ((wg_in, wg), (wu_in, wu))),
        *zip(cuts_of(wd_in, 4), cuts_of(wd, 4)),
    )
    for copy in copies[:5]:
        copy.wait()

    @pl.loop(0, count, step=64)
    def _(start):
        spot = pl.ds(pl.multiple_of(start, 64), 64)
        wide = [p[spot, :].astype(F32) for p in (own, near, far, last)]
        square = sum(jnp.sum(w * w, axis=1, keepdims=True) for w in wide)
        scale = lax.rsqrt(square * (1.0 / width) + 1e-05)
        for k in range(4):
            rows[k, spot, :] = (wide[k] * scale * gain[:, spots[k]]).astype(BF)

    gate = up = 0.0
    for k in range(4):
        copies[5 + 2 * k].wait()
        gate += jnp.dot(rows[k], wg[spots[k], :], preferred_element_type=F32)
        copies[6 + 2 * k].wait()
        up += jnp.dot(rows[k], wu[spots[k], :], preferred_element_type=F32)
    act = (gate * (1.0 / (1.0 + jnp.exp(-gate))) * up).astype(BF)
    for copy in copies[13:]:
        copy.wait()
    for k, out in ((3, last_out), (1, near_out), (2, pass_out), (0, keep_out)):
        out[...] = jnp.dot(act, wd[:, spots[k]], preferred_element_type=F32).astype(BF)


def run_expert(place, gain, own, near, far, last, wg, wu, wd):
    rows, share = own.shape
    width, inner = wg.shape
    weights = (in_hbm(wg), in_hbm(wu), in_hbm(wd))
    operands = (in_hbm(gain.reshape(1, width)), own, near, far, last, *weights)
    return pl.pallas_call(
        expert_kernel,
        in_specs=[pl.BlockSpec(memory_space=pltpu.SMEM)]
        + [pl.BlockSpec(memory_space=pl.ANY)] * len(operands),
        out_shape=[jax.ShapeDtypeStruct((rows, share), BF)] * 4,
        scratch_shapes=[pltpu.VMEM(a.shape, a.dtype) for a in operands]
        + [
            pltpu.VMEM((4, rows, share), BF),
            pltpu.SemaphoreType.DMA((17,)),
        ],
        compiler_params=params(16),
        cost_estimate=pl.CostEstimate(flops=1, bytes_accessed=1, transcendentals=0),
        name="expert",
    )(place.reshape(1), *operands)


def body(
    tokens,
    input_heads,
    z_gate,
    b_proj,
    c_proj,
    step_size,
    decay_log,
    skip_gain,
    init_state,
    norm_gain,
    out_weight,
    moe_gain,
    routes,
    route_weights,
    w_gate,
    w_up,
    w_down,
):
    tok_rows, inner = input_heads.shape
    state_size = init_state.shape[2]
    seq_count = lax.axis_size("seq")
    place = lax.axis_index("tp")
    step_t = step_size.T
    outgoing, cum_t = own_state(input_heads, step_t, decay_log.T, b_proj, seq_count)
    got = exchange(outgoing)
    direct = within_block(skip_gain, input_heads, step_t, cum_t, b_proj, c_proj)
    back = entering_state(got, init_state.reshape(inner, state_size))
    arriving = exchange(back).reshape(inner, state_size)
    model_width = out_weight.shape[1]
    share = model_width // 4
    expert_count = w_gate.shape[0] * seq_count
    slot_count = 4 * tok_rows // seq_count
    top_count = routes.shape[1]
    items = top_count * tok_rows
    slots = expert_count * slot_count
    flat_expert = routes.T.reshape(-1)
    onehot = flat_expert[:, None] == jnp.arange(expert_count, dtype=jnp.int32)[None, :]
    before = jnp.arange(items)[:, None] > jnp.arange(items)[None, :]
    earlier = jnp.dot(before.astype(BF), onehot.astype(BF), preferred_element_type=F32)
    rank = jnp.sum(jnp.where(onehot, earlier, 0.0), axis=1).astype(jnp.int32)
    few = seq_count == 8
    layout = flat_expert
    if few:
        bits = flat_expert ^ lax.axis_index("seq")
        order = PARTS[0] + PARTS[1]
        layout = sum(jnp.where(bits == k, spot, 0) for spot, k in enumerate(order))
    placed = layout * slot_count + rank
    spots = placed[:, None] == jnp.arange(slots, dtype=jnp.int32)[None, :]
    spots = spots.reshape(top_count, tok_rows, slots)
    fill = jnp.any(spots, axis=0).astype(BF)
    combine = jnp.sum(jnp.where(spots, route_weights.T[:, :, None], 0.0), axis=0)
    direct = after(direct, fill, combine)

    to_near, to_last, keep, passing = mixer_tail(
        place, c_proj, arriving, cum_t, direct, z_gate, norm_gain, out_weight, tokens
    )

    from_last = swap(to_last, 1)
    from_near = swap(to_near, 1)
    from_far = swap((passing + from_last.astype(F32)).astype(BF), 2)
    hidden = (keep + from_near.astype(F32) + from_far.astype(F32)).astype(BF)

    outgoing = lax.dot_general(
        fill, hidden, (((0,), (0,)), ((), ())), preferred_element_type=F32
    ).astype(BF)
    outgoing = outgoing.reshape(expert_count, slot_count, share)

    middle = len(PARTS[0]) if few else expert_count // 2
    cut = middle * slot_count
    if few:
        own = exchange_parts((outgoing[:middle], outgoing[middle:]))
    else:
        arrived = exchange(outgoing).reshape(slots, share)
        own = [arrived[:cut], arrived[cut:]]
    far = [swap(part, 2) for part in own]
    near = [swap(part, 1) for part in own]
    weights = (w_gate[0], w_up[0], w_down[0])
    last = swap(far[0], 1)
    to_near0, to_last0, keep0, pass0 = run_expert(
        place, moe_gain, own[0], near[0], far[0], last, *weights
    )
    from_last0 = swap(to_last0, 1)
    last = swap(after(far[1], to_last0), 1)
    pass0 = (pass0.astype(F32) + from_last0.astype(F32)).astype(BF)
    from_far0 = swap(pass0, 2)
    to_near1, to_last1, keep1, pass1 = run_expert(
        place, moe_gain, after(own[1], pass0), near[1], far[1], last, *weights
    )
    from_last1 = swap(to_last1, 1)
    from_near0 = swap(after(to_near0, from_far0), 1)
    pass1 = (pass1.astype(F32) + from_last1.astype(F32)).astype(BF)
    from_far1 = swap(pass1, 2)
    from_near1 = swap(after(to_near1, pass1), 1)
    results = [
        (keep.astype(F32) + from_near.astype(F32) + from_far.astype(F32)).astype(BF)
        for keep, from_near, from_far in (
            (keep0, from_near0, from_far0),
            (keep1, from_near1, from_far1),
        )
    ]
    if few:
        results = [part.reshape(-1, slot_count, share) for part in results]
        returned = jnp.concatenate(exchange_parts(results))
    else:
        results = jnp.concatenate(results).reshape(expert_count, slot_count, share)
        returned = exchange(results).reshape(slots, share)
    mixed = hidden.astype(F32) + jnp.dot(
        combine,
        returned.astype(F32),
        precision=lax.Precision.HIGHEST,
        preferred_element_type=F32,
    )
    return mixed.astype(BF)


def solution(mesh):
    in_specs = (
        P("seq", None),
        P("seq", "tp"),
        P("seq", "tp"),
        P("seq", None),
        P("seq", None),
        P("seq", "tp"),
        P("seq", "tp"),
        P("tp"),
        P("tp", None, None),
        P("tp"),
        P("tp", None),
        P(),
        P("seq", None),
        P("seq", None),
        P("seq", None, "tp"),
        P("seq", None, "tp"),
        P("seq", "tp", None),
    )
    out_specs = P("seq", "tp")
    return jax.shard_map(body, mesh=mesh, in_specs=in_specs, out_specs=out_specs, check_vma=False)
```

```python
import jax
import jax.numpy as jnp
from jax import lax
from jax.experimental import pallas as pl
from jax.experimental.pallas import tpu as pltpu
from jax.sharding import PartitionSpec as P

BF = jnp.bfloat16
F32 = jnp.float32
MIB = 1024 * 1024
LANES = 128


def swap(value, bit):
    count = lax.axis_size("tp")
    return lax.ppermute(value, "tp", [(i, i ^ bit) for i in range(count)])


def exchange(value):
    return lax.all_to_all(value, "seq", split_axis=0, concat_axis=0, tiled=True)


def after(value, *others):
    return lax.optimization_barrier((value, *others))[0]


def in_hbm(value):
    return pltpu.with_memory_space_constraint(value, pltpu.HBM)


def params(mib):
    return pltpu.CompilerParams(vmem_limit_bytes=mib * MIB)


def whole(*shape):
    return pl.BlockSpec(shape, lambda *_: (0,) * len(shape))


def by_pair(left, right, size):
    lane = lax.broadcasted_iota(jnp.int32, (size, LANES), 1)
    return jnp.where(lane < LANES // 2, left, right)


def state_kernel(x, step_t, decay_t, b, out, cum_out):
    count, rows, _ = out.shape
    part = rows - 16
    heads, toks = decay_t.shape
    row = lax.broadcasted_iota(jnp.int32, (toks, toks), 0)
    col = lax.broadcasted_iota(jnp.int32, (toks, toks), 1)
    upper = (row <= col).astype(F32)
    cum_t = jnp.dot(
        decay_t[...], upper, precision=lax.Precision.HIGHEST, preferred_element_type=F32
    )
    cum_out[...] = cum_t
    end = cum_t[:, toks - 1 : toks]
    scale = (jnp.exp(end - cum_t) * step_t[...]).T
    decay = jnp.broadcast_to(jnp.exp(end), (heads, LANES))
    high = decay.astype(BF).astype(F32)
    extra = by_pair(high, decay - high, heads).astype(BF)
    for k in range(count):
        out[k, pl.ds(part, 16), :] = extra
    for p in range(heads // 2):
        pair = x[:, p * LANES : (p + 1) * LANES].astype(F32)
        factor = by_pair(scale[:, 2 * p : 2 * p + 1], scale[:, 2 * p + 1 : 2 * p + 2], toks)
        state = lax.dot_general(
            (pair * factor).astype(BF),
            b[...],
            (((0,), (0,)), ((), ())),
            preferred_element_type=F32,
        ).astype(BF)
        for k in range(LANES // part):
            out[p * (LANES // part) + k, pl.ds(0, part), :] = state[k * part : (k + 1) * part]


def own_state(x, step_t, decay_t, b, count):
    heads, toks = decay_t.shape
    part = x.shape[1] // count
    return pl.pallas_call(
        state_kernel,
        out_shape=[
            jax.ShapeDtypeStruct((count, part + 16, b.shape[1]), BF),
            jax.ShapeDtypeStruct((heads, toks), F32),
        ],
        compiler_params=params(8),
        name="own_state",
    )(in_hbm(x), in_hbm(step_t), in_hbm(decay_t), in_hbm(b))


def prefix_kernel(place_ref, got, start, back):
    count, part, _ = back.shape
    heads = 16
    held = max(1, heads // count)
    group = part // held
    first = place_ref[0] * heads // count
    row = lax.broadcasted_iota(jnp.int32, (heads, LANES), 0)
    carries = [start[pl.ds(h * group, group), :] for h in range(held)]
    for turn in range(count):
        extra = got[turn, pl.ds(part, 16), :].astype(F32)
        scale = extra[:, :1] + extra[:, LANES // 2 : LANES // 2 + 1]
        for h in range(held):
            spot = pl.ds(h * group, group)
            back[turn, spot, :] = carries[h].astype(BF)
            factor = jnp.sum(jnp.where(row == first + h, scale, 0.0), axis=0, keepdims=True)
            carries[h] = factor * carries[h] + got[turn, spot, :].astype(F32)


PARTS = ((0, 1, 4, 5), (6, 7, 2, 3))


def exchange_parts(pieces, early=False):
    parts = []
    for order, part in zip(PARTS, pieces):
        got = []
        for spot, k in enumerate(order):
            piece = part[spot]
            if k > 0:
                piece = lax.ppermute(piece, "seq", [(i, i ^ k) for i in range(8)])
            got.append(piece)
        parts.append(got)
    if early:
        parts[0][0] = after(parts[0][0], parts[1][0])
    return [jnp.concatenate(got) for got in parts]


def entering_state(got, init_rows):
    count, rows, width = got.shape
    part = rows - 16
    place = lax.axis_index("seq")
    start = lax.dynamic_slice_in_dim(init_rows, place * part, part, 0)
    vmem = pl.BlockSpec(memory_space=pltpu.VMEM)
    return pl.pallas_call(
        prefix_kernel,
        in_specs=[pl.BlockSpec(memory_space=pltpu.SMEM), vmem, vmem],
        out_shape=jax.ShapeDtypeStruct((count, part, width), BF),
        compiler_params=params(8),
        name="prefix",
    )(place.reshape(1), got, start)


def within_kernel(skip, x, step_t, cum_t, b, c, out):
    heads, toks = cum_t.shape
    row = lax.broadcasted_iota(jnp.int32, (toks, toks), 0)
    col = lax.broadcasted_iota(jnp.int32, (toks, toks), 1)
    causal = row >= col
    nt = (((1,), (1,)), ((), ()))
    scores = lax.dot_general(c[...], b[...], nt, preferred_element_type=F32)
    cum = cum_t[...].T
    for p in range(heads // 2):
        pair = x[:, p * LANES : (p + 1) * LANES]
        sums = []
        for h in (2 * p, 2 * p + 1):
            gap = cum[:, h : h + 1] - cum_t[h : h + 1, :]
            decay = jnp.where(causal, jnp.exp(jnp.where(causal, gap, 0.0)), 0.0)
            weights = (decay * scores * step_t[h : h + 1, :]).astype(BF)
            sums.append(jnp.dot(weights, pair, preferred_element_type=F32))
        gain = by_pair(skip[2 * p], skip[2 * p + 1], toks)
        out[:, p * LANES : (p + 1) * LANES] = (
            by_pair(sums[0], sums[1], toks) + gain * pair.astype(F32)
        )


def within_block(skip, x, step_t, cum_t, b, c):
    toks, inner = x.shape
    heads = cum_t.shape[0]
    vmem = pl.BlockSpec(memory_space=pltpu.VMEM)
    return pl.pallas_call(
        within_kernel,
        in_specs=[pl.BlockSpec(memory_space=pltpu.SMEM)] + [vmem] * 5,
        out_shape=jax.ShapeDtypeStruct((toks, inner), F32),
        compiler_params=params(8),
        cost_estimate=pl.CostEstimate(
            flops=4 * heads * toks * toks * LANES,
            bytes_accessed=6 * toks * inner,
            transcendentals=heads * toks * toks,
        ),
        name="within_block",
    )(skip, in_hbm(x), in_hbm(step_t), cum_t, in_hbm(b), in_hbm(c))


def fetch(sems, *pairs):
    copies = [pltpu.make_async_copy(src, dst, sems.at[i]) for i, (src, dst) in enumerate(pairs)]
    for copy in copies:
        copy.start()
    return copies


def cuts_of(ref, count):
    rows = ref.shape[0] // count
    return [ref.at[pl.ds(k * rows, rows)] for k in range(count)]


def quarters(place_ref, share):
    return [pl.ds(pl.multiple_of((place_ref[0] ^ k) * share, share), share) for k in range(4)]


def tail_kernel(
    place_ref, c_in, cum_in, gain_in, arriving_in, direct_in, z_in, weight_in, tokens_in,
    near, last, keep, passing,
    c, cum_t, gain, arriving, direct, z, weight, tokens, normed, sems,
):
    heads, toks = cum_t.shape
    share = near.shape[1]
    spots = quarters(place_ref, share)
    copies = fetch(
        sems,
        (cum_in, cum_t),
        (gain_in, gain),
        (c_in, c),
        (arriving_in, arriving),
        (z_in, z),
        (direct_in, direct),
        *zip(cuts_of(weight_in, 8), cuts_of(weight, 8)),
        (tokens_in.at[:, spots[0]], tokens),
    )
    for copy in copies[:6]:
        copy.wait()
    grown = jnp.exp(cum_t[...]).T
    lane = lax.broadcasted_iota(jnp.int32, (toks, LANES), 1)
    left = lane < LANES // 2
    nt = (((1,), (1,)), ((), ()))
    for p in range(heads // 2):
        spot = pl.ds(p * LANES, LANES)
        inter = lax.dot_general(c[...], arriving[spot, :], nt, preferred_element_type=F32)
        factor = by_pair(grown[:, 2 * p : 2 * p + 1], grown[:, 2 * p + 1 : 2 * p + 2], toks)
        wide = z[:, spot].astype(F32)
        gated = (direct[:, spot] + inter * factor) * (wide * (1.0 / (1.0 + jnp.exp(-wide))))
        square = gated * gated
        first = jnp.sum(jnp.where(left, square, 0.0), axis=1, keepdims=True)
        second = jnp.sum(jnp.where(left, 0.0, square), axis=1, keepdims=True)
        mean = by_pair(first, second, toks) * (2.0 / LANES)
        normed[:, spot] = (gated * lax.rsqrt(mean + 1e-05) * gain[:, spot]).astype(BF)
    for copy in copies[6:]:
        copy.wait()
    for k, out in ((3, last), (1, near), (2, passing), (0, keep)):
        part = jnp.dot(normed[...], weight[:, spots[k]], preferred_element_type=F32)
        if k == 0:
            part += tokens[...].astype(F32)
        out[...] = part.astype(out.dtype)


def mixer_tail(place, c, arriving, cum_t, direct, z, gain, weight, tokens):
    heads, toks = cum_t.shape
    inner, width = weight.shape
    share = width // 4
    operands = (c, cum_t, gain.reshape(1, inner), arriving, direct, z, weight, tokens)
    fixed = (0, 2, 5, 6, 7)
    operands = [in_hbm(a) if i in fixed else a for i, a in enumerate(operands)]
    return pl.pallas_call(
        tail_kernel,
        in_specs=[pl.BlockSpec(memory_space=pltpu.SMEM)]
        + [pl.BlockSpec(memory_space=pl.ANY)] * len(operands),
        out_shape=[jax.ShapeDtypeStruct((toks, share), kind) for kind in (BF, BF, F32, F32)],
        scratch_shapes=[pltpu.VMEM(a.shape, a.dtype) for a in operands[:-1]]
        + [
            pltpu.VMEM((toks, share), BF),
            pltpu.VMEM((toks, inner), BF),
            pltpu.SemaphoreType.DMA((15,)),
        ],
        compiler_params=params(12),
        cost_estimate=pl.CostEstimate(
            flops=2 * toks * inner * width,
            bytes_accessed=2 * inner * width + 14 * toks * inner,
            transcendentals=toks * inner,
        ),
        name="mixer_tail",
    )(place.reshape(1), *operands)


def expert_kernel(
    place_ref, gain_in, own_in, near_in, far_in, last_in, wg_in, wu_in, wd_in,
    near_out, last_out, keep_out, pass_out,
    gain, own, near, far, last, wg, wu, wd, rows, sems,
):
    count, share = own.shape
    width = 4 * share
    spots = quarters(place_ref, share)
    copies = fetch(
        sems,
        (gain_in, gain),
        (own_in, own),
        (near_in, near),
        (far_in, far),
        (last_in, last),
        *((w_in.at[s], w.at[s]) for s in spots for w_in, w in ((wg_in, wg), (wu_in, wu))),
        *zip(cuts_of(wd_in, 4), cuts_of(wd, 4)),
    )
    for copy in copies[:5]:
        copy.wait()

    @pl.loop(0, count, step=64)
    def _(start):
        spot = pl.ds(pl.multiple_of(start, 64), 64)
        wide = [p[spot, :].astype(F32) for p in (own, near, far, last)]
        square = sum(jnp.sum(w * w, axis=1, keepdims=True) for w in wide)
        scale = lax.rsqrt(square * (1.0 / width) + 1e-05)
        for k in range(4):
            rows[k, spot, :] = (wide[k] * scale * gain[:, spots[k]]).astype(BF)

    gate = up = 0.0
    for k in range(4):
        copies[5 + 2 * k].wait()
        gate += jnp.dot(rows[k], wg[spots[k], :], preferred_element_type=F32)
        copies[6 + 2 * k].wait()
        up += jnp.dot(rows[k], wu[spots[k], :], preferred_element_type=F32)
    act = (gate * (1.0 / (1.0 + jnp.exp(-gate))) * up).astype(BF)
    for copy in copies[13:]:
        copy.wait()
    for k, out in ((3, last_out), (1, near_out), (2, pass_out), (0, keep_out)):
        out[...] = jnp.dot(act, wd[:, spots[k]], preferred_element_type=F32).astype(BF)


def run_expert(place, gain, own, near, far, last, wg, wu, wd):
    rows, share = own.shape
    width, inner = wg.shape
    weights = (in_hbm(wg), in_hbm(wu), in_hbm(wd))
    operands = (in_hbm(gain.reshape(1, width)), own, near, far, last, *weights)
    return pl.pallas_call(
        expert_kernel,
        in_specs=[pl.BlockSpec(memory_space=pltpu.SMEM)]
        + [pl.BlockSpec(memory_space=pl.ANY)] * len(operands),
        out_shape=[jax.ShapeDtypeStruct((rows, share), BF)] * 4,
        scratch_shapes=[pltpu.VMEM(a.shape, a.dtype) for a in operands]
        + [
            pltpu.VMEM((4, rows, share), BF),
            pltpu.SemaphoreType.DMA((17,)),
        ],
        compiler_params=params(16),
        cost_estimate=pl.CostEstimate(flops=1, bytes_accessed=1, transcendentals=0),
        name="expert",
    )(place.reshape(1), *operands)


def body(
    tokens,
    input_heads,
    z_gate,
    b_proj,
    c_proj,
    step_size,
    decay_log,
    skip_gain,
    init_state,
    norm_gain,
    out_weight,
    moe_gain,
    routes,
    route_weights,
    w_gate,
    w_up,
    w_down,
):
    tok_rows, inner = input_heads.shape
    state_size = init_state.shape[2]
    seq_count = lax.axis_size("seq")
    place = lax.axis_index("tp")
    step_t = step_size.T
    outgoing, cum_t = own_state(input_heads, step_t, decay_log.T, b_proj, seq_count)
    got = exchange(outgoing)
    direct = within_block(skip_gain, input_heads, step_t, cum_t, b_proj, c_proj)
    back = entering_state(got, init_state.reshape(inner, state_size))
    arriving = exchange(back).reshape(inner, state_size)
    model_width = out_weight.shape[1]
    share = model_width // 4
    expert_count = w_gate.shape[0] * seq_count
    slot_count = 4 * tok_rows // seq_count
    top_count = routes.shape[1]
    items = top_count * tok_rows
    slots = expert_count * slot_count
    flat_expert = routes.T.reshape(-1)
    onehot = flat_expert[:, None] == jnp.arange(expert_count, dtype=jnp.int32)[None, :]
    before = jnp.arange(items)[:, None] > jnp.arange(items)[None, :]
    earlier = jnp.dot(before.astype(BF), onehot.astype(BF), preferred_element_type=F32)
    rank = jnp.sum(jnp.where(onehot, earlier, 0.0), axis=1).astype(jnp.int32)
    few = seq_count == 8
    layout = flat_expert
    if few:
        bits = flat_expert ^ lax.axis_index("seq")
        order = PARTS[0] + PARTS[1]
        layout = sum(jnp.where(bits == k, spot, 0) for spot, k in enumerate(order))
    placed = layout * slot_count + rank
    spots = placed[:, None] == jnp.arange(slots, dtype=jnp.int32)[None, :]
    spots = spots.reshape(top_count, tok_rows, slots)
    fill = jnp.any(spots, axis=0).astype(BF)
    combine = jnp.sum(jnp.where(spots, route_weights.T[:, :, None], 0.0), axis=0)
    direct = after(direct, fill, combine)

    to_near, to_last, keep, passing = mixer_tail(
        place, c_proj, arriving, cum_t, direct, z_gate, norm_gain, out_weight, tokens
    )

    from_last = swap(to_last, 1)
    from_near = swap(to_near, 1)
    from_far = swap((passing + from_last.astype(F32)).astype(BF), 2)
    hidden = (keep + from_near.astype(F32) + from_far.astype(F32)).astype(BF)

    outgoing = lax.dot_general(
        fill, hidden, (((0,), (0,)), ((), ())), preferred_element_type=F32
    ).astype(BF)
    outgoing = outgoing.reshape(expert_count, slot_count, share)

    middle = len(PARTS[0]) if few else expert_count // 2
    cut = middle * slot_count
    if few:
        own = exchange_parts((outgoing[:middle], outgoing[middle:]), early=True)
    else:
        arrived = exchange(outgoing).reshape(slots, share)
        own = [arrived[:cut], arrived[cut:]]
    far = [swap(part, 2) for part in own]
    near = [swap(part, 1) for part in own]
    weights = (w_gate[0], w_up[0], w_down[0])
    last = swap(far[0], 1)
    to_near0, to_last0, keep0, pass0 = run_expert(
        place, moe_gain, own[0], near[0], far[0], last, *weights
    )
    from_last0 = swap(to_last0, 1)
    last = swap(after(far[1], to_last0), 1)
    pass0 = (pass0.astype(F32) + from_last0.astype(F32)).astype(BF)
    from_far0 = swap(pass0, 2)
    to_near1, to_last1, keep1, pass1 = run_expert(
        place, moe_gain, after(own[1], pass0), near[1], far[1], last, *weights
    )
    from_last1 = swap(to_last1, 1)
    from_near0 = swap(after(to_near0, from_far0), 1)
    pass1 = (pass1.astype(F32) + from_last1.astype(F32)).astype(BF)
    from_far1 = swap(pass1, 2)
    from_near1 = swap(after(to_near1, pass1), 1)
    results = [
        (keep.astype(F32) + from_near.astype(F32) + from_far.astype(F32)).astype(BF)
        for keep, from_near, from_far in (
            (keep0, from_near0, from_far0),
            (keep1, from_near1, from_far1),
        )
    ]
    if few:
        results = [part.reshape(-1, slot_count, share) for part in results]
        returned = jnp.concatenate(exchange_parts(results))
    else:
        results = jnp.concatenate(results).reshape(expert_count, slot_count, share)
        returned = exchange(results).reshape(slots, share)
    mixed = hidden.astype(F32) + jnp.dot(
        combine,
        returned.astype(F32),
        precision=lax.Precision.HIGHEST,
        preferred_element_type=F32,
    )
    return mixed.astype(BF)


def solution(mesh):
    in_specs = (
        P("seq", None),
        P("seq", "tp"),
        P("seq", "tp"),
        P("seq", None),
        P("seq", None),
        P("seq", "tp"),
        P("seq", "tp"),
        P("tp"),
        P("tp", None, None),
        P("tp"),
        P("tp", None),
        P(),
        P("seq", None),
        P("seq", None),
        P("seq", None, "tp"),
        P("seq", None, "tp"),
        P("seq", "tp", None),
    )
    out_specs = P("seq", "tp")
    return jax.shard_map(body, mesh=mesh, in_specs=in_specs, out_specs=out_specs, check_vma=False)
```

```python
import jax
import jax.numpy as jnp
from jax import lax
from jax.experimental import pallas as pl
from jax.experimental.pallas import tpu as pltpu
from jax.sharding import PartitionSpec as P

BF = jnp.bfloat16
F32 = jnp.float32
MIB = 1024 * 1024
LANES = 128


def swap(value, bit):
    count = lax.axis_size("tp")
    return lax.ppermute(value, "tp", [(i, i ^ bit) for i in range(count)])


def exchange(value):
    return lax.all_to_all(value, "seq", split_axis=0, concat_axis=0, tiled=True)


def after(value, *others):
    return lax.optimization_barrier((value, *others))[0]


def in_hbm(value):
    return pltpu.with_memory_space_constraint(value, pltpu.HBM)


def params(mib):
    return pltpu.CompilerParams(vmem_limit_bytes=mib * MIB)


def whole(*shape):
    return pl.BlockSpec(shape, lambda *_: (0,) * len(shape))


def by_pair(left, right, size):
    lane = lax.broadcasted_iota(jnp.int32, (size, LANES), 1)
    return jnp.where(lane < LANES // 2, left, right)


def state_kernel(x, step_t, decay_t, b, out, cum_out):
    count, rows, _ = out.shape
    part = rows - 16
    heads, toks = decay_t.shape
    row = lax.broadcasted_iota(jnp.int32, (toks, toks), 0)
    col = lax.broadcasted_iota(jnp.int32, (toks, toks), 1)
    upper = (row <= col).astype(F32)
    cum_t = jnp.dot(
        decay_t[...], upper, precision=lax.Precision.HIGHEST, preferred_element_type=F32
    )
    cum_out[...] = cum_t
    end = cum_t[:, toks - 1 : toks]
    scale = (jnp.exp(end - cum_t) * step_t[...]).T
    decay = jnp.broadcast_to(jnp.exp(end), (heads, LANES))
    high = decay.astype(BF).astype(F32)
    extra = by_pair(high, decay - high, heads).astype(BF)
    for k in range(count):
        out[k, pl.ds(part, 16), :] = extra
    for p in range(heads // 2):
        pair = x[:, p * LANES : (p + 1) * LANES].astype(F32)
        factor = by_pair(scale[:, 2 * p : 2 * p + 1], scale[:, 2 * p + 1 : 2 * p + 2], toks)
        state = lax.dot_general(
            (pair * factor).astype(BF),
            b[...],
            (((0,), (0,)), ((), ())),
            preferred_element_type=F32,
        ).astype(BF)
        for k in range(LANES // part):
            out[p * (LANES // part) + k, pl.ds(0, part), :] = state[k * part : (k + 1) * part]


def own_state(x, step_t, decay_t, b, count):
    heads, toks = decay_t.shape
    part = x.shape[1] // count
    return pl.pallas_call(
        state_kernel,
        out_shape=[
            jax.ShapeDtypeStruct((count, part + 16, b.shape[1]), BF),
            jax.ShapeDtypeStruct((heads, toks), F32),
        ],
        compiler_params=params(8),
        name="own_state",
    )(in_hbm(x), in_hbm(step_t), in_hbm(decay_t), in_hbm(b))


def prefix_kernel(place_ref, got, start, back):
    count, part, _ = back.shape
    heads = 16
    held = max(1, heads // count)
    group = part // held
    first = place_ref[0] * heads // count
    row = lax.broadcasted_iota(jnp.int32, (heads, LANES), 0)
    carries = [start[pl.ds(h * group, group), :] for h in range(held)]
    for turn in range(count):
        extra = got[turn, pl.ds(part, 16), :].astype(F32)
        scale = extra[:, :1] + extra[:, LANES // 2 : LANES // 2 + 1]
        for h in range(held):
            spot = pl.ds(h * group, group)
            back[turn, spot, :] = carries[h].astype(BF)
            factor = jnp.sum(jnp.where(row == first + h, scale, 0.0), axis=0, keepdims=True)
            carries[h] = factor * carries[h] + got[turn, spot, :].astype(F32)


PARTS = ((0, 1, 4, 5), (6, 7, 2, 3))


def exchange_parts(pieces, early=False):
    parts = []
    for order, part in zip(PARTS, pieces):
        got = []
        for spot, k in enumerate(order):
            piece = part[spot]
            if k > 0:
                piece = lax.ppermute(piece, "seq", [(i, i ^ k) for i in range(8)])
            got.append(piece)
        parts.append(got)
    if early:
        parts[0][0] = after(parts[0][0], parts[1][0])
    return [jnp.concatenate(got) for got in parts]


def entering_state(got, init_rows):
    count, rows, width = got.shape
    part = rows - 16
    place = lax.axis_index("seq")
    start = lax.dynamic_slice_in_dim(init_rows, place * part, part, 0)
    vmem = pl.BlockSpec(memory_space=pltpu.VMEM)
    return pl.pallas_call(
        prefix_kernel,
        in_specs=[pl.BlockSpec(memory_space=pltpu.SMEM), vmem, vmem],
        out_shape=jax.ShapeDtypeStruct((count, part, width), BF),
        compiler_params=params(8),
        name="prefix",
    )(place.reshape(1), got, start)


def within_kernel(skip, x, step_t, cum_t, b, c, out):
    heads, toks = cum_t.shape
    row = lax.broadcasted_iota(jnp.int32, (toks, toks), 0)
    col = lax.broadcasted_iota(jnp.int32, (toks, toks), 1)
    causal = row >= col
    nt = (((1,), (1,)), ((), ()))
    scores = lax.dot_general(c[...], b[...], nt, preferred_element_type=F32)
    cum = cum_t[...].T
    for p in range(heads // 2):
        pair = x[:, p * LANES : (p + 1) * LANES]
        sums = []
        for h in (2 * p, 2 * p + 1):
            gap = cum[:, h : h + 1] - cum_t[h : h + 1, :]
            decay = jnp.where(causal, jnp.exp(jnp.where(causal, gap, 0.0)), 0.0)
            weights = (decay * scores * step_t[h : h + 1, :]).astype(BF)
            sums.append(jnp.dot(weights, pair, preferred_element_type=F32))
        gain = by_pair(skip[2 * p], skip[2 * p + 1], toks)
        out[:, p * LANES : (p + 1) * LANES] = (
            by_pair(sums[0], sums[1], toks) + gain * pair.astype(F32)
        )


def within_block(skip, x, step_t, cum_t, b, c):
    toks, inner = x.shape
    heads = cum_t.shape[0]
    vmem = pl.BlockSpec(memory_space=pltpu.VMEM)
    return pl.pallas_call(
        within_kernel,
        in_specs=[pl.BlockSpec(memory_space=pltpu.SMEM)] + [vmem] * 5,
        out_shape=jax.ShapeDtypeStruct((toks, inner), F32),
        compiler_params=params(8),
        cost_estimate=pl.CostEstimate(
            flops=4 * heads * toks * toks * LANES,
            bytes_accessed=6 * toks * inner,
            transcendentals=heads * toks * toks,
        ),
        name="within_block",
    )(skip, in_hbm(x), in_hbm(step_t), cum_t, in_hbm(b), in_hbm(c))


def fetch(sems, *pairs):
    copies = [pltpu.make_async_copy(src, dst, sems.at[i]) for i, (src, dst) in enumerate(pairs)]
    for copy in copies:
        copy.start()
    return copies


def cuts_of(ref, count):
    rows = ref.shape[0] // count
    return [ref.at[pl.ds(k * rows, rows)] for k in range(count)]


def quarters(place_ref, share):
    return [pl.ds(pl.multiple_of((place_ref[0] ^ k) * share, share), share) for k in range(4)]


def tail_kernel(
    place_ref, c_in, cum_in, gain_in, arriving_in, direct_in, z_in, weight_in, tokens_in,
    near, last, keep, passing,
    c, cum_t, gain, arriving, direct, z, weight, tokens, normed, sems,
):
    heads, toks = cum_t.shape
    share = near.shape[1]
    spots = quarters(place_ref, share)
    copies = fetch(
        sems,
        (cum_in, cum_t),
        (gain_in, gain),
        (c_in, c),
        (arriving_in, arriving),
        (z_in, z),
        (direct_in, direct),
        *zip(cuts_of(weight_in, 8), cuts_of(weight, 8)),
        (tokens_in.at[:, spots[0]], tokens),
    )
    for copy in copies[:6]:
        copy.wait()
    grown = jnp.exp(cum_t[...]).T
    lane = lax.broadcasted_iota(jnp.int32, (toks, LANES), 1)
    left = lane < LANES // 2
    nt = (((1,), (1,)), ((), ()))
    for p in range(heads // 2):
        spot = pl.ds(p * LANES, LANES)
        inter = lax.dot_general(c[...], arriving[spot, :], nt, preferred_element_type=F32)
        factor = by_pair(grown[:, 2 * p : 2 * p + 1], grown[:, 2 * p + 1 : 2 * p + 2], toks)
        wide = z[:, spot].astype(F32)
        gated = (direct[:, spot] + inter * factor) * (wide * (1.0 / (1.0 + jnp.exp(-wide))))
        square = gated * gated
        first = jnp.sum(jnp.where(left, square, 0.0), axis=1, keepdims=True)
        second = jnp.sum(jnp.where(left, 0.0, square), axis=1, keepdims=True)
        mean = by_pair(first, second, toks) * (2.0 / LANES)
        normed[:, spot] = (gated * lax.rsqrt(mean + 1e-05) * gain[:, spot]).astype(BF)
    for copy in copies[6:]:
        copy.wait()
    for k, out in ((3, last), (1, near), (2, passing), (0, keep)):
        part = jnp.dot(normed[...], weight[:, spots[k]], preferred_element_type=F32)
        if k == 0:
            part += tokens[...].astype(F32)
        out[...] = part.astype(out.dtype)


def mixer_tail(place, c, arriving, cum_t, direct, z, gain, weight, tokens):
    heads, toks = cum_t.shape
    inner, width = weight.shape
    share = width // 4
    operands = (c, cum_t, gain.reshape(1, inner), arriving, direct, z, weight, tokens)
    fixed = (0, 2, 5, 6, 7)
    operands = [in_hbm(a) if i in fixed else a for i, a in enumerate(operands)]
    return pl.pallas_call(
        tail_kernel,
        in_specs=[pl.BlockSpec(memory_space=pltpu.SMEM)]
        + [pl.BlockSpec(memory_space=pl.ANY)] * len(operands),
        out_shape=[jax.ShapeDtypeStruct((toks, share), kind) for kind in (BF, BF, F32, F32)],
        scratch_shapes=[pltpu.VMEM(a.shape, a.dtype) for a in operands[:-1]]
        + [
            pltpu.VMEM((toks, share), BF),
            pltpu.VMEM((toks, inner), BF),
            pltpu.SemaphoreType.DMA((15,)),
        ],
        compiler_params=params(12),
        cost_estimate=pl.CostEstimate(
            flops=2 * toks * inner * width,
            bytes_accessed=2 * inner * width + 14 * toks * inner,
            transcendentals=toks * inner,
        ),
        name="mixer_tail",
    )(place.reshape(1), *operands)


def expert_kernel(
    place_ref, gain_in, own_in, near_in, far_in, last_in, wg_in, wu_in, wd_in,
    near_out, last_out, keep_out, pass_out,
    gain, own, near, far, last, wg, wu, wd, rows, sems,
):
    count, share = own.shape
    width = 4 * share
    spots = quarters(place_ref, share)
    copies = fetch(
        sems,
        (gain_in, gain),
        (own_in, own),
        (near_in, near),
        (far_in, far),
        (last_in, last),
        *((w_in.at[s], w.at[s]) for s in spots for w_in, w in ((wg_in, wg), (wu_in, wu))),
        *zip(cuts_of(wd_in, 4), cuts_of(wd, 4)),
    )
    for copy in copies[:5]:
        copy.wait()

    @pl.loop(0, count, step=64)
    def _(start):
        spot = pl.ds(pl.multiple_of(start, 64), 64)
        wide = [p[spot, :].astype(F32) for p in (own, near, far, last)]
        square = sum(jnp.sum(w * w, axis=1, keepdims=True) for w in wide)
        scale = lax.rsqrt(square * (1.0 / width) + 1e-05)
        for k in range(4):
            rows[k, spot, :] = (wide[k] * scale * gain[:, spots[k]]).astype(BF)

    gate = up = 0.0
    for k in range(4):
        copies[5 + 2 * k].wait()
        gate += jnp.dot(rows[k], wg[spots[k], :], preferred_element_type=F32)
        copies[6 + 2 * k].wait()
        up += jnp.dot(rows[k], wu[spots[k], :], preferred_element_type=F32)
    act = (gate * (1.0 / (1.0 + jnp.exp(-gate))) * up).astype(BF)
    for copy in copies[13:]:
        copy.wait()
    for k, out in ((3, last_out), (1, near_out), (2, pass_out), (0, keep_out)):
        out[...] = jnp.dot(act, wd[:, spots[k]], preferred_element_type=F32).astype(BF)


def run_expert(place, gain, own, near, far, last, wg, wu, wd):
    rows, share = own.shape
    width, inner = wg.shape
    weights = (wg, wu, wd)
    operands = (in_hbm(gain.reshape(1, width)), own, near, far, last, *weights)
    return pl.pallas_call(
        expert_kernel,
        in_specs=[pl.BlockSpec(memory_space=pltpu.SMEM)]
        + [pl.BlockSpec(memory_space=pl.ANY)] * len(operands),
        out_shape=[jax.ShapeDtypeStruct((rows, share), BF)] * 4,
        scratch_shapes=[pltpu.VMEM(a.shape, a.dtype) for a in operands]
        + [
            pltpu.VMEM((4, rows, share), BF),
            pltpu.SemaphoreType.DMA((17,)),
        ],
        compiler_params=params(16),
        cost_estimate=pl.CostEstimate(flops=1, bytes_accessed=1, transcendentals=0),
        name="expert",
    )(place.reshape(1), *operands)


def body(
    tokens,
    input_heads,
    z_gate,
    b_proj,
    c_proj,
    step_size,
    decay_log,
    skip_gain,
    init_state,
    norm_gain,
    out_weight,
    moe_gain,
    routes,
    route_weights,
    w_gate,
    w_up,
    w_down,
):
    tok_rows, inner = input_heads.shape
    state_size = init_state.shape[2]
    seq_count = lax.axis_size("seq")
    place = lax.axis_index("tp")
    step_t = step_size.T
    outgoing, cum_t = own_state(input_heads, step_t, decay_log.T, b_proj, seq_count)
    got = exchange(outgoing)
    direct = within_block(skip_gain, input_heads, step_t, cum_t, b_proj, c_proj)
    back = entering_state(got, init_state.reshape(inner, state_size))
    arriving = exchange(back).reshape(inner, state_size)
    model_width = out_weight.shape[1]
    share = model_width // 4
    expert_count = w_gate.shape[0] * seq_count
    slot_count = 4 * tok_rows // seq_count
    top_count = routes.shape[1]
    items = top_count * tok_rows
    slots = expert_count * slot_count
    flat_expert = routes.T.reshape(-1)
    onehot = flat_expert[:, None] == jnp.arange(expert_count, dtype=jnp.int32)[None, :]
    before = jnp.arange(items)[:, None] > jnp.arange(items)[None, :]
    earlier = jnp.dot(before.astype(BF), onehot.astype(BF), preferred_element_type=F32)
    rank = jnp.sum(jnp.where(onehot, earlier, 0.0), axis=1).astype(jnp.int32)
    few = seq_count == 8
    layout = flat_expert
    if few:
        bits = flat_expert ^ lax.axis_index("seq")
        order = PARTS[0] + PARTS[1]
        layout = sum(jnp.where(bits == k, spot, 0) for spot, k in enumerate(order))
    placed = layout * slot_count + rank
    spots = placed[:, None] == jnp.arange(slots, dtype=jnp.int32)[None, :]
    spots = spots.reshape(top_count, tok_rows, slots)
    fill = jnp.any(spots, axis=0).astype(BF)
    combine = jnp.sum(jnp.where(spots, route_weights.T[:, :, None], 0.0), axis=0)
    direct = after(direct, fill, combine)

    to_near, to_last, keep, passing = mixer_tail(
        place, c_proj, arriving, cum_t, direct, z_gate, norm_gain, out_weight, tokens
    )

    from_last = swap(to_last, 1)
    from_near = swap(to_near, 1)
    from_far = swap((passing + from_last.astype(F32)).astype(BF), 2)
    hidden = (keep + from_near.astype(F32) + from_far.astype(F32)).astype(BF)

    outgoing = lax.dot_general(
        fill, hidden, (((0,), (0,)), ((), ())), preferred_element_type=F32
    ).astype(BF)
    outgoing = outgoing.reshape(expert_count, slot_count, share)

    middle = len(PARTS[0]) if few else expert_count // 2
    cut = middle * slot_count
    if few:
        own = exchange_parts((outgoing[:middle], outgoing[middle:]), early=True)
    else:
        arrived = exchange(outgoing).reshape(slots, share)
        own = [arrived[:cut], arrived[cut:]]
    far = [swap(part, 2) for part in own]
    near = [swap(part, 1) for part in own]
    weights = (w_gate[0], w_up[0], w_down[0])
    last = swap(far[0], 1)
    to_near0, to_last0, keep0, pass0 = run_expert(
        place, moe_gain, own[0], near[0], far[0], last, *weights
    )
    from_last0 = swap(to_last0, 1)
    last = swap(after(far[1], to_last0), 1)
    pass0 = (pass0.astype(F32) + from_last0.astype(F32)).astype(BF)
    from_far0 = swap(pass0, 2)
    to_near1, to_last1, keep1, pass1 = run_expert(
        place, moe_gain, after(own[1], pass0), near[1], far[1], last, *weights
    )
    from_last1 = swap(to_last1, 1)
    from_near0 = swap(after(to_near0, from_far0), 1)
    pass1 = (pass1.astype(F32) + from_last1.astype(F32)).astype(BF)
    from_far1 = swap(pass1, 2)
    from_near1 = swap(after(to_near1, pass1), 1)
    results = [
        (keep.astype(F32) + from_near.astype(F32) + from_far.astype(F32)).astype(BF)
        for keep, from_near, from_far in (
            (keep0, from_near0, from_far0),
            (keep1, from_near1, from_far1),
        )
    ]
    if few:
        results = [part.reshape(-1, slot_count, share) for part in results]
        returned = jnp.concatenate(exchange_parts(results))
    else:
        results = jnp.concatenate(results).reshape(expert_count, slot_count, share)
        returned = exchange(results).reshape(slots, share)
    mixed = hidden.astype(F32) + jnp.dot(
        combine,
        returned.astype(F32),
        precision=lax.Precision.HIGHEST,
        preferred_element_type=F32,
    )
    return mixed.astype(BF)


def solution(mesh):
    in_specs = (
        P("seq", None),
        P("seq", "tp"),
        P("seq", "tp"),
        P("seq", None),
        P("seq", None),
        P("seq", "tp"),
        P("seq", "tp"),
        P("tp"),
        P("tp", None, None),
        P("tp"),
        P("tp", None),
        P(),
        P("seq", None),
        P("seq", None),
        P("seq", None, "tp"),
        P("seq", None, "tp"),
        P("seq", "tp", None),
    )
    out_specs = P("seq", "tp")
    return jax.shard_map(body, mesh=mesh, in_specs=in_specs, out_specs=out_specs, check_vma=False)
```

```python
import jax
import jax.numpy as jnp
from jax import lax
from jax.experimental import pallas as pl
from jax.experimental.pallas import tpu as pltpu
from jax.sharding import PartitionSpec as P

BF = jnp.bfloat16
F32 = jnp.float32
MIB = 1024 * 1024
LANES = 128


def swap(value, bit):
    count = lax.axis_size("tp")
    return lax.ppermute(value, "tp", [(i, i ^ bit) for i in range(count)])


def exchange(value):
    return lax.all_to_all(value, "seq", split_axis=0, concat_axis=0, tiled=True)


def after(value, *others):
    return lax.optimization_barrier((value, *others))[0]


def in_hbm(value):
    return pltpu.with_memory_space_constraint(value, pltpu.HBM)


def params(mib):
    return pltpu.CompilerParams(vmem_limit_bytes=mib * MIB)


def whole(*shape):
    return pl.BlockSpec(shape, lambda *_: (0,) * len(shape))


def by_pair(left, right, size):
    lane = lax.broadcasted_iota(jnp.int32, (size, LANES), 1)
    return jnp.where(lane < LANES // 2, left, right)


def state_kernel(x, step_t, decay_t, b, out, cum_out):
    count, rows, _ = out.shape
    part = rows - 16
    heads, toks = decay_t.shape
    row = lax.broadcasted_iota(jnp.int32, (toks, toks), 0)
    col = lax.broadcasted_iota(jnp.int32, (toks, toks), 1)
    upper = (row <= col).astype(F32)
    cum_t = jnp.dot(
        decay_t[...], upper, precision=lax.Precision.HIGHEST, preferred_element_type=F32
    )
    cum_out[...] = cum_t
    end = cum_t[:, toks - 1 : toks]
    scale = (jnp.exp(end - cum_t) * step_t[...]).T
    decay = jnp.broadcast_to(jnp.exp(end), (heads, LANES))
    high = decay.astype(BF).astype(F32)
    extra = by_pair(high, decay - high, heads).astype(BF)
    for k in range(count):
        out[k, pl.ds(part, 16), :] = extra
    for p in range(heads // 2):
        pair = x[:, p * LANES : (p + 1) * LANES].astype(F32)
        factor = by_pair(scale[:, 2 * p : 2 * p + 1], scale[:, 2 * p + 1 : 2 * p + 2], toks)
        state = lax.dot_general(
            (pair * factor).astype(BF),
            b[...],
            (((0,), (0,)), ((), ())),
            preferred_element_type=F32,
        ).astype(BF)
        for k in range(LANES // part):
            out[p * (LANES // part) + k, pl.ds(0, part), :] = state[k * part : (k + 1) * part]


def own_state(x, step_t, decay_t, b, count):
    heads, toks = decay_t.shape
    part = x.shape[1] // count
    return pl.pallas_call(
        state_kernel,
        out_shape=[
            jax.ShapeDtypeStruct((count, part + 16, b.shape[1]), BF),
            jax.ShapeDtypeStruct((heads, toks), F32),
        ],
        compiler_params=params(8),
        name="own_state",
    )(in_hbm(x), in_hbm(step_t), in_hbm(decay_t), in_hbm(b))


def prefix_kernel(place_ref, got, start, back):
    count, part, _ = back.shape
    heads = 16
    held = max(1, heads // count)
    group = part // held
    first = place_ref[0] * heads // count
    row = lax.broadcasted_iota(jnp.int32, (heads, LANES), 0)
    carries = [start[pl.ds(h * group, group), :] for h in range(held)]
    for turn in range(count):
        extra = got[turn, pl.ds(part, 16), :].astype(F32)
        scale = extra[:, :1] + extra[:, LANES // 2 : LANES // 2 + 1]
        for h in range(held):
            spot = pl.ds(h * group, group)
            back[turn, spot, :] = carries[h].astype(BF)
            factor = jnp.sum(jnp.where(row == first + h, scale, 0.0), axis=0, keepdims=True)
            carries[h] = factor * carries[h] + got[turn, spot, :].astype(F32)


PARTS = ((0, 1, 4, 5), (6, 7, 2, 3))


def exchange_parts(pieces, early=False):
    parts = []
    for order, part in zip(PARTS, pieces):
        got = []
        for spot, k in enumerate(order):
            piece = part[spot]
            if k > 0:
                piece = lax.ppermute(piece, "seq", [(i, i ^ k) for i in range(8)])
            got.append(piece)
        parts.append(got)
    if early:
        parts[0][0] = after(parts[0][0], parts[1][0])
    return [jnp.concatenate(got) for got in parts]


def entering_state(got, init_rows):
    count, rows, width = got.shape
    part = rows - 16
    place = lax.axis_index("seq")
    start = lax.dynamic_slice_in_dim(init_rows, place * part, part, 0)
    vmem = pl.BlockSpec(memory_space=pltpu.VMEM)
    return pl.pallas_call(
        prefix_kernel,
        in_specs=[pl.BlockSpec(memory_space=pltpu.SMEM), vmem, vmem],
        out_shape=jax.ShapeDtypeStruct((count, part, width), BF),
        compiler_params=params(8),
        name="prefix",
    )(place.reshape(1), got, start)


def within_kernel(skip, x, step_t, cum_t, b, c, out):
    heads, toks = cum_t.shape
    row = lax.broadcasted_iota(jnp.int32, (toks, toks), 0)
    col = lax.broadcasted_iota(jnp.int32, (toks, toks), 1)
    causal = row >= col
    nt = (((1,), (1,)), ((), ()))
    scores = lax.dot_general(c[...], b[...], nt, preferred_element_type=F32)
    cum = cum_t[...].T
    for p in range(heads // 2):
        pair = x[:, p * LANES : (p + 1) * LANES]
        sums = []
        for h in (2 * p, 2 * p + 1):
            gap = cum[:, h : h + 1] - cum_t[h : h + 1, :]
            decay = jnp.where(causal, jnp.exp(jnp.where(causal, gap, 0.0)), 0.0)
            weights = (decay * scores * step_t[h : h + 1, :]).astype(BF)
            sums.append(jnp.dot(weights, pair, preferred_element_type=F32))
        gain = by_pair(skip[2 * p], skip[2 * p + 1], toks)
        out[:, p * LANES : (p + 1) * LANES] = (
            by_pair(sums[0], sums[1], toks) + gain * pair.astype(F32)
        )


def within_block(skip, x, step_t, cum_t, b, c):
    toks, inner = x.shape
    heads = cum_t.shape[0]
    vmem = pl.BlockSpec(memory_space=pltpu.VMEM)
    return pl.pallas_call(
        within_kernel,
        in_specs=[pl.BlockSpec(memory_space=pltpu.SMEM)] + [vmem] * 5,
        out_shape=jax.ShapeDtypeStruct((toks, inner), F32),
        compiler_params=params(8),
        cost_estimate=pl.CostEstimate(
            flops=4 * heads * toks * toks * LANES,
            bytes_accessed=6 * toks * inner,
            transcendentals=heads * toks * toks,
        ),
        name="within_block",
    )(skip, in_hbm(x), in_hbm(step_t), cum_t, in_hbm(b), in_hbm(c))


def fetch(sems, *pairs):
    copies = [pltpu.make_async_copy(src, dst, sems.at[i]) for i, (src, dst) in enumerate(pairs)]
    for copy in copies:
        copy.start()
    return copies


def cuts_of(ref, count):
    rows = ref.shape[0] // count
    return [ref.at[pl.ds(k * rows, rows)] for k in range(count)]


def quarters(place_ref, share):
    return [pl.ds(pl.multiple_of((place_ref[0] ^ k) * share, share), share) for k in range(4)]


def tail_kernel(
    place_ref, c_in, cum_in, gain_in, arriving_in, direct_in, z_in, weight_in, tokens_in,
    near, last, keep, passing,
    c, cum_t, gain, arriving, direct, z, weight, tokens, normed, sems,
):
    heads, toks = cum_t.shape
    share = near.shape[1]
    spots = quarters(place_ref, share)
    copies = fetch(
        sems,
        (cum_in, cum_t),
        (gain_in, gain),
        (c_in, c),
        (arriving_in, arriving),
        (z_in, z),
        (direct_in, direct),
        *zip(cuts_of(weight_in, 8), cuts_of(weight, 8)),
        (tokens_in.at[:, spots[0]], tokens),
    )
    for copy in copies[:6]:
        copy.wait()
    grown = jnp.exp(cum_t[...]).T
    lane = lax.broadcasted_iota(jnp.int32, (toks, LANES), 1)
    left = lane < LANES // 2
    nt = (((1,), (1,)), ((), ()))
    for p in range(heads // 2):
        spot = pl.ds(p * LANES, LANES)
        inter = lax.dot_general(c[...], arriving[spot, :], nt, preferred_element_type=F32)
        factor = by_pair(grown[:, 2 * p : 2 * p + 1], grown[:, 2 * p + 1 : 2 * p + 2], toks)
        wide = z[:, spot].astype(F32)
        gated = (direct[:, spot] + inter * factor) * (wide * (1.0 / (1.0 + jnp.exp(-wide))))
        square = gated * gated
        first = jnp.sum(jnp.where(left, square, 0.0), axis=1, keepdims=True)
        second = jnp.sum(jnp.where(left, 0.0, square), axis=1, keepdims=True)
        mean = by_pair(first, second, toks) * (2.0 / LANES)
        normed[:, spot] = (gated * lax.rsqrt(mean + 1e-05) * gain[:, spot]).astype(BF)
    for copy in copies[6:]:
        copy.wait()
    for k, out in ((3, last), (1, near), (2, passing), (0, keep)):
        part = jnp.dot(normed[...], weight[:, spots[k]], preferred_element_type=F32)
        if k == 0:
            part += tokens[...].astype(F32)
        out[...] = part.astype(out.dtype)


def mixer_tail(place, c, arriving, cum_t, direct, z, gain, weight, tokens):
    heads, toks = cum_t.shape
    inner, width = weight.shape
    share = width // 4
    operands = (c, cum_t, gain.reshape(1, inner), arriving, direct, z, weight, tokens)
    fixed = (0, 2, 5, 6, 7)
    operands = [in_hbm(a) if i in fixed else a for i, a in enumerate(operands)]
    return pl.pallas_call(
        tail_kernel,
        in_specs=[pl.BlockSpec(memory_space=pltpu.SMEM)]
        + [pl.BlockSpec(memory_space=pl.ANY)] * len(operands),
        out_shape=[jax.ShapeDtypeStruct((toks, share), kind) for kind in (BF, BF, F32, F32)],
        scratch_shapes=[pltpu.VMEM(a.shape, a.dtype) for a in operands[:-1]]
        + [
            pltpu.VMEM((toks, share), BF),
            pltpu.VMEM((toks, inner), BF),
            pltpu.SemaphoreType.DMA((15,)),
        ],
        compiler_params=params(12),
        cost_estimate=pl.CostEstimate(
            flops=2 * toks * inner * width,
            bytes_accessed=2 * inner * width + 14 * toks * inner,
            transcendentals=toks * inner,
        ),
        name="mixer_tail",
    )(place.reshape(1), *operands)


def expert_kernel(
    place_ref, gain_in, own_in, near_in, far_in, last_in, wg_in, wu_in, wd_in,
    near_out, last_out, keep_out, pass_out,
    gain, own, near, far, last, wg, wu, wd, rows, sems,
):
    count, share = own.shape
    width = 4 * share
    spots = quarters(place_ref, share)
    copies = fetch(
        sems,
        (gain_in, gain),
        (own_in, own),
        (near_in, near),
        (far_in, far),
        (last_in, last),
        *((w_in.at[s], w.at[s]) for s in spots for w_in, w in ((wg_in, wg), (wu_in, wu))),
        *zip(cuts_of(wd_in, 4), cuts_of(wd, 4)),
    )
    for copy in copies[:5]:
        copy.wait()

    @pl.loop(0, count, step=64)
    def _(start):
        spot = pl.ds(pl.multiple_of(start, 64), 64)
        wide = [p[spot, :].astype(F32) for p in (own, near, far, last)]
        square = sum(jnp.sum(w * w, axis=1, keepdims=True) for w in wide)
        scale = lax.rsqrt(square * (1.0 / width) + 1e-05)
        for k in range(4):
            rows[k, spot, :] = (wide[k] * scale * gain[:, spots[k]]).astype(BF)

    gate = up = 0.0
    for k in range(4):
        copies[5 + 2 * k].wait()
        gate += jnp.dot(rows[k], wg[spots[k], :], preferred_element_type=F32)
        copies[6 + 2 * k].wait()
        up += jnp.dot(rows[k], wu[spots[k], :], preferred_element_type=F32)
    act = (gate * (1.0 / (1.0 + jnp.exp(-gate))) * up).astype(BF)
    for copy in copies[13:]:
        copy.wait()
    for k, out in ((3, last_out), (1, near_out), (2, pass_out), (0, keep_out)):
        out[...] = jnp.dot(act, wd[:, spots[k]], preferred_element_type=F32).astype(BF)


def run_expert(place, gain, own, near, far, last, wg, wu, wd):
    rows, share = own.shape
    width, inner = wg.shape
    weights = (in_hbm(wg), in_hbm(wu), in_hbm(wd))
    operands = (in_hbm(gain.reshape(1, width)), own, near, far, last, *weights)
    return pl.pallas_call(
        expert_kernel,
        in_specs=[pl.BlockSpec(memory_space=pltpu.SMEM)]
        + [pl.BlockSpec(memory_space=pl.ANY)] * len(operands),
        out_shape=[jax.ShapeDtypeStruct((rows, share), BF)] * 4,
        scratch_shapes=[pltpu.VMEM(a.shape, a.dtype) for a in operands]
        + [
            pltpu.VMEM((4, rows, share), BF),
            pltpu.SemaphoreType.DMA((17,)),
        ],
        compiler_params=params(16),
        cost_estimate=pl.CostEstimate(flops=1, bytes_accessed=1, transcendentals=0),
        name="expert",
    )(place.reshape(1), *operands)


def body(
    tokens,
    input_heads,
    z_gate,
    b_proj,
    c_proj,
    step_size,
    decay_log,
    skip_gain,
    init_state,
    norm_gain,
    out_weight,
    moe_gain,
    routes,
    route_weights,
    w_gate,
    w_up,
    w_down,
):
    tok_rows, inner = input_heads.shape
    state_size = init_state.shape[2]
    seq_count = lax.axis_size("seq")
    place = lax.axis_index("tp")
    step_t = step_size.T
    outgoing, cum_t = own_state(input_heads, step_t, decay_log.T, b_proj, seq_count)
    got = exchange(outgoing)
    direct = within_block(skip_gain, input_heads, step_t, cum_t, b_proj, c_proj)
    back = entering_state(got, init_state.reshape(inner, state_size))
    arriving = exchange(back).reshape(inner, state_size)
    model_width = out_weight.shape[1]
    share = model_width // 4
    expert_count = w_gate.shape[0] * seq_count
    slot_count = 4 * tok_rows // seq_count
    top_count = routes.shape[1]
    items = top_count * tok_rows
    slots = expert_count * slot_count
    flat_expert = routes.T.reshape(-1)
    onehot = flat_expert[:, None] == jnp.arange(expert_count, dtype=jnp.int32)[None, :]
    before = jnp.arange(items)[:, None] > jnp.arange(items)[None, :]
    earlier = jnp.dot(before.astype(BF), onehot.astype(BF), preferred_element_type=F32)
    rank = jnp.sum(jnp.where(onehot, earlier, 0.0), axis=1).astype(jnp.int32)
    few = seq_count == 8
    layout = flat_expert
    if few:
        bits = flat_expert ^ lax.axis_index("seq")
        order = PARTS[0] + PARTS[1]
        layout = sum(jnp.where(bits == k, spot, 0) for spot, k in enumerate(order))
    placed = layout * slot_count + rank
    spots = placed[:, None] == jnp.arange(slots, dtype=jnp.int32)[None, :]
    spots = spots.reshape(top_count, tok_rows, slots)
    fill = jnp.any(spots, axis=0).astype(BF)
    combine = jnp.sum(jnp.where(spots, route_weights.T[:, :, None], 0.0), axis=0)
    direct = after(direct, fill, combine)

    to_near, to_last, keep, passing = mixer_tail(
        place, c_proj, arriving, cum_t, direct, z_gate, norm_gain, out_weight, tokens
    )

    from_last = swap(to_last, 1)
    from_near = swap(to_near, 1)
    from_far = swap((passing + from_last.astype(F32)).astype(BF), 2)
    hidden = (keep + from_near.astype(F32) + from_far.astype(F32)).astype(BF)

    outgoing = lax.dot_general(
        fill, hidden, (((0,), (0,)), ((), ())), preferred_element_type=F32
    ).astype(BF)
    outgoing = outgoing.reshape(expert_count, slot_count, share)

    middle = len(PARTS[0]) if few else expert_count // 2
    cut = middle * slot_count
    if few:
        own = exchange_parts((outgoing[:middle], outgoing[middle:]), early=True)
    else:
        arrived = exchange(outgoing).reshape(slots, share)
        own = [arrived[:cut], arrived[cut:]]
    far = [swap(part, 2) for part in own]
    near = [swap(part, 1) for part in own]
    weights = (w_gate[0], w_up[0], w_down[0])
    last = swap(far[0], 1)
    to_near0, to_last0, keep0, pass0 = run_expert(
        place, moe_gain, own[0], near[0], far[0], last, *weights
    )
    from_last0 = swap(to_last0, 1)
    last = swap(after(far[1], to_last0), 1)
    pass0 = (pass0.astype(F32) + from_last0.astype(F32)).astype(BF)
    from_far0 = swap(pass0, 2)
    to_near1, to_last1, keep1, pass1 = run_expert(
        place, moe_gain, after(own[1], pass0), near[1], far[1], last, *weights
    )
    from_last1 = swap(to_last1, 1)
    from_near0 = swap(after(to_near0, pass0), 1)
    pass1 = (pass1.astype(F32) + from_last1.astype(F32)).astype(BF)
    from_far1 = swap(pass1, 2)
    from_near1 = swap(after(to_near1, pass1), 1)
    results = [
        (keep.astype(F32) + from_near.astype(F32) + from_far.astype(F32)).astype(BF)
        for keep, from_near, from_far in (
            (keep0, from_near0, from_far0),
            (keep1, from_near1, from_far1),
        )
    ]
    if few:
        results = [part.reshape(-1, slot_count, share) for part in results]
        returned = jnp.concatenate(exchange_parts(results))
    else:
        results = jnp.concatenate(results).reshape(expert_count, slot_count, share)
        returned = exchange(results).reshape(slots, share)
    mixed = hidden.astype(F32) + jnp.dot(
        combine,
        returned.astype(F32),
        precision=lax.Precision.HIGHEST,
        preferred_element_type=F32,
    )
    return mixed.astype(BF)


def solution(mesh):
    in_specs = (
        P("seq", None),
        P("seq", "tp"),
        P("seq", "tp"),
        P("seq", None),
        P("seq", None),
        P("seq", "tp"),
        P("seq", "tp"),
        P("tp"),
        P("tp", None, None),
        P("tp"),
        P("tp", None),
        P(),
        P("seq", None),
        P("seq", None),
        P("seq", None, "tp"),
        P("seq", None, "tp"),
        P("seq", "tp", None),
    )
    out_specs = P("seq", "tp")
    return jax.shard_map(body, mesh=mesh, in_specs=in_specs, out_specs=out_specs, check_vma=False)
```
